32 devices in a mesh: seq: 4 (over x, core), exp: 8 (over z, y).
Axes of the slice: x: 2, y: 2, z: 4, core: 2. Of those that a mesh axis runs over, the one named last changes fastest.
Arguments:
- tokens: bfloat16 [1024, 7168], P('exp', 'seq'), may hold values from -6 to 6
- out_grad: bfloat16 [1024, 7168], P('exp', 'seq'), may hold values from -6 to 6
- expert_ids: int32 [1024, 8], P('exp'), may hold values from 0 to 63, as said below
- route_weights: float32 [1024, 8], P('exp'), may hold values from 0.2 to 2.5
- gate_proj: bfloat16 [8, 7168, 2048], P('exp', None, 'seq'), may hold values from -0.0625 to 0.0625
- up_proj: bfloat16 [8, 7168, 2048], P('exp', None, 'seq'), may hold values from -0.0625 to 0.0625
- down_proj: bfloat16 [8, 2048, 7168], P('exp', 'seq'), may hold values from -0.125 to 0.125
Outputs:
- token_grad: bfloat16 [1024, 7168], P('exp', 'seq')
- route_grad: float32 [1024, 8], P('exp', 'seq')
The draws below stay inside these ranges and needn't reach their ends.
Inputs may be any that keep to these rules, and one draw needn't show every extreme that they name: `expert_ids`: each row names 8 different experts, at most one of them below 8; between 96 and all of the 128 rows of one index of exp name one below 8; those rows name any one expert below 8 at most 32 times, and in every draw one such expert exactly 32 times on every index of exp.
All inputs are finite; a program needn't handle non-finite values.
Results may differ from the reference program's by a relative error of at most 0.0049.
Values may be sent and summed in bfloat16 or wider, within the bound.
No kernel may reach another device: no remote copies, remote signals or barrier semaphores. Data moves between devices by JAX's collectives and lax.ppermute only.
A program may use at most 128 MiB of HBM per device.

```python
import math
import jax
import jax.numpy as jnp
from jax import lax

D = 7168
FF = 2048
TOPK = 8
TOK_DEV = 128
EXPERTS = 8
ROUTED = 64
MOST = 32
TOKENS = 1024
N_EXP = 8


def draw_expert_ids(key, part):
    block_count = TOKENS // TOK_DEV
    pool_size = EXPERTS * MOST
    outside_count = ROUTED - EXPERTS
    hottest = jax.random.randint(jax.random.fold_in(key, 1), (), 0, EXPERTS)
    favour = jax.random.randint(jax.random.fold_in(key, 2), (EXPERTS,), 1, 9)
    entries = jnp.arange(pool_size, dtype=jnp.int32)
    owners = entries // MOST

    def one_block(block_index):
        block_key = jax.random.fold_in(key, 1000 + block_index)
        subkeys = jax.random.split(block_key, 5)
        jitter = jax.random.randint(subkeys[0], (pool_size,), 0, 4096)
        scores = jnp.where(owners == hottest, 0, 1 + jitter // favour[owners])
        ranking = jnp.argsort(scores * pool_size + entries, stable=True)
        picked = owners[ranking][:TOK_DEV]
        live_rows = TOK_DEV - jax.random.randint(subkeys[1], (), 0, TOK_DEV // 4 + 1)
        window_ids = jnp.where(jnp.arange(TOK_DEV, dtype=jnp.int32) < live_rows, picked, -1)
        window_ids = window_ids[jax.random.permutation(subkeys[2], TOK_DEV)]
        offsets = jax.random.randint(subkeys[3], (TOK_DEV, 1), 0, outside_count)
        strides = jnp.arange(TOPK, dtype=jnp.int32)[None, :] * (outside_count // TOPK)
        outside_ids = EXPERTS + (offsets + strides) % outside_count
        position = jax.random.randint(subkeys[4], (TOK_DEV, 1), 0, TOPK)
        chosen = (jnp.arange(TOPK, dtype=jnp.int32)[None, :] == position) & (window_ids[:, None] >= 0)
        return jnp.where(chosen, window_ids[:, None], outside_ids)
    drawn = jax.vmap(one_block)(jnp.arange(block_count, dtype=jnp.int32))
    return drawn.reshape(TOKENS, TOPK).astype(jnp.int32)


def steps_of(stream_key, dims, cuts, least, top_value):
    level, own = 1.0, jax.random.fold_in(stream_key, 6)
    for axis_at, blocks in cuts:
        draws = jnp.exp(jax.random.uniform(jax.random.fold_in(own, axis_at), (blocks,), jnp.float32, least / len(cuts), top_value / len(cuts)))
        level = level * jnp.repeat(draws, dims[axis_at] // blocks).reshape([-1 if axis == axis_at else 1 for axis in range(len(dims))])
    return level


def bell_draw(key, dims, width, bound, shards=(), kind=jnp.bfloat16):
    values = width * jax.random.normal(key, dims, jnp.float32)
    if shards:
        values = values * steps_of(key, dims, shards, -0.22, 0.18)
    return jnp.clip(values, -bound, bound).astype(kind)


def setup_inputs(seed: int = 0) -> dict:
    streams_of = jax.random.split(jax.random.key(seed), 8)
    return {
        "tokens": bell_draw(streams_of[0], (TOKENS, D), 1.0, 6.0, ((0, 8), (1, 4))),
        "out_grad": bell_draw(streams_of[1], (TOKENS, D), 1.0, 6.0, ((0, 8), (1, 4))),
        "expert_ids": draw_expert_ids(jax.random.fold_in(streams_of[7], 71), 0),
        "route_weights": jnp.clip(jnp.exp(math.log(2.5) - 2.5257286 * jax.random.uniform(streams_of[3], (TOKENS, TOPK), jnp.float32) ** steps_of(streams_of[3], (TOKENS, TOPK), ((0, 8),), -0.2, 0.2)), 0.2, 2.5),
        "gate_proj": bell_draw(streams_of[4], (EXPERTS, D, FF), D ** -0.5, 0.0625, ((0, 8), (2, 4))),
        "up_proj": bell_draw(streams_of[5], (EXPERTS, D, FF), D ** -0.5, 0.0625, ((0, 8), (2, 4))),
        "down_proj": bell_draw(streams_of[6], (EXPERTS, FF, D), FF ** -0.5, 0.125, ((0, 8), (1, 4))),
    }


def expert_front(row_inputs, row_grads, w_gate, w_up, w_down):
    pre_gate = jnp.dot(row_inputs, w_gate, preferred_element_type=jnp.float32)
    pre_up = jnp.dot(row_inputs, w_up, preferred_element_type=jnp.float32)
    back_grad = jnp.dot(row_grads, w_down.T, preferred_element_type=jnp.float32)
    gate_sig = jax.nn.sigmoid(pre_gate)
    active = pre_gate * gate_sig
    route_part = jnp.sum(active * pre_up * back_grad, axis=-1)
    grad_gate = (back_grad * pre_up * gate_sig * (1.0 + pre_gate * (1.0 - gate_sig))).astype(jnp.bfloat16)
    grad_up = (back_grad * active).astype(jnp.bfloat16)
    return grad_gate, grad_up, route_part


def expert_back(grad_gate, grad_up, w_gate, w_up):
    return (jnp.dot(grad_gate, w_gate.T, preferred_element_type=jnp.float32)
            + jnp.dot(grad_up, w_up.T, preferred_element_type=jnp.float32))


def reference(tokens, out_grad, expert_ids, route_weights, gate_proj, up_proj, down_proj):
    capacity = N_EXP * MOST
    pair_count = TOKENS * TOPK
    flat_ids = expert_ids.reshape(-1)
    flat_weights = jnp.concatenate([route_weights.reshape(-1), jnp.zeros((1,), jnp.float32)])
    padded_x = jnp.concatenate([tokens, jnp.zeros((1, D), jnp.bfloat16)], axis=0)
    padded_dy = jnp.concatenate([out_grad, jnp.zeros((1, D), jnp.bfloat16)], axis=0)

    def visit_expert(running, expert):
        grad_total, route_total = running
        located = jnp.nonzero(flat_ids == expert, size=capacity, fill_value=pair_count)[0].astype(jnp.int32)
        token_row = (located // TOPK).astype(jnp.int32)
        w_gate = gate_proj[expert]
        w_up = up_proj[expert]
        grad_gate, grad_up, route_part = expert_front(padded_x[token_row], padded_dy[token_row], w_gate, w_up, down_proj[expert])
        pair_grad = expert_back(grad_gate, grad_up, w_gate, w_up)
        grad_total = grad_total.at[token_row].add(flat_weights[located][:, None] * pair_grad)
        route_total = route_total.at[located].add(route_part)
        return (grad_total, route_total), None

    initial = (jnp.zeros((TOKENS + 1, D), jnp.float32), jnp.zeros((pair_count + 1,), jnp.float32))
    (grad_total, route_total), _ = lax.scan(visit_expert, initial, jnp.arange(EXPERTS, dtype=jnp.int32))
    return grad_total[:TOKENS].astype(jnp.bfloat16), route_total[:pair_count].reshape(TOKENS, TOPK)
```

```python
import functools

import jax
import jax.numpy as jnp
from jax import lax
from jax.experimental import pallas as pl
from jax.experimental.pallas import tpu as pltpu
from jax.sharding import PartitionSpec as P

CONTRACT = (((1,), (1,)), ((), ()))
BF16 = jnp.bfloat16
F32 = jnp.float32
VMEM_BYTES = 56 * 1024 * 1024
EXTRA = 128
RETURN_CHUNKS = 2


def params():
    return pltpu.CompilerParams(vmem_limit_bytes=VMEM_BYTES)


def pack_kernel(ids_ref, x_ref, dy_ref, pick_ref, px_ref, pdy_ref, *, experts, most):
    ids = ids_ref[...]
    tokens = ids.shape[0]
    named = jnp.min(ids, axis=1, keepdims=True)
    hot = named == lax.broadcasted_iota(jnp.int32, (tokens, experts), 1)
    rows = lax.broadcasted_iota(jnp.int32, (tokens, tokens), 0)
    cols = lax.broadcasted_iota(jnp.int32, (tokens, tokens), 1)
    before = (cols < rows).astype(F32).astype(BF16)
    hot_f = hot.astype(F32)
    earlier = jnp.dot(before, hot_f.astype(BF16), preferred_element_type=F32)
    rank = jnp.sum(earlier * hot_f, axis=1, keepdims=True).astype(jnp.int32)
    target = jnp.where(named < experts, named * most + rank, -1)
    slots = lax.broadcasted_iota(jnp.int32, (tokens, experts * most), 1)
    pick = (target == slots).astype(F32)
    pick_ref[...] = pick.astype(BF16)
    place = pick.T.astype(BF16)
    px_ref[...] = jnp.dot(place, x_ref[...], preferred_element_type=F32).astype(BF16)
    pdy_ref[...] = jnp.dot(place, dy_ref[...], preferred_element_type=F32).astype(BF16)


def pack(ids, x, dy, experts, most):
    slots = experts * most
    tokens, width = x.shape
    return pl.pallas_call(
        functools.partial(pack_kernel, experts=experts, most=most),
        out_shape=(
            jax.ShapeDtypeStruct((tokens, slots), BF16),
            jax.ShapeDtypeStruct((slots, width), BF16),
            jax.ShapeDtypeStruct((slots, width), BF16),
        ),
        compiler_params=params(),
        name="pack",
    )(ids, x, dy)


def forward_kernel(order_ref, *refs, count):
    pieces = refs[:count]
    wg_ref, wu_ref, gate_ref, up_ref = refs[count:]
    step = pl.program_id(0)

    @pl.when(step == 0)
    def _():
        gate_ref[...] = jnp.zeros_like(gate_ref)
        up_ref[...] = jnp.zeros_like(up_ref)

    for j in range(count):

        @pl.when(step == j)
        def _(j=j):
            rows = pieces[j][...]
            gate_ref[...] += jnp.dot(rows, wg_ref[...], preferred_element_type=F32)
            up_ref[...] += jnp.dot(rows, wu_ref[...], preferred_element_type=F32)


def forward(order, pieces, wg, wu):
    count = len(pieces)
    slots, part = pieces[0].shape
    hidden = wg.shape[1]
    whole = pl.BlockSpec((slots, part), lambda j, order: (0, 0))
    weight = pl.BlockSpec((part, hidden), lambda j, order: (order[j], 0))
    out = pl.BlockSpec((slots, hidden), lambda j, order: (0, 0))
    return pl.pallas_call(
        functools.partial(forward_kernel, count=count),
        grid_spec=pltpu.PrefetchScalarGridSpec(
            num_scalar_prefetch=1,
            grid=(count,),
            in_specs=[whole] * count + [weight, weight],
            out_specs=[out, out],
        ),
        out_shape=[jax.ShapeDtypeStruct((slots, hidden), F32)] * 2,
        compiler_params=params(),
        cost_estimate=pl.CostEstimate(
            flops=4 * slots * part * count * hidden,
            bytes_accessed=4 * part * count * hidden + 2 * slots * part * count,
            transcendentals=0,
        ),
        name="forward",
    )(order, *pieces, wg, wu)


def middle_kernel(order_ref, *refs, count):
    pieces = refs[:count]
    wd_ref, gate_ref, up_ref, gg_ref, gu_ref, route_ref, back = refs[count:]
    step = pl.program_id(0)

    @pl.when(step == 0)
    def _():
        back[...] = jnp.zeros_like(back)

    for j in range(count):

        @pl.when(step == j)
        def _(j=j):
            back[...] += lax.dot_general(
                pieces[j][...], wd_ref[...], CONTRACT, preferred_element_type=F32
            )

    @pl.when(step == count - 1)
    def _():
        back_grad = back[...]
        pre_gate = gate_ref[...]
        pre_up = up_ref[...]
        sig = 1.0 / (1.0 + jnp.exp(-pre_gate))
        active = pre_gate * sig
        grad_up = back_grad * active
        gg_ref[...] = (back_grad * pre_up * sig * (1.0 + pre_gate * (1.0 - sig))).astype(BF16)
        gu_ref[...] = grad_up.astype(BF16)
        total = jnp.sum(grad_up * pre_up, axis=1, keepdims=True)
        route_ref[...] = jnp.broadcast_to(total, route_ref.shape)


def middle(order, pieces, wd, pre_gate, pre_up):
    count = len(pieces)
    slots, part = pieces[0].shape
    hidden = wd.shape[0]
    whole = pl.BlockSpec((slots, part), lambda j, order: (0, 0))
    weight = pl.BlockSpec((hidden, part), lambda j, order: (0, order[j]))
    kept = pl.BlockSpec((slots, hidden), lambda j, order: (0, 0))
    route = pl.BlockSpec((slots, EXTRA), lambda j, order: (0, 0))
    return pl.pallas_call(
        functools.partial(middle_kernel, count=count),
        grid_spec=pltpu.PrefetchScalarGridSpec(
            num_scalar_prefetch=1,
            grid=(count,),
            in_specs=[whole] * count + [weight, kept, kept],
            out_specs=[kept, kept, route],
            scratch_shapes=[pltpu.VMEM((slots, hidden), F32)],
        ),
        out_shape=[
            jax.ShapeDtypeStruct((slots, hidden), BF16),
            jax.ShapeDtypeStruct((slots, hidden), BF16),
            jax.ShapeDtypeStruct((slots, EXTRA), F32),
        ],
        compiler_params=params(),
        cost_estimate=pl.CostEstimate(
            flops=2 * slots * part * count * hidden,
            bytes_accessed=2 * part * count * hidden + 2 * slots * part * count,
            transcendentals=slots * hidden,
        ),
        name="middle",
    )(order, *pieces, wd, pre_gate, pre_up)


def backward_kernel(order_ref, gg_ref, gu_ref, wg_ref, wu_ref, send_ref, keep_ref):
    def product():
        return lax.dot_general(
            gg_ref[...], wg_ref[...], CONTRACT, preferred_element_type=F32
        ) + lax.dot_general(gu_ref[...], wu_ref[...], CONTRACT, preferred_element_type=F32)

    @pl.when(pl.program_id(0) == 0)
    def _():
        send_ref[...] = product().astype(BF16)

    @pl.when(pl.program_id(0) == 1)
    def _():
        keep_ref[...] = product()


def backward(order, gg, gu, wg, wu, part):
    slots, hidden = gg.shape
    grad = pl.BlockSpec((slots, hidden), lambda j, order: (0, 0))
    weight = pl.BlockSpec((part, hidden), lambda j, order: (order[j], 0))
    out = pl.BlockSpec((slots, part), lambda j, order: (0, 0))
    return pl.pallas_call(
        backward_kernel,
        grid_spec=pltpu.PrefetchScalarGridSpec(
            num_scalar_prefetch=1,
            grid=(2,),
            in_specs=[grad, grad, weight, weight],
            out_specs=[out, out],
        ),
        out_shape=[
            jax.ShapeDtypeStruct((slots, part), BF16),
            jax.ShapeDtypeStruct((slots, part), F32),
        ],
        compiler_params=params(),
        cost_estimate=pl.CostEstimate(
            flops=8 * slots * part * hidden,
            bytes_accessed=8 * part * hidden + 6 * slots * part,
            transcendentals=0,
        ),
        name="backward",
    )(order, gg, gu, wg, wu)


def combine_kernel(ids_ref, weights_ref, pick_ref, *refs, experts, chunks):
    came = refs[:chunks]
    grad_ref, route_ref = refs[chunks:]
    ids = ids_ref[...]
    inside = ids < experts
    weight = jnp.sum(jnp.where(inside, weights_ref[...], 0.0), axis=1, keepdims=True)
    pick = pick_ref[...]
    at = 0
    for j in range(chunks):
        taken = jnp.dot(pick, came[j][...], preferred_element_type=F32)
        width = taken.shape[1]
        if j == 0:
            width -= EXTRA
            total = taken[:, width : width + 1] + taken[:, width + 1 : width + 2]
            route_ref[...] = jnp.where(inside, total, 0.0)
        grad_ref[:, at : at + width] = (weight * taken[:, :width]).astype(BF16)
        at += width


def combine(ids, weights, pick, came, experts, width):
    tokens = ids.shape[0]
    return pl.pallas_call(
        functools.partial(combine_kernel, experts=experts, chunks=len(came)),
        out_shape=(
            jax.ShapeDtypeStruct((tokens, width), BF16),
            jax.ShapeDtypeStruct(ids.shape, F32),
        ),
        compiler_params=params(),
        name="combine",
    )(ids, weights, pick, *came)


def local(tokens, out_grad, expert_ids, route_weights, gate_proj, up_proj, down_proj):
    seq_count = lax.axis_size("seq")
    exp_count = lax.axis_size("exp")
    tok_dev, part = tokens.shape
    top_count = expert_ids.shape[1]
    expert_count = exp_count * gate_proj.shape[0]
    most = max(2, 2 * ((tok_dev + expert_count - 1) // expert_count))
    slots = expert_count * most
    wg, wu, wd = gate_proj[0], up_proj[0], down_proj[0]

    seq_at = lax.axis_index("seq")
    chips = seq_count // 2
    core = seq_at % 2
    chip = seq_at // 2

    def other_core(value):
        return lax.ppermute(value, "seq", [(s, s ^ 1) for s in range(seq_count)])

    def chip_shift(value, k):
        return lax.ppermute(value, "seq", [(s, (s + 2 * k) % seq_count) for s in range(seq_count)])

    def over_exp(value):
        rows, width = value.shape
        return lax.all_to_all(
            value.reshape(exp_count, rows // exp_count, width), "exp", 0, 0, tiled=True
        ).reshape(rows, width)

    def gathered(own):
        shares = [own] + [chip_shift(own, k) for k in range(1, chips)]
        pieces = []
        for share in shares:
            pieces += [share, other_core(share)]
        return pieces

    order = jnp.stack(
        [((chip - k) % chips) * 2 + c for k in range(chips) for c in (core, 1 - core)]
    ).astype(jnp.int32)

    pick, packed_x, packed_dy = pack(expert_ids, tokens, out_grad, expert_count, most)
    came_x = over_exp(packed_x)
    came_x, packed_dy = lax.optimization_barrier((came_x, packed_dy))
    pieces_x = gathered(came_x)
    pieces_dy = gathered(over_exp(packed_dy))

    pre_gate, pre_up = forward(order, pieces_x, wg, wu)
    gg, gu, route = middle(order, pieces_dy, wd, pre_gate, pre_up)

    shares = []
    for k in list(range(1, chips)) + [0]:
        there = ((chip + k) % chips) * 2
        both = jnp.stack([there + 1 - core, there + core]).astype(jnp.int32)
        shares.append((k, *backward(both, gg, gu, wg, wu, part)))

    route = route + other_core(route)
    route = route + sum(chip_shift(route, k) for k in range(1, chips))
    high = route.astype(BF16)
    low = (route - high.astype(F32)).astype(BF16)
    lane = lax.broadcasted_iota(jnp.int32, route.shape, 1)
    extra = jnp.where(lane == 0, high, low)

    width = part // RETURN_CHUNKS
    came = []
    for c in range(RETURN_CHUNKS):
        cut = slice(c * width, (c + 1) * width)
        total = None
        for k, send, keep in shares:
            summed = keep[:, cut] + other_core(send[:, cut]).astype(F32)
            if k:
                summed = chip_shift(summed.astype(BF16), k).astype(F32)
            total = summed if total is None else total + summed
        total = total.astype(BF16)
        if c == 0:
            total = jnp.concatenate([total, extra], axis=1)
        came.append(over_exp(total))

    own_grad, route_full = combine(
        expert_ids, route_weights, pick, came, expert_count, part
    )
    columns = top_count // seq_count
    own_route = lax.dynamic_slice_in_dim(route_full, seq_at * columns, columns, 1)
    return own_grad, own_route


def solution(mesh):
    in_specs = (
        P("exp", "seq"),
        P("exp", "seq"),
        P("exp", None),
        P("exp", None),
        P("exp", None, "seq"),
        P("exp", None, "seq"),
        P("exp", "seq", None),
    )
    out_specs = (P("exp", "seq"), P("exp", "seq"))
    return jax.shard_map(local, mesh=mesh, in_specs=in_specs, out_specs=out_specs, check_vma=False)
```

```python
import functools

import jax
import jax.numpy as jnp
from jax import lax
from jax.experimental import pallas as pl
from jax.experimental.pallas import tpu as pltpu
from jax.sharding import PartitionSpec as P

CONTRACT = (((1,), (1,)), ((), ()))
BF16 = jnp.bfloat16
F32 = jnp.float32
VMEM_BYTES = 16 * 1024 * 1024
EXTRA = 128
GROUPS = 8


def params():
    return pltpu.CompilerParams(vmem_limit_bytes=VMEM_BYTES)


def write_pieces(rows, refs):
    most = refs[0].shape[0]
    for s, ref in enumerate(refs):
        ref[...] = rows[s * most : (s + 1) * most].astype(BF16)


def pack_kernel(ids_ref, x_ref, place_ref, *pieces, experts, most):
    ids = ids_ref[...]
    tokens = ids.shape[1]
    named = jnp.min(ids, axis=0, keepdims=True)
    hot = (named == lax.broadcasted_iota(jnp.int32, (experts, tokens), 0)).astype(F32)
    rows = lax.broadcasted_iota(jnp.int32, (tokens, tokens), 0)
    cols = lax.broadcasted_iota(jnp.int32, (tokens, tokens), 1)
    before = (rows < cols).astype(F32).astype(BF16)
    earlier = jnp.dot(hot.astype(BF16), before, preferred_element_type=F32)
    rank = jnp.sum(earlier * hot, axis=0, keepdims=True).astype(jnp.int32)
    target = jnp.where(named < experts, (named ^ lax.axis_index("exp")) * most + rank, -1)
    slots = lax.broadcasted_iota(jnp.int32, (experts * most, tokens), 0)
    place = (target == slots).astype(F32).astype(BF16)
    place_ref[...] = place
    write_pieces(jnp.dot(place, x_ref[...], preferred_element_type=F32), pieces)


def pack_again_kernel(place_ref, dy_ref, after_ref, *pieces):
    write_pieces(jnp.dot(place_ref[...], dy_ref[...], preferred_element_type=F32), pieces)


def pack(ids_t, x, experts, most):
    slots = experts * most
    tokens, width = x.shape
    place, *pieces = pl.pallas_call(
        functools.partial(pack_kernel, experts=experts, most=most),
        out_shape=[jax.ShapeDtypeStruct((slots, tokens), BF16)]
        + [jax.ShapeDtypeStruct((most, width), BF16)] * experts,
        compiler_params=params(),
        name="pack",
    )(ids_t, x)
    return place, pieces


def pack_again(place, dy, experts, after):
    slots = place.shape[0]
    whole = pl.BlockSpec(memory_space=pltpu.VMEM)
    return pl.pallas_call(
        pack_again_kernel,
        in_specs=[whole, whole, pl.BlockSpec(memory_space=pl.ANY)],
        out_shape=[jax.ShapeDtypeStruct((slots // experts, dy.shape[1]), BF16)] * experts,
        compiler_params=params(),
        name="pack_again",
    )(place, dy, after)


def combine_kernel(ids_ref, own_ids_ref, weights_ref, place_ref, *refs, experts, count):
    came = jnp.concatenate([ref[...] for ref in refs[:count]], axis=0)
    grad_ref, route_ref = refs[count:]
    tokens, width = grad_ref.shape
    weight = jnp.sum(jnp.where(ids_ref[...] < experts, weights_ref[...], 0.0), axis=0, keepdims=True)
    column = jnp.broadcast_to(weight, (tokens, tokens)).T[:, :1]
    pick = place_ref[...].astype(F32).T.astype(BF16)
    taken = jnp.dot(pick, came, preferred_element_type=F32)
    grad_ref[...] = (column * taken[:, :width]).astype(BF16)
    extra = taken[:, width:].T
    total = extra[0:1] + extra[1:2]
    route_ref[...] = jnp.where(own_ids_ref[...] < experts, total, 0.0)


def combine(ids_t, own_ids_t, weights_t, place, came, experts, width):
    tokens = ids_t.shape[1]
    return pl.pallas_call(
        functools.partial(combine_kernel, experts=experts, count=len(came)),
        out_shape=(
            jax.ShapeDtypeStruct((tokens, width), BF16),
            jax.ShapeDtypeStruct(own_ids_t.shape, F32),
        ),
        compiler_params=params(),
        name="combine",
    )(ids_t, own_ids_t, weights_t, place, *came)


def local(tokens, out_grad, expert_ids, route_weights, gate_proj, up_proj, down_proj):
    seq_count = lax.axis_size("seq")
    exp_count = lax.axis_size("exp")
    tok_dev, part = tokens.shape
    top_count = expert_ids.shape[1]
    expert_count = exp_count * gate_proj.shape[0]
    most = max(2, 2 * ((tok_dev + expert_count - 1) // expert_count))
    wg, wu, wd = gate_proj[0], up_proj[0], down_proj[0]
    chips = seq_count // 2
    per_group = max(1, exp_count // GROUPS)
    groups = exp_count // per_group

    seq_at = lax.axis_index("seq")
    core = seq_at % 2
    chip = seq_at // 2

    def other_core(value):
        return lax.ppermute(value, "seq", [(s, s ^ 1) for s in range(seq_count)])

    def chip_shift(value, k):
        return lax.ppermute(value, "seq", [(s, (s + 2 * k) % seq_count) for s in range(seq_count)])

    def exp_swap(value, s):
        return lax.ppermute(value, "exp", [(e, e ^ s) for e in range(exp_count)]) if s else value

    def joined(values, axis=0):
        return values[0] if len(values) == 1 else jnp.concatenate(values, axis=axis)

    def spread(pieces):
        came = [exp_swap(piece, s) for s, piece in enumerate(pieces)]
        came = [joined(came[g * per_group : (g + 1) * per_group]) for g in range(groups)]
        shares = [joined(came)]
        for k in range(1, chips):
            shares.append(joined([chip_shift(value, k) for value in came]))
        return came, [(share, other_core(share)) for share in shares]

    def quarter(k):
        from_chip = (chip - k) % chips
        return from_chip * 2 + core, from_chip * 2 + 1 - core

    def over_width(shares, weight, axis):
        total = None
        for k, pair in enumerate(shares):
            for rows, at in zip(pair, quarter(k)):
                block = lax.dynamic_slice_in_dim(weight, at * part, part, axis)
                term = lax.dot_general(
                    rows, block, (((1,), (axis,)), ((), ())), preferred_element_type=F32
                )
                total = term if total is None else total + term
        return total

    ids_t = expert_ids.T
    weights_t = route_weights.T
    columns = top_count // seq_count
    own_ids_t = lax.dynamic_slice_in_dim(ids_t, seq_at * columns, columns, 0)

    place, pieces_x = pack(ids_t, tokens, expert_count, most)
    came_x, shares_x = spread(pieces_x)
    pieces_dy = pack_again(place, out_grad, expert_count, came_x[groups // 2])
    _, shares_dy = spread(pieces_dy)

    pre_gate = over_width(shares_x, wg, 0)
    pre_up = over_width(shares_x, wu, 0)
    back_grad = over_width(shares_dy, wd, 1)

    sig = jax.nn.sigmoid(pre_gate)
    active = pre_gate * sig
    grad_gate = (back_grad * pre_up * sig * (1.0 + pre_gate * (1.0 - sig))).astype(BF16)
    grad_up = (back_grad * active).astype(BF16)
    route = jnp.sum(active * pre_up * back_grad, axis=-1)

    def block_grad(at):
        gate = lax.dynamic_slice_in_dim(wg, at * part, part, 0)
        up = lax.dynamic_slice_in_dim(wu, at * part, part, 0)
        return lax.dot_general(
            grad_gate, gate, CONTRACT, preferred_element_type=F32
        ) + lax.dot_general(grad_up, up, CONTRACT, preferred_element_type=F32)

    def chip_sum(k):
        there = (chip + k) % chips * 2
        sent = other_core(block_grad(there + 1 - core).astype(BF16))
        return block_grad(there + core) + sent.astype(F32)

    group_rows = per_group * most
    arrived = []
    for k in range(1, chips):
        summed = chip_sum(k).astype(BF16)
        arrived.append(
            [
                chip_shift(summed[g * group_rows : (g + 1) * group_rows], k)
                for g in range(groups)
            ]
        )
    own = chip_sum(0)

    route = route + other_core(route)
    route = route + sum(chip_shift(route, k) for k in range(1, chips))
    high = route.astype(BF16)
    low = (route - high.astype(F32)).astype(BF16)
    lane = lax.broadcasted_iota(jnp.int32, (route.shape[0], EXTRA), 1)
    extra = jnp.where(lane == 0, high[:, None], jnp.where(lane == 1, low[:, None], 0))

    came = []
    for g in range(groups):
        cut = slice(g * group_rows, (g + 1) * group_rows)
        total = own[cut]
        for values in arrived:
            total = total + values[g].astype(F32)
        total = jnp.concatenate([total.astype(BF16), extra[cut]], axis=1)
        for j in range(per_group):
            came.append(exp_swap(total[j * most : (j + 1) * most], g * per_group + j))

    own_grad, own_route_t = combine(
        ids_t, own_ids_t, weights_t, place, came, expert_count, part
    )
    return own_grad, own_route_t.T


def solution(mesh):
    in_specs = (
        P("exp", "seq"),
        P("exp", "seq"),
        P("exp", None),
        P("exp", None),
        P("exp", None, "seq"),
        P("exp", None, "seq"),
        P("exp", "seq", None),
    )
    out_specs = (P("exp", "seq"), P("exp", "seq"))
    return jax.shard_map(local, mesh=mesh, in_specs=in_specs, out_specs=out_specs, check_vma=False)
```

```python
import functools

import jax
import jax.numpy as jnp
from jax import lax
from jax.experimental import pallas as pl
from jax.experimental.pallas import tpu as pltpu
from jax.sharding import PartitionSpec as P

CONTRACT = (((1,), (1,)), ((), ()))
BF16 = jnp.bfloat16
F32 = jnp.float32
VMEM_BYTES = 16 * 1024 * 1024
EXTRA = 128


def params():
    return pltpu.CompilerParams(vmem_limit_bytes=VMEM_BYTES)


def write_pieces(rows, refs):
    most = refs[0].shape[0]
    for s, ref in enumerate(refs):
        ref[...] = rows[s * most : (s + 1) * most].astype(BF16)


def pack_kernel(ids_ref, x_ref, place_ref, *pieces, experts, most):
    ids = ids_ref[...]
    tokens = ids.shape[1]
    named = jnp.min(ids, axis=0, keepdims=True)
    hot = (named == lax.broadcasted_iota(jnp.int32, (experts, tokens), 0)).astype(F32)
    rows = lax.broadcasted_iota(jnp.int32, (tokens, tokens), 0)
    cols = lax.broadcasted_iota(jnp.int32, (tokens, tokens), 1)
    before = (rows < cols).astype(F32).astype(BF16)
    earlier = jnp.dot(hot.astype(BF16), before, preferred_element_type=F32)
    rank = jnp.sum(earlier * hot, axis=0, keepdims=True).astype(jnp.int32)
    target = jnp.where(named < experts, (named ^ lax.axis_index("exp")) * most + rank, -1)
    slots = lax.broadcasted_iota(jnp.int32, (experts * most, tokens), 0)
    place = (target == slots).astype(F32).astype(BF16)
    place_ref[...] = place
    write_pieces(jnp.dot(place, x_ref[...], preferred_element_type=F32), pieces)


def pack_again_kernel(place_ref, dy_ref, *refs, first, gates):
    pieces = refs[gates:]
    most = pieces[0].shape[0]
    place = place_ref[first * most : (first + len(pieces)) * most]
    write_pieces(jnp.dot(place, dy_ref[...], preferred_element_type=F32), pieces)


def pack(ids_t, x, experts, most):
    slots = experts * most
    tokens, width = x.shape
    place, *pieces = pl.pallas_call(
        functools.partial(pack_kernel, experts=experts, most=most),
        out_shape=[jax.ShapeDtypeStruct((slots, tokens), BF16)]
        + [jax.ShapeDtypeStruct((most, width), BF16)] * experts,
        compiler_params=params(),
        name="pack",
    )(ids_t, x)
    return place, pieces


def pack_again(place, dy, experts, group, after):
    most = place.shape[0] // experts
    whole = pl.BlockSpec(memory_space=pltpu.VMEM)
    return pl.pallas_call(
        functools.partial(pack_again_kernel, first=group[0], gates=len(after)),
        in_specs=[whole, whole] + [pl.BlockSpec(memory_space=pl.ANY)] * len(after),
        out_shape=[jax.ShapeDtypeStruct((most, dy.shape[1]), BF16)] * len(group),
        compiler_params=params(),
        name="pack_again",
    )(place, dy, *after)


def total_kernel(keep_ref, sent_ref, extra_ref, *refs, count):
    total = keep_ref[...] + sent_ref[...].astype(F32)
    for ref in refs[:count]:
        total += ref[...].astype(F32)
    total = total.astype(BF16)
    extra = extra_ref[...]
    pieces = refs[count:]
    most = pieces[0].shape[0]
    width = total.shape[1]
    for j, ref in enumerate(pieces):
        ref[:, :width] = total[j * most : (j + 1) * most]
        ref[:, width:] = extra[j * most : (j + 1) * most]


def totals(keep, sent, extra, arrived, group, most):
    rows = len(group) * most
    width = keep.shape[1]
    block = group[0] // len(group)

    def rows_of(value):
        return pl.BlockSpec((rows, value.shape[1]), lambda i: (block, 0))

    whole = pl.BlockSpec((rows, width), lambda i: (0, 0))
    piece = pl.BlockSpec((most, width + EXTRA), lambda i: (0, 0))
    return pl.pallas_call(
        functools.partial(total_kernel, count=len(arrived)),
        grid=(1,),
        in_specs=[rows_of(keep), rows_of(sent), rows_of(extra)] + [whole] * len(arrived),
        out_specs=[piece] * len(group),
        out_shape=[jax.ShapeDtypeStruct((most, width + EXTRA), BF16)] * len(group),
        compiler_params=params(),
        name="totals",
    )(keep, sent, extra, *arrived)


def combine_kernel(ids_ref, own_ids_ref, weights_ref, place_ref, *refs, experts, count):
    came = jnp.concatenate([ref[...] for ref in refs[:count]], axis=0)
    grad_ref, route_ref = refs[count:]
    tokens, width = grad_ref.shape
    weight = jnp.sum(jnp.where(ids_ref[...] < experts, weights_ref[...], 0.0), axis=0, keepdims=True)
    column = jnp.broadcast_to(weight, (tokens, tokens)).T[:, :1]
    pick = place_ref[...].astype(F32).T.astype(BF16)
    taken = jnp.dot(pick, came, preferred_element_type=F32)
    grad_ref[...] = (column * taken[:, :width]).astype(BF16)
    extra = taken[:, width:].T
    total = extra[0:1] + extra[1:2]
    route_ref[...] = jnp.where(own_ids_ref[...] < experts, total, 0.0)


def combine(ids_t, own_ids_t, weights_t, place, came, experts, width):
    tokens = ids_t.shape[1]
    return pl.pallas_call(
        functools.partial(combine_kernel, experts=experts, count=len(came)),
        out_shape=(
            jax.ShapeDtypeStruct((tokens, width), BF16),
            jax.ShapeDtypeStruct(own_ids_t.shape, F32),
        ),
        compiler_params=params(),
        name="combine",
    )(ids_t, own_ids_t, weights_t, place, *came)


def local(tokens, out_grad, expert_ids, route_weights, gate_proj, up_proj, down_proj):
    seq_count = lax.axis_size("seq")
    exp_count = lax.axis_size("exp")
    tok_dev, part = tokens.shape
    top_count = expert_ids.shape[1]
    expert_count = exp_count * gate_proj.shape[0]
    most = max(2, 2 * ((tok_dev + expert_count - 1) // expert_count))
    wg, wu, wd = gate_proj[0], up_proj[0], down_proj[0]
    chips = seq_count // 2
    half = exp_count // 2
    quarter = max(1, half // 2)
    groups = [range(0, half), range(half, half + quarter), range(half + quarter, exp_count)]
    groups = [group for group in groups if len(group)]

    seq_at = lax.axis_index("seq")
    core = seq_at % 2
    chip = seq_at // 2

    def other_core(value):
        return lax.ppermute(value, "seq", [(s, s ^ 1) for s in range(seq_count)])

    def chip_shift(value, k):
        return lax.ppermute(value, "seq", [(s, (s + 2 * k) % seq_count) for s in range(seq_count)])

    def exp_swap(value, s):
        return lax.ppermute(value, "exp", [(e, e ^ s) for e in range(exp_count)]) if s else value

    def joined(values, axis=0):
        return values[0] if len(values) == 1 else jnp.concatenate(values, axis=axis)

    def blocks_from(k):
        from_chip = (chip - k) % chips
        return from_chip * 2 + core, from_chip * 2 + 1 - core

    def over_width(shares, weight, axis):
        total = None
        for k, pair in enumerate(shares):
            for rows, at in zip(pair, blocks_from(k)):
                block = lax.dynamic_slice_in_dim(weight, at * part, part, axis)
                term = lax.dot_general(
                    rows, block, (((1,), (axis,)), ((), ())), preferred_element_type=F32
                )
                total = term if total is None else total + term
        return total

    ids_t = expert_ids.T
    weights_t = route_weights.T
    columns = top_count // seq_count
    own_ids_t = lax.dynamic_slice_in_dim(ids_t, seq_at * columns, columns, 0)

    def from_chips(came):
        return [
            [chip_shift(joined([came[s] for s in group]), k) for group in groups]
            for k in range(1, chips)
        ]

    place, pieces_x = pack(ids_t, tokens, expert_count, most)
    came_x = [exp_swap(piece, s) for s, piece in enumerate(pieces_x)]
    shares_x = []
    for share in [joined(came_x)] + [joined(values) for values in from_chips(came_x)]:
        shares_x.append((share, other_core(share)))

    came_dy = [None] * exp_count
    for group in groups[1:] + groups[:1]:
        after = [came_x[s] for s in (groups[-1] if group is groups[0] else group)]
        pieces = pack_again(place, out_grad, expert_count, group, after)
        for s, piece in zip(group, pieces):
            came_dy[s] = exp_swap(piece, s)
    own_dy = joined(came_dy)
    shares_dy = [(own_dy, other_core(own_dy))]
    for values in from_chips(came_dy):
        shares_dy.append((joined(values), joined([other_core(value) for value in values])))

    pre_gate = over_width(shares_x, wg, 0)
    pre_up = over_width(shares_x, wu, 0)
    back_grad = over_width(shares_dy, wd, 1)

    sig = jax.nn.sigmoid(pre_gate)
    active = pre_gate * sig
    grad_gate = (back_grad * pre_up * sig * (1.0 + pre_gate * (1.0 - sig))).astype(BF16)
    grad_up = (back_grad * active).astype(BF16)
    route = jnp.sum(active * pre_up * back_grad, axis=-1)

    def block_grad(at):
        gate = lax.dynamic_slice_in_dim(wg, at * part, part, 0)
        up = lax.dynamic_slice_in_dim(wu, at * part, part, 0)
        return lax.dot_general(
            grad_gate, gate, CONTRACT, preferred_element_type=F32
        ) + lax.dot_general(grad_up, up, CONTRACT, preferred_element_type=F32)

    def chip_part(k):
        there = (chip + k) % chips * 2
        sent = other_core(block_grad(there + 1 - core).astype(BF16))
        return block_grad(there + core), sent

    arrived = []
    for k in range(1, chips):
        keep, sent = chip_part(k)
        summed = (keep + sent.astype(F32)).astype(BF16)
        arrived.append(
            [chip_shift(summed[group[0] * most : (group[-1] + 1) * most], k) for group in groups]
        )
    keep, sent = chip_part(0)

    route = route + other_core(route)
    route = route + sum(chip_shift(route, k) for k in range(1, chips))
    high = route.astype(BF16)
    low = (route - high.astype(F32)).astype(BF16)
    lane = lax.broadcasted_iota(jnp.int32, (route.shape[0], EXTRA), 1)
    extra = jnp.where(lane == 0, high[:, None], jnp.where(lane == 1, low[:, None], 0))

    came = [None] * exp_count
    for g in list(range(1, len(groups))) + [0]:
        values = [from_chip[g] for from_chip in arrived]
        pieces = totals(keep, sent, extra, values, groups[g], most)
        for s, piece in zip(groups[g], pieces):
            came[s] = exp_swap(piece, s)

    own_grad, own_route_t = combine(
        ids_t, own_ids_t, weights_t, place, came, expert_count, part
    )
    return own_grad, own_route_t.T


def solution(mesh):
    in_specs = (
        P("exp", "seq"),
        P("exp", "seq"),
        P("exp", None),
        P("exp", None),
        P("exp", None, "seq"),
        P("exp", None, "seq"),
        P("exp", "seq", None),
    )
    out_specs = (P("exp", "seq"), P("exp", "seq"))
    return jax.shard_map(local, mesh=mesh, in_specs=in_specs, out_specs=out_specs, check_vma=False)
```

```python
import functools

import jax
import jax.numpy as jnp
from jax import lax
from jax.experimental import pallas as pl
from jax.experimental.pallas import tpu as pltpu
from jax.sharding import PartitionSpec as P

CONTRACT = (((1,), (1,)), ((), ()))
BF16 = jnp.bfloat16
F32 = jnp.float32
VMEM_BYTES = 16 * 1024 * 1024
EXTRA = 128


def params():
    return pltpu.CompilerParams(vmem_limit_bytes=VMEM_BYTES)


def write_pieces(place, values, refs):
    most = refs[0].shape[0]
    at = 0
    for value in values:
        rows = jnp.dot(place, value, preferred_element_type=F32)
        width = rows.shape[1]
        for j, ref in enumerate(refs):
            ref[:, at : at + width] = rows[j * most : (j + 1) * most].astype(BF16)
        at += width


def pack_kernel(ids_ref, x_ref, dy_ref, place_ref, *pieces, experts, most):
    ids = ids_ref[...]
    tokens = ids.shape[1]
    named = jnp.min(ids, axis=0, keepdims=True)
    hot = (named == lax.broadcasted_iota(jnp.int32, (experts, tokens), 0)).astype(F32)
    rows = lax.broadcasted_iota(jnp.int32, (tokens, tokens), 0)
    cols = lax.broadcasted_iota(jnp.int32, (tokens, tokens), 1)
    before = (rows < cols).astype(F32).astype(BF16)
    earlier = jnp.dot(hot.astype(BF16), before, preferred_element_type=F32)
    rank = jnp.sum(earlier * hot, axis=0, keepdims=True).astype(jnp.int32)
    target = jnp.where(named < experts, (named ^ lax.axis_index("exp")) * most + rank, -1)
    slots = lax.broadcasted_iota(jnp.int32, (experts * most, tokens), 0)
    place = (target == slots).astype(F32).astype(BF16)
    place_ref[...] = place
    write_pieces(place[: len(pieces) * most], (x_ref[...], dy_ref[...]), pieces)


def pack(ids_t, x, dy, experts, most, count):
    tokens, width = x.shape
    place, *pieces = pl.pallas_call(
        functools.partial(pack_kernel, experts=experts, most=most),
        out_shape=[jax.ShapeDtypeStruct((experts * most, tokens), BF16)]
        + [jax.ShapeDtypeStruct((most, 2 * width), BF16)] * count,
        compiler_params=params(),
        name="pack",
    )(ids_t, x, dy)
    return place, pieces


def pack_again_kernel(place_ref, value_ref, *refs, first, gates):
    pieces = refs[gates:]
    most = pieces[0].shape[0]
    place = place_ref[first * most : (first + len(pieces)) * most]
    write_pieces(place, (value_ref[...],), pieces)


def pack_again(place, value, experts, group, after):
    most = place.shape[0] // experts
    whole = pl.BlockSpec(memory_space=pltpu.VMEM)
    return pl.pallas_call(
        functools.partial(pack_again_kernel, first=group[0], gates=len(after)),
        in_specs=[whole, whole] + [pl.BlockSpec(memory_space=pl.ANY)] * len(after),
        out_shape=[jax.ShapeDtypeStruct((most, value.shape[1]), BF16)] * len(group),
        compiler_params=params(),
        name="pack_again",
    )(place, value, *after)


def copy_kernel(*refs, count, gates):
    for taken, given in zip(refs[:count], refs[count + gates :]):
        given[...] = taken[...]


def copied(values, after):
    whole = pl.BlockSpec(memory_space=pltpu.VMEM)
    return pl.pallas_call(
        functools.partial(copy_kernel, count=len(values), gates=len(after)),
        in_specs=[whole] * len(values) + [pl.BlockSpec(memory_space=pl.ANY)] * len(after),
        out_shape=[jax.ShapeDtypeStruct(value.shape, value.dtype) for value in values],
        compiler_params=params(),
        name="copied",
    )(*values, *after)


def total_kernel(keep_ref, sent_ref, extra_ref, *refs, count):
    total = keep_ref[...] + sent_ref[...].astype(F32)
    for ref in refs[:count]:
        total += ref[...].astype(F32)
    total = total.astype(BF16)
    extra = extra_ref[...]
    pieces = refs[count:]
    most = pieces[0].shape[0]
    width = total.shape[1]
    for j, ref in enumerate(pieces):
        ref[:, :width] = total[j * most : (j + 1) * most]
        ref[:, width:] = extra[j * most : (j + 1) * most]


def totals(keep, sent, extra, arrived, group, most):
    rows = len(group) * most
    width = keep.shape[1]
    block = group[0] // len(group)

    def rows_of(value):
        return pl.BlockSpec((rows, value.shape[1]), lambda i: (block, 0))

    whole = pl.BlockSpec((rows, width), lambda i: (0, 0))
    piece = pl.BlockSpec((most, width + EXTRA), lambda i: (0, 0))
    return pl.pallas_call(
        functools.partial(total_kernel, count=len(arrived)),
        grid=(1,),
        in_specs=[rows_of(keep), rows_of(sent), rows_of(extra)] + [whole] * len(arrived),
        out_specs=[piece] * len(group),
        out_shape=[jax.ShapeDtypeStruct((most, width + EXTRA), BF16)] * len(group),
        compiler_params=params(),
        name="totals",
    )(keep, sent, extra, *arrived)


def combine_kernel(ids_ref, own_ids_ref, weights_ref, place_ref, *refs, experts, count):
    came = jnp.concatenate([ref[...] for ref in refs[:count]], axis=0)
    grad_ref, route_ref = refs[count:]
    tokens, width = grad_ref.shape
    weight = jnp.sum(jnp.where(ids_ref[...] < experts, weights_ref[...], 0.0), axis=0, keepdims=True)
    column = jnp.broadcast_to(weight, (tokens, tokens)).T[:, :1]
    pick = place_ref[...].astype(F32).T.astype(BF16)
    taken = jnp.dot(pick, came, preferred_element_type=F32)
    grad_ref[...] = (column * taken[:, :width]).astype(BF16)
    extra = taken[:, width:].T
    total = extra[0:1] + extra[1:2]
    route_ref[...] = jnp.where(own_ids_ref[...] < experts, total, 0.0)


def combine(ids_t, own_ids_t, weights_t, place, came, experts, width):
    tokens = ids_t.shape[1]
    return pl.pallas_call(
        functools.partial(combine_kernel, experts=experts, count=len(came)),
        out_shape=(
            jax.ShapeDtypeStruct((tokens, width), BF16),
            jax.ShapeDtypeStruct(own_ids_t.shape, F32),
        ),
        compiler_params=params(),
        name="combine",
    )(ids_t, own_ids_t, weights_t, place, *came)


def local(tokens, out_grad, expert_ids, route_weights, gate_proj, up_proj, down_proj):
    seq_count = lax.axis_size("seq")
    exp_count = lax.axis_size("exp")
    tok_dev, part = tokens.shape
    top_count = expert_ids.shape[1]
    expert_count = exp_count * gate_proj.shape[0]
    most = max(2, 2 * ((tok_dev + expert_count - 1) // expert_count))
    wg, wu, wd = gate_proj[0], up_proj[0], down_proj[0]
    chips = seq_count // 2
    cuts = sorted({exp_count * j // 4 for j in range(5)})
    groups = [range(start, stop) for start, stop in zip(cuts, cuts[1:])]
    last = groups[-1]

    seq_at = lax.axis_index("seq")
    core = seq_at % 2
    chip = seq_at // 2

    def other_core(value):
        return lax.ppermute(value, "seq", [(s, s ^ 1) for s in range(seq_count)])

    def chip_shift(value, k):
        return lax.ppermute(value, "seq", [(s, (s + 2 * k) % seq_count) for s in range(seq_count)])

    def exp_swap(value, s):
        return lax.ppermute(value, "exp", [(e, e ^ s) for e in range(exp_count)]) if s else value

    def joined(values, axis=0):
        return values[0] if len(values) == 1 else jnp.concatenate(values, axis=axis)

    def blocks_from(k):
        from_chip = (chip - k) % chips
        return from_chip * 2 + core, from_chip * 2 + 1 - core

    def over_width(shares, weight, axis):
        total = None
        for k, pair in enumerate(shares):
            for rows, at in zip(pair, blocks_from(k)):
                block = lax.dynamic_slice_in_dim(weight, at * part, part, axis)
                term = lax.dot_general(
                    rows, block, (((1,), (axis,)), ((), ())), preferred_element_type=F32
                )
                total = term if total is None else total + term
        return total

    ids_t = expert_ids.T
    weights_t = route_weights.T
    columns = top_count // seq_count
    own_ids_t = lax.dynamic_slice_in_dim(ids_t, seq_at * columns, columns, 0)

    def from_chips(rows):
        return [chip_shift(rows, k) for k in range(1, chips)]

    place, pieces = pack(ids_t, tokens, out_grad, expert_count, most, last[0])
    came = [exp_swap(piece, s) for s, piece in enumerate(pieces)]
    both = [joined([came[s] for s in group]) for group in groups[:-1]]
    both_chips = [from_chips(rows) for rows in both]

    def first_of(values, count):
        return [value for chip_values in values[:count] for value in chip_values[:1]]

    after = [came[s] for s in groups[-2]]
    pieces = pack_again(place, tokens, expert_count, last, after + first_of(both_chips, 1))
    last_x = [exp_swap(piece, s) for s, piece in zip(last, pieces)]
    after = last_x + first_of(both_chips[1:], 1)
    pieces = pack_again(place, out_grad, expert_count, last, after)
    last_dy = joined([exp_swap(piece, s) for s, piece in zip(last, pieces)])
    last_x = joined(last_x)
    last_x_chips = from_chips(last_x)
    after = first_of(both_chips[2:], 1) + last_x_chips[:1]
    last_dy_chips = from_chips(copied([last_dy], after)[0])

    def of_x(values):
        return [value[:, :part] for value in values]

    def of_dy(values):
        return [value[:, part:] for value in values]

    own_x = joined(of_x(both) + [last_x])
    own_dy = joined(of_dy(both) + [last_dy])
    shares_x = [(own_x, other_core(own_x))]
    shares_dy = [(own_dy, other_core(own_dy))]
    for k in range(chips - 1):
        here = [values[k] for values in both_chips]
        rows_x = joined(of_x(here) + [last_x_chips[k]])
        shares_x.append((rows_x, other_core(rows_x)))
        early_dy = joined(of_dy(here))
        late_dy = last_dy_chips[k]
        shares_dy.append(
            (joined([early_dy, late_dy]), joined([other_core(early_dy), other_core(late_dy)]))
        )

    pre_gate = over_width(shares_x, wg, 0)
    pre_up = over_width(shares_x, wu, 0)
    back_grad = over_width(shares_dy, wd, 1)

    sig = jax.nn.sigmoid(pre_gate)
    active = pre_gate * sig
    grad_gate = (back_grad * pre_up * sig * (1.0 + pre_gate * (1.0 - sig))).astype(BF16)
    grad_up = (back_grad * active).astype(BF16)
    route = jnp.sum(active * pre_up * back_grad, axis=-1)

    def block_grad(grads, at):
        gate = lax.dynamic_slice_in_dim(wg, at * part, part, 0)
        up = lax.dynamic_slice_in_dim(wu, at * part, part, 0)
        return lax.dot_general(
            grads[0], gate, CONTRACT, preferred_element_type=F32
        ) + lax.dot_general(grads[1], up, CONTRACT, preferred_element_type=F32)

    def chip_part(grads, k):
        there = (chip + k) % chips * 2
        sent = other_core(block_grad(grads, there + 1 - core).astype(BF16))
        return block_grad(grads, there + core), sent

    def rows_of(value, group):
        return value[group[0] * most : (group[-1] + 1) * most]

    grads = (grad_gate, grad_up)
    arrived, summed = [], []
    for k in range(1, chips):
        keep, sent = chip_part(grads, k)
        summed.append((keep + sent.astype(F32)).astype(BF16))
    order = [last, groups[-2], range(0, groups[-2][0])]
    for k, values in enumerate(summed, 1):
        there = []
        for group in order:
            rows = copied([rows_of(values, group)], there[-1:])[0]
            there.append(chip_shift(rows, k))
        arrived.append(there)
    if summed:
        grads = copied(grads, summed)
    keep, sent = chip_part(grads, 0)

    route = route + other_core(route)
    route = route + sum(chip_shift(route, k) for k in range(1, chips))
    high = route.astype(BF16)
    low = (route - high.astype(F32)).astype(BF16)
    lane = lax.broadcasted_iota(jnp.int32, (route.shape[0], EXTRA), 1)
    extra = jnp.where(lane == 0, high[:, None], jnp.where(lane == 1, low[:, None], 0))

    came = [None] * exp_count
    for g, group in enumerate(order):
        values = [from_chip[g] for from_chip in arrived]
        pieces = totals(keep, sent, extra, values, group, most)
        for s, piece in zip(group, pieces):
            came[s] = exp_swap(piece, s)

    own_grad, own_route_t = combine(
        ids_t, own_ids_t, weights_t, place, came, expert_count, part
    )
    return own_grad, own_route_t.T


def solution(mesh):
    in_specs = (
        P("exp", "seq"),
        P("exp", "seq"),
        P("exp", None),
        P("exp", None),
        P("exp", None, "seq"),
        P("exp", None, "seq"),
        P("exp", "seq", None),
    )
    out_specs = (P("exp", "seq"), P("exp", "seq"))
    return jax.shard_map(local, mesh=mesh, in_specs=in_specs, out_specs=out_specs, check_vma=False)
```

```python
import functools

import jax
import jax.numpy as jnp
from jax import lax
from jax.experimental import pallas as pl
from jax.experimental.pallas import tpu as pltpu
from jax.sharding import PartitionSpec as P

CONTRACT = (((1,), (1,)), ((), ()))
BF16 = jnp.bfloat16
F32 = jnp.float32
VMEM_BYTES = 16 * 1024 * 1024
EXTRA = 128


def params():
    return pltpu.CompilerParams(vmem_limit_bytes=VMEM_BYTES)


def write_pieces(place, values, refs):
    most = refs[0].shape[0]
    at = 0
    for value in values:
        rows = jnp.dot(place, value, preferred_element_type=F32)
        width = rows.shape[1]
        for j, ref in enumerate(refs):
            ref[:, at : at + width] = rows[j * most : (j + 1) * most].astype(BF16)
        at += width


def pack_kernel(ids_ref, x_ref, dy_ref, place_ref, *pieces, experts, most, sequence):
    ids = ids_ref[...]
    tokens = ids.shape[1]
    named = jnp.min(ids, axis=0, keepdims=True)
    hot = (named == lax.broadcasted_iota(jnp.int32, (experts, tokens), 0)).astype(F32)
    rows = lax.broadcasted_iota(jnp.int32, (tokens, tokens), 0)
    cols = lax.broadcasted_iota(jnp.int32, (tokens, tokens), 1)
    before = (rows < cols).astype(F32).astype(BF16)
    earlier = jnp.dot(hot.astype(BF16), before, preferred_element_type=F32)
    rank = jnp.sum(earlier * hot, axis=0, keepdims=True).astype(jnp.int32)
    distance = named ^ lax.axis_index("exp")
    at = jnp.zeros_like(distance)
    for position, s in enumerate(sequence):
        at = jnp.where(distance == s, position, at)
    target = jnp.where(named < experts, at * most + rank, -1)
    slots = lax.broadcasted_iota(jnp.int32, (experts * most, tokens), 0)
    place = (target == slots).astype(F32).astype(BF16)
    place_ref[...] = place
    write_pieces(place[: len(pieces) * most], (x_ref[...], dy_ref[...]), pieces)


def pack(ids_t, x, dy, experts, most, sequence, count):
    tokens, width = x.shape
    place, *pieces = pl.pallas_call(
        functools.partial(pack_kernel, experts=experts, most=most, sequence=sequence),
        out_shape=[jax.ShapeDtypeStruct((experts * most, tokens), BF16)]
        + [jax.ShapeDtypeStruct((most, 2 * width), BF16)] * count,
        compiler_params=params(),
        name="pack",
    )(ids_t, x, dy)
    return place, pieces


def pack_again_kernel(place_ref, x_ref, dy_ref, *refs, first, gates):
    pieces = refs[gates:]
    most = pieces[0].shape[0]
    place = place_ref[first * most : (first + len(pieces)) * most]
    write_pieces(place, (x_ref[...], dy_ref[...]), pieces)


def pack_again(place, x, dy, experts, first, count, after):
    most = place.shape[0] // experts
    whole = pl.BlockSpec(memory_space=pltpu.VMEM)
    return pl.pallas_call(
        functools.partial(pack_again_kernel, first=first, gates=len(after)),
        in_specs=[whole] * 3 + [pl.BlockSpec(memory_space=pl.ANY)] * len(after),
        out_shape=[jax.ShapeDtypeStruct((most, 2 * x.shape[1]), BF16)] * count,
        compiler_params=params(),
        name="pack_again",
    )(place, x, dy, *after)


def copy_kernel(*refs, count, gates):
    for taken, given in zip(refs[:count], refs[count + gates :]):
        given[...] = taken[...]


def copied(values, after):
    whole = pl.BlockSpec(memory_space=pltpu.VMEM)
    return pl.pallas_call(
        functools.partial(copy_kernel, count=len(values), gates=len(after)),
        in_specs=[whole] * len(values) + [pl.BlockSpec(memory_space=pl.ANY)] * len(after),
        out_shape=[jax.ShapeDtypeStruct(value.shape, value.dtype) for value in values],
        compiler_params=params(),
        name="copied",
    )(*values, *after)


def hold_kernel(weight_ref, held_ref, done):
    copy = pltpu.make_async_copy(weight_ref, held_ref, done)
    copy.start()
    copy.wait()


def held(weight):
    return pl.pallas_call(
        hold_kernel,
        in_specs=[pl.BlockSpec(memory_space=pltpu.HBM)],
        out_specs=pl.BlockSpec(memory_space=pl.ANY),
        out_shape=pltpu.VMEM(weight.shape, weight.dtype),
        scratch_shapes=[pltpu.SemaphoreType.DMA],
        compiler_params=params(),
        cost_estimate=pl.CostEstimate(
            flops=0, bytes_accessed=2 * weight.size * weight.dtype.itemsize, transcendentals=0
        ),
        name="held",
    )(weight)


def total_kernel(keep_ref, sent_ref, extra_ref, *refs, count):
    total = keep_ref[...] + sent_ref[...].astype(F32)
    for ref in refs[:count]:
        total += ref[...].astype(F32)
    total = total.astype(BF16)
    extra = extra_ref[...]
    pieces = refs[count:]
    most = pieces[0].shape[0]
    width = total.shape[1]
    for j, ref in enumerate(pieces):
        ref[:, :width] = total[j * most : (j + 1) * most]
        ref[:, width:] = extra[j * most : (j + 1) * most]


def totals(keep, sent, extra, arrived, first, count, most):
    rows = count * most
    width = keep.shape[1]
    block = first // count

    def rows_of(value):
        return pl.BlockSpec((rows, value.shape[1]), lambda i: (block, 0))

    whole = pl.BlockSpec((rows, width), lambda i: (0, 0))
    piece = pl.BlockSpec((most, width + EXTRA), lambda i: (0, 0))
    return pl.pallas_call(
        functools.partial(total_kernel, count=len(arrived)),
        grid=(1,),
        in_specs=[rows_of(keep), rows_of(sent), rows_of(extra)] + [whole] * len(arrived),
        out_specs=[piece] * count,
        out_shape=[jax.ShapeDtypeStruct((most, width + EXTRA), BF16)] * count,
        compiler_params=params(),
        name="totals",
    )(keep, sent, extra, *arrived)


def combine_kernel(ids_ref, own_ids_ref, weights_ref, place_ref, *refs, experts, count):
    came = jnp.concatenate([ref[...] for ref in refs[:count]], axis=0)
    grad_ref, route_ref = refs[count:]
    tokens, width = grad_ref.shape
    weight = jnp.sum(jnp.where(ids_ref[...] < experts, weights_ref[...], 0.0), axis=0, keepdims=True)
    column = jnp.broadcast_to(weight, (tokens, tokens)).T[:, :1]
    pick = place_ref[...].astype(F32).T.astype(BF16)
    taken = jnp.dot(pick, came, preferred_element_type=F32)
    grad_ref[...] = (column * taken[:, :width]).astype(BF16)
    extra = taken[:, width:].T
    total = extra[0:1] + extra[1:2]
    route_ref[...] = jnp.where(own_ids_ref[...] < experts, total, 0.0)


def combine(ids_t, own_ids_t, weights_t, place, came, experts, width):
    tokens = ids_t.shape[1]
    return pl.pallas_call(
        functools.partial(combine_kernel, experts=experts, count=len(came)),
        out_shape=(
            jax.ShapeDtypeStruct((tokens, width), BF16),
            jax.ShapeDtypeStruct(own_ids_t.shape, F32),
        ),
        compiler_params=params(),
        name="combine",
    )(ids_t, own_ids_t, weights_t, place, *came)


def local(tokens, out_grad, expert_ids, route_weights, gate_proj, up_proj, down_proj):
    seq_count = lax.axis_size("seq")
    exp_count = lax.axis_size("exp")
    tok_dev, part = tokens.shape
    top_count = expert_ids.shape[1]
    expert_count = exp_count * gate_proj.shape[0]
    most = max(2, 2 * ((tok_dev + expert_count - 1) // expert_count))
    wg, wu, wd = gate_proj[0], up_proj[0], down_proj[0]
    chips = seq_count // 2
    unit = exp_count // 8
    sequence = [u * unit + j for u in (0, 1, 2, 4, 3, 5, 6, 7) for j in range(unit)]

    seq_at = lax.axis_index("seq")
    core = seq_at % 2
    chip = seq_at // 2

    def other_core(value):
        return lax.ppermute(value, "seq", [(s, s ^ 1) for s in range(seq_count)])

    def chip_shift(value, k):
        return lax.ppermute(value, "seq", [(s, (s + 2 * k) % seq_count) for s in range(seq_count)])

    def exp_swap(value, s):
        return lax.ppermute(value, "exp", [(e, e ^ s) for e in range(exp_count)]) if s else value

    def joined(values, axis=0):
        return values[0] if len(values) == 1 else jnp.concatenate(values, axis=axis)

    def blocks_from(k):
        from_chip = (chip - k) % chips
        return from_chip * 2 + core, from_chip * 2 + 1 - core

    def over_width(shares, weight, axis):
        total = None
        for k, pair in enumerate(shares):
            for rows, at in zip(pair, blocks_from(k)):
                block = lax.dynamic_slice_in_dim(weight, at * part, part, axis)
                term = lax.dot_general(
                    rows, block, (((1,), (axis,)), ((), ())), preferred_element_type=F32
                )
                total = term if total is None else total + term
        return total

    ids_t = expert_ids.T
    weights_t = route_weights.T
    columns = top_count // seq_count
    own_ids_t = lax.dynamic_slice_in_dim(ids_t, seq_at * columns, columns, 0)

    def from_chips(rows):
        return [chip_shift(rows, k) for k in range(1, chips)]

    def swapped(pieces, first):
        return [exp_swap(piece, sequence[first + j]) for j, piece in enumerate(pieces)]

    def again(first, count, after):
        pieces = pack_again(place, tokens, out_grad, expert_count, first, count, after)
        return swapped(pieces, first)

    near = 2 * unit
    place, pieces = pack(
        ids_t, tokens, out_grad, expert_count, most, sequence, 2 * near
    )
    came = swapped(pieces, 0)
    wg = held(wg)
    came += again(2 * near, near, came[near - 1 : near] + [wg])
    rows = [joined(came[j * near : (j + 1) * near]) for j in range(3)]
    chip_rows = [from_chips(rows[0]), from_chips(rows[1])]
    wu = held(wu)
    came += again(3 * near, unit, came[2 * near - 1 : 2 * near] + chip_rows[0][:1] + [wu])
    wd = held(wd)
    came += again(3 * near + unit, unit, came[3 * near - 1 : 3 * near] + chip_rows[1][:1] + [wd])
    chip_rows.append(from_chips(copied([rows[2]], chip_rows[0][:1])[0]))
    rows.append(joined(came[3 * near : 3 * near + unit]))
    chip_rows.append(from_chips(copied([rows[3]], chip_rows[1][:1])[0]))
    end = joined(came[3 * near + unit :])
    end_x, end_dy = copied(
        [end[:, :part], end[:, part:]], chip_rows[2][:1] + chip_rows[3][:1]
    )
    chip_end_x, chip_end_dy = from_chips(end_x), from_chips(end_dy)

    def x_of(values, last):
        return joined([value[:, :part] for value in values] + [last])

    def dy_of(values, last):
        return joined([value[:, part:] for value in values] + [last])

    own_x, own_dy = x_of(rows, end[:, :part]), dy_of(rows, end[:, part:])
    shares_x = [(own_x, other_core(own_x))]
    shares_dy = [(own_dy, other_core(own_dy))]
    for k in range(chips - 1):
        here = [values[k] for values in chip_rows]
        rows_x = x_of(here, chip_end_x[k])
        shares_x.append((rows_x, other_core(rows_x)))
        rows_dy = dy_of(here, chip_end_dy[k])
        shares_dy.append((rows_dy, other_core(rows_dy)))

    pre_gate = over_width(shares_x, wg, 0)
    pre_up = over_width(shares_x, wu, 0)
    back_grad = over_width(shares_dy, wd, 1)

    sig = jax.nn.sigmoid(pre_gate)
    active = pre_gate * sig
    grad_gate = (back_grad * pre_up * sig * (1.0 + pre_gate * (1.0 - sig))).astype(BF16)
    grad_up = (back_grad * active).astype(BF16)
    route = jnp.sum(active * pre_up * back_grad, axis=-1)

    def block_grad(grads, at):
        gate = lax.dynamic_slice_in_dim(wg, at * part, part, 0)
        up = lax.dynamic_slice_in_dim(wu, at * part, part, 0)
        return lax.dot_general(
            grads[0], gate, CONTRACT, preferred_element_type=F32
        ) + lax.dot_general(grads[1], up, CONTRACT, preferred_element_type=F32)

    def chip_part(grads, k):
        there = (chip + k) % chips * 2
        sent = other_core(block_grad(grads, there + 1 - core).astype(BF16))
        return block_grad(grads, there + core), sent

    grads = (grad_gate, grad_up)
    summed = []
    for k in range(1, chips):
        keep, sent = chip_part(grads, k)
        summed.append((keep + sent.astype(F32)).astype(BF16))
    keep, sent = chip_part(copied(grads, summed), 0)

    route = route + other_core(route)
    route = route + sum(chip_shift(route, k) for k in range(1, chips))
    high = route.astype(BF16)
    low = (route - high.astype(F32)).astype(BF16)
    lane = lax.broadcasted_iota(jnp.int32, (route.shape[0], EXTRA), 1)
    extra = jnp.where(lane == 0, high[:, None], jnp.where(lane == 1, low[:, None], 0))

    back = [None] * exp_count
    after = []
    for first in range(exp_count - near, -1, -near):
        cut = slice(first * most, (first + near) * most)
        arrived = [
            chip_shift(copied([values[cut]], after)[0], k) for k, values in enumerate(summed, 1)
        ]
        pieces = totals(keep, sent, extra, arrived, first, near, most)
        back[first : first + near] = swapped(pieces, first)
        after = [pieces[0]]

    own_grad, own_route_t = combine(
        ids_t, own_ids_t, weights_t, place, back, expert_count, part
    )
    return own_grad, own_route_t.T


def solution(mesh):
    in_specs = (
        P("exp", "seq"),
        P("exp", "seq"),
        P("exp", None),
        P("exp", None),
        P("exp", None, "seq"),
        P("exp", None, "seq"),
        P("exp", "seq", None),
    )
    out_specs = (P("exp", "seq"), P("exp", "seq"))
    return jax.shard_map(local, mesh=mesh, in_specs=in_specs, out_specs=out_specs, check_vma=False)
```

```python
import functools

import jax
import jax.numpy as jnp
from jax import lax
from jax.experimental import pallas as pl
from jax.experimental.pallas import tpu as pltpu
from jax.sharding import PartitionSpec as P

CONTRACT = (((1,), (1,)), ((), ()))
BF16 = jnp.bfloat16
F32 = jnp.float32
VMEM_BYTES = 8 * 1024 * 1024
EXTRA = 128


def params():
    return pltpu.CompilerParams(vmem_limit_bytes=VMEM_BYTES)


def write_pieces(place, values, group, refs):
    most = refs[0].shape[0]
    start, stop = min(group), max(group) + 1
    at = 0
    for value in values:
        rows = jnp.dot(place[start * most : stop * most], value, preferred_element_type=F32)
        width = rows.shape[1]
        for s, ref in zip(group, refs):
            first = (s - start) * most
            ref[:, at : at + width] = rows[first : first + most].astype(BF16)
        at += width


def pack_kernel(ids_ref, x_ref, dy_ref, place_ref, *pieces, experts, most, group):
    ids = ids_ref[...]
    tokens = ids.shape[1]
    named = jnp.min(ids, axis=0, keepdims=True)
    hot = (named == lax.broadcasted_iota(jnp.int32, (experts, tokens), 0)).astype(F32)
    rows = lax.broadcasted_iota(jnp.int32, (tokens, tokens), 0)
    cols = lax.broadcasted_iota(jnp.int32, (tokens, tokens), 1)
    before = (rows < cols).astype(F32).astype(BF16)
    earlier = jnp.dot(hot.astype(BF16), before, preferred_element_type=F32)
    rank = jnp.sum(earlier * hot, axis=0, keepdims=True).astype(jnp.int32)
    target = jnp.where(named < experts, (named ^ lax.axis_index("exp")) * most + rank, -1)
    slots = lax.broadcasted_iota(jnp.int32, (experts * most, tokens), 0)
    place = (target == slots).astype(F32).astype(BF16)
    place_ref[...] = place
    write_pieces(place, (x_ref[...], dy_ref[...]), group, pieces)


def pack(ids_t, x, dy, experts, most, group):
    tokens, width = x.shape
    place, *pieces = pl.pallas_call(
        functools.partial(pack_kernel, experts=experts, most=most, group=group),
        out_shape=[jax.ShapeDtypeStruct((experts * most, tokens), BF16)]
        + [jax.ShapeDtypeStruct((most, 2 * width), BF16)] * len(group),
        compiler_params=params(),
        name="pack",
    )(ids_t, x, dy)
    return place, pieces


def pack_again_kernel(place_ref, x_ref, dy_ref, *refs, group, gates):
    write_pieces(place_ref[...], (x_ref[...], dy_ref[...]), group, refs[gates:])


def pack_again(place, x, dy, experts, group, after):
    most = place.shape[0] // experts
    whole = pl.BlockSpec(memory_space=pltpu.VMEM)
    return pl.pallas_call(
        functools.partial(pack_again_kernel, group=group, gates=len(after)),
        in_specs=[whole] * 3 + [pl.BlockSpec(memory_space=pl.ANY)] * len(after),
        out_shape=[jax.ShapeDtypeStruct((most, 2 * x.shape[1]), BF16)] * len(group),
        compiler_params=params(),
        name="pack_again",
    )(place, x, dy, *after)


def copy_kernel(*refs, count, gates):
    for taken, given in zip(refs[:count], refs[count + gates :]):
        given[...] = taken[...]


def copied(values, after):
    whole = pl.BlockSpec(memory_space=pltpu.VMEM)
    return pl.pallas_call(
        functools.partial(copy_kernel, count=len(values), gates=len(after)),
        in_specs=[whole] * len(values) + [pl.BlockSpec(memory_space=pl.ANY)] * len(after),
        out_shape=[jax.ShapeDtypeStruct(value.shape, value.dtype) for value in values],
        compiler_params=params(),
        name="copied",
    )(*values, *after)


def total_kernel(keep_ref, sent_ref, extra_ref, *refs, count):
    total = keep_ref[...] + sent_ref[...].astype(F32)
    for ref in refs[:count]:
        total += ref[...].astype(F32)
    total = total.astype(BF16)
    extra = extra_ref[...]
    pieces = refs[count:]
    most = pieces[0].shape[0]
    width = total.shape[1]
    for j, ref in enumerate(pieces):
        ref[:, :width] = total[j * most : (j + 1) * most]
        ref[:, width:] = extra[j * most : (j + 1) * most]


def totals(keep, sent, extra, arrived, first, count, most):
    rows = count * most
    width = keep.shape[1]
    block = first // count

    def rows_of(value):
        return pl.BlockSpec((rows, value.shape[1]), lambda i: (block, 0))

    whole = pl.BlockSpec((rows, width), lambda i: (0, 0))
    piece = pl.BlockSpec((most, width + EXTRA), lambda i: (0, 0))
    return pl.pallas_call(
        functools.partial(total_kernel, count=len(arrived)),
        grid=(1,),
        in_specs=[rows_of(keep), rows_of(sent), rows_of(extra)] + [whole] * len(arrived),
        out_specs=[piece] * count,
        out_shape=[jax.ShapeDtypeStruct((most, width + EXTRA), BF16)] * count,
        compiler_params=params(),
        name="totals",
    )(keep, sent, extra, *arrived)


def combine_kernel(ids_ref, own_ids_ref, weights_ref, place_ref, *refs, experts, count):
    came = jnp.concatenate([ref[...] for ref in refs[:count]], axis=0)
    grad_ref, route_ref = refs[count:]
    tokens, width = grad_ref.shape
    weight = jnp.sum(jnp.where(ids_ref[...] < experts, weights_ref[...], 0.0), axis=0, keepdims=True)
    column = jnp.broadcast_to(weight, (tokens, tokens)).T[:, :1]
    pick = place_ref[...].astype(F32).T.astype(BF16)
    taken = jnp.dot(pick, came, preferred_element_type=F32)
    grad_ref[...] = (column * taken[:, :width]).astype(BF16)
    extra = taken[:, width:].T
    total = extra[0:1] + extra[1:2]
    route_ref[...] = jnp.where(own_ids_ref[...] < experts, total, 0.0)


def combine(ids_t, own_ids_t, weights_t, place, came, experts, width):
    tokens = ids_t.shape[1]
    return pl.pallas_call(
        functools.partial(combine_kernel, experts=experts, count=len(came)),
        out_shape=(
            jax.ShapeDtypeStruct((tokens, width), BF16),
            jax.ShapeDtypeStruct(own_ids_t.shape, F32),
        ),
        compiler_params=params(),
        name="combine",
    )(ids_t, own_ids_t, weights_t, place, *came)


def local(tokens, out_grad, expert_ids, route_weights, gate_proj, up_proj, down_proj):
    seq_count = lax.axis_size("seq")
    exp_count = lax.axis_size("exp")
    tok_dev, part = tokens.shape
    top_count = expert_ids.shape[1]
    expert_count = exp_count * gate_proj.shape[0]
    most = max(2, 2 * ((tok_dev + expert_count - 1) // expert_count))
    wg, wu, wd = gate_proj[0], up_proj[0], down_proj[0]
    chips = seq_count // 2
    unit = exp_count // 8

    def of_units(*units):
        return [u * unit + j for u in units for j in range(unit)]

    seq_at = lax.axis_index("seq")
    core = seq_at % 2
    chip = seq_at // 2

    def other_core(value):
        return lax.ppermute(value, "seq", [(s, s ^ 1) for s in range(seq_count)])

    def chip_shift(value, k):
        return lax.ppermute(value, "seq", [(s, (s + 2 * k) % seq_count) for s in range(seq_count)])

    def exp_swap(value, s):
        return lax.ppermute(value, "exp", [(e, e ^ s) for e in range(exp_count)]) if s else value

    def joined(values, axis=0):
        return values[0] if len(values) == 1 else jnp.concatenate(values, axis=axis)

    def blocks_from(k):
        from_chip = (chip - k) % chips
        return from_chip * 2 + core, from_chip * 2 + 1 - core

    def over_width(shares, weight, axis):
        total = None
        for k, pair in enumerate(shares):
            for rows, at in zip(pair, blocks_from(k)):
                block = lax.dynamic_slice_in_dim(weight, at * part, part, axis)
                term = lax.dot_general(
                    rows, block, (((1,), (axis,)), ((), ())), preferred_element_type=F32
                )
                total = term if total is None else total + term
        return total

    ids_t = expert_ids.T
    weights_t = route_weights.T
    columns = top_count // seq_count
    own_ids_t = lax.dynamic_slice_in_dim(ids_t, seq_at * columns, columns, 0)

    def from_chips(rows):
        return [chip_shift(rows, k) for k in range(1, chips)]

    came = [None] * exp_count

    def send(pieces, group):
        for s, piece in zip(group, pieces):
            came[s] = exp_swap(piece, s)

    def send_more(group, after):
        send(pack_again(place, tokens, out_grad, expert_count, group, after), group)

    def arrived_of(group):
        return joined([came[s] for s in group])

    near = of_units(0, 1, 2, 4)
    place, pieces = pack(ids_t, tokens, out_grad, expert_count, most, near)
    send(pieces, near)
    pairs = [of_units(0, 1), of_units(2, 4), of_units(3, 5)]
    rows = {0: from_chips(arrived_of(pairs[0])), 1: from_chips(arrived_of(pairs[1]))}
    send_more(pairs[2], [came[pairs[0][-1]]])
    send_more(of_units(6), [came[pairs[1][-1]]] + rows[0][:1])
    send_more(of_units(7), [came[pairs[2][-1]]] + rows[1][:1])
    rows[2] = from_chips(copied([arrived_of(pairs[2])], rows[0][:1])[0])
    rows[3] = from_chips(copied([arrived_of(of_units(6))], rows[1][:1])[0])
    end = arrived_of(of_units(7))
    end_x, end_dy = copied([end[:, :part], end[:, part:]], rows[2][:1] + rows[3][:1])
    end_x, end_dy = from_chips(end_x), from_chips(end_dy)

    def in_order(k):
        found = {}
        for values, group in zip(
            (rows[0][k], rows[1][k], rows[2][k], rows[3][k]), pairs + [of_units(6)]
        ):
            for j, s in enumerate(group):
                found[s] = values[j * most : (j + 1) * most]
        early = [found[s] for s in sorted(found)]
        return (
            joined([value[:, :part] for value in early] + [end_x[k]]),
            joined([value[:, part:] for value in early] + [end_dy[k]]),
        )

    both = [(joined([v[:, :part] for v in came]), joined([v[:, part:] for v in came]))]
    both += [in_order(k) for k in range(chips - 1)]
    shares_x = [(x, other_core(x)) for x, _ in both]
    shares_dy = [(dy, other_core(dy)) for _, dy in both]

    pre_gate = over_width(shares_x, wg, 0)
    pre_up = over_width(shares_x, wu, 0)
    back_grad = over_width(shares_dy, wd, 1)

    sig = jax.nn.sigmoid(pre_gate)
    active = pre_gate * sig
    grad_gate = (back_grad * pre_up * sig * (1.0 + pre_gate * (1.0 - sig))).astype(BF16)
    grad_up = (back_grad * active).astype(BF16)
    route = jnp.sum(active * pre_up * back_grad, axis=-1)

    def block_grad(grads, at):
        gate = lax.dynamic_slice_in_dim(wg, at * part, part, 0)
        up = lax.dynamic_slice_in_dim(wu, at * part, part, 0)
        return lax.dot_general(
            grads[0], gate, CONTRACT, preferred_element_type=F32
        ) + lax.dot_general(grads[1], up, CONTRACT, preferred_element_type=F32)

    def chip_part(grads, k):
        there = (chip + k) % chips * 2
        sent = other_core(block_grad(grads, there + 1 - core).astype(BF16))
        return block_grad(grads, there + core), sent

    grads = (grad_gate, grad_up)
    summed = []
    for k in range(1, chips):
        keep, sent = chip_part(grads, k)
        summed.append((keep + sent.astype(F32)).astype(BF16))
    keep, sent = chip_part(copied(grads, summed), 0)

    if summed:
        route = copied([route.reshape(1, -1)], summed)[0].reshape(-1)
    route = route + other_core(route)
    route = route + sum(chip_shift(route, k) for k in range(1, chips))
    high = route.astype(BF16)
    low = (route - high.astype(F32)).astype(BF16)
    lane = lax.broadcasted_iota(jnp.int32, (route.shape[0], EXTRA), 1)
    extra = jnp.where(lane == 0, high[:, None], jnp.where(lane == 1, low[:, None], 0))

    back = [None] * exp_count
    half = exp_count // 2
    after = []
    for first in (half, 0):
        cut = slice(first * most, (first + half) * most)
        arrived = [
            chip_shift(copied([values[cut]], after)[0], k) for k, values in enumerate(summed, 1)
        ]
        pieces = totals(keep, sent, extra, arrived, first, half, most)
        for j, piece in enumerate(pieces):
            back[first + j] = exp_swap(piece, first + j)
        after = pieces[:1]

    own_grad, own_route_t = combine(
        ids_t, own_ids_t, weights_t, place, back, expert_count, part
    )
    return own_grad, own_route_t.T


def solution(mesh):
    in_specs = (
        P("exp", "seq"),
        P("exp", "seq"),
        P("exp", None),
        P("exp", None),
        P("exp", None, "seq"),
        P("exp", None, "seq"),
        P("exp", "seq", None),
    )
    out_specs = (P("exp", "seq"), P("exp", "seq"))
    return jax.shard_map(local, mesh=mesh, in_specs=in_specs, out_specs=out_specs, check_vma=False)
```

```python
import functools

import jax
import jax.numpy as jnp
from jax import lax
from jax.experimental import pallas as pl
from jax.experimental.pallas import tpu as pltpu
from jax.sharding import PartitionSpec as P

CONTRACT = (((1,), (1,)), ((), ()))
BF16 = jnp.bfloat16
F32 = jnp.float32
VMEM_BYTES = 12 * 1024 * 1024
EXTRA = 128


def params():
    return pltpu.CompilerParams(vmem_limit_bytes=VMEM_BYTES)


def write_pieces(place, values, group, refs):
    most = refs[0].shape[0]
    start, stop = min(group), max(group) + 1
    at = 0
    for value in values:
        rows = jnp.dot(place[start * most : stop * most], value, preferred_element_type=F32)
        width = rows.shape[1]
        for s, ref in zip(group, refs):
            first = (s - start) * most
            ref[:, at : at + width] = rows[first : first + most].astype(BF16)
        at += width


def pack_kernel(ids_ref, x_ref, dy_ref, place_ref, *pieces, experts, most, group):
    ids = ids_ref[...]
    tokens = ids.shape[1]
    named = jnp.min(ids, axis=0, keepdims=True)
    hot = (named == lax.broadcasted_iota(jnp.int32, (experts, tokens), 0)).astype(F32)
    rows = lax.broadcasted_iota(jnp.int32, (tokens, tokens), 0)
    cols = lax.broadcasted_iota(jnp.int32, (tokens, tokens), 1)
    before = (rows < cols).astype(F32).astype(BF16)
    earlier = jnp.dot(hot.astype(BF16), before, preferred_element_type=F32)
    rank = jnp.sum(earlier * hot, axis=0, keepdims=True).astype(jnp.int32)
    target = jnp.where(named < experts, (named ^ lax.axis_index("exp")) * most + rank, -1)
    slots = lax.broadcasted_iota(jnp.int32, (experts * most, tokens), 0)
    place = (target == slots).astype(F32).astype(BF16)
    place_ref[...] = place
    write_pieces(place, (x_ref[...], dy_ref[...]), group, pieces)


def pack(ids_t, x, dy, experts, most, group):
    tokens, width = x.shape
    place, *pieces = pl.pallas_call(
        functools.partial(pack_kernel, experts=experts, most=most, group=group),
        out_shape=[jax.ShapeDtypeStruct((experts * most, tokens), BF16)]
        + [jax.ShapeDtypeStruct((most, 2 * width), BF16)] * len(group),
        compiler_params=params(),
        name="pack",
    )(ids_t, x, dy)
    return place, pieces


def pack_again_kernel(place_ref, x_ref, dy_ref, *refs, group, gates):
    write_pieces(place_ref[...], (x_ref[...], dy_ref[...]), group, refs[gates:])


def pack_again(place, x, dy, experts, group, after):
    most = place.shape[0] // experts
    whole = pl.BlockSpec(memory_space=pltpu.VMEM)
    return pl.pallas_call(
        functools.partial(pack_again_kernel, group=group, gates=len(after)),
        in_specs=[whole] * 3 + [pl.BlockSpec(memory_space=pl.ANY)] * len(after),
        out_shape=[jax.ShapeDtypeStruct((most, 2 * x.shape[1]), BF16)] * len(group),
        compiler_params=params(),
        name="pack_again",
    )(place, x, dy, *after)


def copy_kernel(*refs, count, gates):
    for taken, given in zip(refs[:count], refs[count + gates :]):
        given[...] = taken[...]


def copied(values, after):
    whole = pl.BlockSpec(memory_space=pltpu.VMEM)
    return pl.pallas_call(
        functools.partial(copy_kernel, count=len(values), gates=len(after)),
        in_specs=[whole] * len(values) + [pl.BlockSpec(memory_space=pl.ANY)] * len(after),
        out_shape=[jax.ShapeDtypeStruct(value.shape, value.dtype) for value in values],
        compiler_params=params(),
        name="copied",
    )(*values, *after)


def added_kernel(keep_ref, sent_ref, *refs):
    refs[-1][...] = (keep_ref[...] + sent_ref[...].astype(F32)).astype(BF16)


def added(keep, sent, first, rows, after):
    width = keep.shape[1]
    block = pl.BlockSpec((rows, width), lambda i: (first // rows, 0))
    return pl.pallas_call(
        added_kernel,
        grid=(1,),
        in_specs=[block, block] + [pl.BlockSpec(memory_space=pl.ANY)] * len(after),
        out_specs=pl.BlockSpec((rows, width), lambda i: (0, 0)),
        out_shape=jax.ShapeDtypeStruct((rows, width), BF16),
        compiler_params=params(),
        name="added",
    )(keep, sent, *after)


def product_kernel(gate_ref, up_ref, wg_ref, wu_ref, out_ref, held, done, *, shift, other):
    _, chunks, size, _ = held.shape
    seq_at = lax.axis_index("seq")
    chips = lax.axis_size("seq") // 2
    core = lax.rem(seq_at, 2)
    there = lax.rem(lax.div(seq_at, 2) + shift, chips)
    block = there * 2 + (1 - core if other else core)

    def copy(which, chunk):
        rows = pl.ds(pl.multiple_of(block * (chunks * size) + chunk * size, size), size)
        return pltpu.make_async_copy(
            (wg_ref, wu_ref)[which].at[rows], held.at[which, chunk], done.at[which, chunk]
        )

    for chunk in range(chunks):
        copy(0, chunk).start()
        copy(1, chunk).start()
    for chunk in range(chunks):
        copy(0, chunk).wait()
        copy(1, chunk).wait()
        total = lax.dot_general(
            gate_ref[...], held[0, chunk], CONTRACT, preferred_element_type=F32
        ) + lax.dot_general(up_ref[...], held[1, chunk], CONTRACT, preferred_element_type=F32)
        out_ref[:, chunk * size : (chunk + 1) * size] = total.astype(out_ref.dtype)


def product(grads, wg, wu, part, shift, other, kind):
    slots, hidden = grads[0].shape
    size = next(size for size in (256, 128, part) if part % size == 0)
    chunks = part // size
    whole = pl.BlockSpec(memory_space=pltpu.VMEM)
    return pl.pallas_call(
        functools.partial(product_kernel, shift=shift, other=other),
        in_specs=[whole, whole] + [pl.BlockSpec(memory_space=pl.ANY)] * 2,
        out_specs=whole,
        out_shape=jax.ShapeDtypeStruct((slots, part), kind),
        scratch_shapes=[
            pltpu.VMEM((2, chunks, size, hidden), BF16),
            pltpu.SemaphoreType.DMA((2, chunks)),
        ],
        compiler_params=params(),
        cost_estimate=pl.CostEstimate(
            flops=4 * slots * hidden * part,
            bytes_accessed=4 * part * hidden,
            transcendentals=0,
        ),
        name="product",
    )(*grads, wg, wu)


def total_kernel(keep_ref, sent_ref, extra_ref, *refs, count):
    total = keep_ref[...] + sent_ref[...].astype(F32)
    for ref in refs[:count]:
        total += ref[...].astype(F32)
    total = total.astype(BF16)
    extra = extra_ref[...]
    pieces = refs[count:]
    most = pieces[0].shape[0]
    width = total.shape[1]
    for j, ref in enumerate(pieces):
        ref[:, :width] = total[j * most : (j + 1) * most]
        ref[:, width:] = extra[j * most : (j + 1) * most]


def totals(keep, sent, extra, arrived, first, count, most):
    rows = count * most
    width = keep.shape[1]
    block = first // count

    def rows_of(value):
        return pl.BlockSpec((rows, value.shape[1]), lambda i: (block, 0))

    whole = pl.BlockSpec((rows, width), lambda i: (0, 0))
    piece = pl.BlockSpec((most, width + EXTRA), lambda i: (0, 0))
    return pl.pallas_call(
        functools.partial(total_kernel, count=len(arrived)),
        grid=(1,),
        in_specs=[rows_of(keep), rows_of(sent), rows_of(extra)] + [whole] * len(arrived),
        out_specs=[piece] * count,
        out_shape=[jax.ShapeDtypeStruct((most, width + EXTRA), BF16)] * count,
        compiler_params=params(),
        name="totals",
    )(keep, sent, extra, *arrived)


def combine_kernel(ids_ref, own_ids_ref, weights_ref, place_ref, *refs, experts, count):
    came = jnp.concatenate([ref[...] for ref in refs[:count]], axis=0)
    grad_ref, route_ref = refs[count:]
    tokens, width = grad_ref.shape
    weight = jnp.sum(jnp.where(ids_ref[...] < experts, weights_ref[...], 0.0), axis=0, keepdims=True)
    column = jnp.broadcast_to(weight, (tokens, tokens)).T[:, :1]
    pick = place_ref[...].astype(F32).T.astype(BF16)
    taken = jnp.dot(pick, came, preferred_element_type=F32)
    grad_ref[...] = (column * taken[:, :width]).astype(BF16)
    extra = taken[:, width:].T
    total = extra[0:1] + extra[1:2]
    route_ref[...] = jnp.where(own_ids_ref[...] < experts, total, 0.0)


def combine(ids_t, own_ids_t, weights_t, place, came, experts, width):
    tokens = ids_t.shape[1]
    return pl.pallas_call(
        functools.partial(combine_kernel, experts=experts, count=len(came)),
        out_shape=(
            jax.ShapeDtypeStruct((tokens, width), BF16),
            jax.ShapeDtypeStruct(own_ids_t.shape, F32),
        ),
        compiler_params=params(),
        name="combine",
    )(ids_t, own_ids_t, weights_t, place, *came)


def local(tokens, out_grad, expert_ids, route_weights, gate_proj, up_proj, down_proj):
    seq_count = lax.axis_size("seq")
    exp_count = lax.axis_size("exp")
    tok_dev, part = tokens.shape
    top_count = expert_ids.shape[1]
    expert_count = exp_count * gate_proj.shape[0]
    most = max(2, 2 * ((tok_dev + expert_count - 1) // expert_count))
    wg, wu, wd = gate_proj[0], up_proj[0], down_proj[0]
    chips = seq_count // 2
    unit = exp_count // 8

    def of_units(*units):
        return [u * unit + j for u in units for j in range(unit)]

    seq_at = lax.axis_index("seq")
    core = seq_at % 2
    chip = seq_at // 2

    def other_core(value):
        return lax.ppermute(value, "seq", [(s, s ^ 1) for s in range(seq_count)])

    def chip_shift(value, k):
        return lax.ppermute(value, "seq", [(s, (s + 2 * k) % seq_count) for s in range(seq_count)])

    def exp_swap(value, s):
        return lax.ppermute(value, "exp", [(e, e ^ s) for e in range(exp_count)]) if s else value

    def joined(values, axis=0):
        return values[0] if len(values) == 1 else jnp.concatenate(values, axis=axis)

    def blocks_from(k):
        from_chip = (chip - k) % chips
        return from_chip * 2 + core, from_chip * 2 + 1 - core

    ids_t = expert_ids.T
    weights_t = route_weights.T
    columns = top_count // seq_count
    own_ids_t = lax.dynamic_slice_in_dim(ids_t, seq_at * columns, columns, 0)

    def from_chips(rows):
        return [chip_shift(rows, k) for k in range(1, chips)]

    came = [None] * exp_count

    def send(pieces, group):
        for s, piece in zip(group, pieces):
            came[s] = exp_swap(piece, s)

    def send_more(group, after):
        send(pack_again(place, tokens, out_grad, expert_count, group, after), group)

    def arrived_of(group):
        return joined([came[s] for s in group])

    near = of_units(0, 1, 2, 4)
    place, pieces = pack(ids_t, tokens, out_grad, expert_count, most, near)
    send(pieces, near)
    pairs = [of_units(0), of_units(1), of_units(2, 4), of_units(3, 5), of_units(6)]
    rows = [from_chips(arrived_of(pairs[0]))]
    send_more(pairs[3], [came[pairs[1][-1]]] + rows[0][:1])
    rows.append(from_chips(arrived_of(pairs[1])))
    rows.append(from_chips(arrived_of(pairs[2])))
    send_more(pairs[4], [came[pairs[2][-1]]] + rows[1][:1])
    send_more(of_units(7), [came[pairs[3][-1]]] + rows[2][:1])
    rows.append(from_chips(copied([arrived_of(pairs[3])], rows[1][:1])[0]))
    rows.append(from_chips(copied([arrived_of(pairs[4])], rows[2][:1])[0]))
    end = arrived_of(of_units(7))
    end_x, end_dy = copied([end[:, :part], end[:, part:]], rows[3][:1] + rows[4][:1])
    end_x, end_dy = from_chips(end_x), from_chips(end_dy)

    def in_order(k):
        found = {}
        for values, group in zip([values[k] for values in rows], pairs):
            for j, s in enumerate(group):
                found[s] = values[j * most : (j + 1) * most]
        early = [found[s] for s in sorted(found)]
        return (
            joined([value[:, :part] for value in early] + [end_x[k]]),
            joined([value[:, part:] for value in early] + [end_dy[k]]),
        )

    both = [(joined([v[:, :part] for v in came]), joined([v[:, part:] for v in came]))]
    both += [in_order(k) for k in range(chips - 1)]
    def over_width(pairs, chip_shifts, weight, axis):
        total = None
        for pair, k in zip(pairs, chip_shifts):
            for value, at in zip(pair, blocks_from(k)):
                block = lax.dynamic_slice_in_dim(weight, at * part, part, axis)
                term = lax.dot_general(
                    value, block, (((1,), (axis,)), ((), ())), preferred_element_type=F32
                )
                total = term if total is None else total + term
        return total

    def three(pairs, chip_shifts):
        xs = [x for x, _ in pairs]
        dys = [dy for _, dy in pairs]
        return (
            over_width(xs, chip_shifts, wg, 0),
            over_width(xs, chip_shifts, wu, 0),
            over_width(dys, chip_shifts, wd, 1),
        )

    def with_other(pair):
        return [(value, other_core(value)) for value in pair]

    early = three([with_other(both[0])], [0])
    later = []
    for x, dy in both[1:]:
        x, dy = copied([x, dy], early)
        later.append(with_other((x, dy)))
    late = three(later, range(1, chips))
    pre_gate, pre_up, back_grad = [first + second for first, second in zip(early, late)]

    sig = jax.nn.sigmoid(pre_gate)
    active = pre_gate * sig
    grad_gate = (back_grad * pre_up * sig * (1.0 + pre_gate * (1.0 - sig))).astype(BF16)
    grad_up = (back_grad * active).astype(BF16)
    route = jnp.sum(active * pre_up * back_grad, axis=-1)

    grads = (grad_gate, grad_up)

    def chip_part(grads, k):
        sent = other_core(product(grads, wg, wu, part, k, True, BF16))
        return product(grads, wg, wu, part, k, False, F32), sent

    half = exp_count // 2
    others = [chip_part(grads, k) for k in range(1, chips)]
    summed = [added(keep, sent, half * most, half * most, []) for keep, sent in others]
    keep, sent = chip_part(copied(grads, summed), 0)

    if summed:
        route = copied([route.reshape(1, -1)], summed)[0].reshape(-1)
    route = route + other_core(route)
    route = route + sum(chip_shift(route, k) for k in range(1, chips))
    high = route.astype(BF16)
    low = (route - high.astype(F32)).astype(BF16)
    lane = lax.broadcasted_iota(jnp.int32, (route.shape[0], EXTRA), 1)
    extra = jnp.where(lane == 0, high[:, None], jnp.where(lane == 1, low[:, None], 0))

    back = [None] * exp_count
    for first in (half, 0):
        if not first:
            summed = [added(*values, 0, half * most, pieces[:1]) for values in others]
        arrived = [chip_shift(values, k) for k, values in enumerate(summed, 1)]
        pieces = totals(keep, sent, extra, arrived, first, half, most)
        for j, piece in enumerate(pieces):
            back[first + j] = exp_swap(piece, first + j)

    own_grad, own_route_t = combine(
        ids_t, own_ids_t, weights_t, place, back, expert_count, part
    )
    return own_grad, own_route_t.T


def solution(mesh):
    in_specs = (
        P("exp", "seq"),
        P("exp", "seq"),
        P("exp", None),
        P("exp", None),
        P("exp", None, "seq"),
        P("exp", None, "seq"),
        P("exp", "seq", None),
    )
    out_specs = (P("exp", "seq"), P("exp", "seq"))
    return jax.shard_map(local, mesh=mesh, in_specs=in_specs, out_specs=out_specs, check_vma=False)
```

```python
import functools

import jax
import jax.numpy as jnp
from jax import lax
from jax.experimental import pallas as pl
from jax.experimental.pallas import tpu as pltpu
from jax.sharding import PartitionSpec as P

CONTRACT = (((1,), (1,)), ((), ()))
BF16 = jnp.bfloat16
F32 = jnp.float32
VMEM_BYTES = 8 * 1024 * 1024
PACK_VMEM_BYTES = 56 * 1024 * 1024
EXTRA = 128


def params(limit=VMEM_BYTES):
    return pltpu.CompilerParams(vmem_limit_bytes=limit)


def write_pieces(place, values, refs):
    most = refs[0].shape[0]
    at = 0
    for value in values:
        rows = jnp.dot(place, value, preferred_element_type=F32)
        width = rows.shape[1]
        for s, ref in enumerate(refs):
            ref[:, at : at + width] = rows[s * most : (s + 1) * most].astype(BF16)
        at += width


def pack_kernel(ids_ref, x_ref, dy_ref, place_ref, *pieces, experts, most):
    ids = ids_ref[...]
    tokens = ids.shape[1]
    named = jnp.min(ids, axis=0, keepdims=True)
    hot = (named == lax.broadcasted_iota(jnp.int32, (experts, tokens), 0)).astype(F32)
    rows = lax.broadcasted_iota(jnp.int32, (tokens, tokens), 0)
    cols = lax.broadcasted_iota(jnp.int32, (tokens, tokens), 1)
    before = (rows < cols).astype(F32).astype(BF16)
    earlier = jnp.dot(hot.astype(BF16), before, preferred_element_type=F32)
    rank = jnp.sum(earlier * hot, axis=0, keepdims=True).astype(jnp.int32)
    target = jnp.where(named < experts, (named ^ lax.axis_index("exp")) * most + rank, -1)
    slots = lax.broadcasted_iota(jnp.int32, (experts * most, tokens), 0)
    place = (target == slots).astype(F32).astype(BF16)
    place_ref[...] = place
    write_pieces(place, (x_ref[...], dy_ref[...]), pieces)


def pack(ids_t, x, dy, experts, most):
    tokens, width = x.shape
    place, *pieces = pl.pallas_call(
        functools.partial(pack_kernel, experts=experts, most=most),
        out_shape=[jax.ShapeDtypeStruct((experts * most, tokens), BF16)]
        + [jax.ShapeDtypeStruct((most, 2 * width), BF16)] * experts,
        compiler_params=params(PACK_VMEM_BYTES),
        name="pack",
    )(ids_t, x, dy)
    return place, pieces


def copy_kernel(*refs, count, gates):
    for taken, given in zip(refs[:count], refs[count + gates :]):
        given[...] = taken[...]


def copied(values, after):
    whole = pl.BlockSpec(memory_space=pltpu.VMEM)
    return pl.pallas_call(
        functools.partial(copy_kernel, count=len(values), gates=len(after)),
        in_specs=[whole] * len(values) + [pl.BlockSpec(memory_space=pl.ANY)] * len(after),
        out_shape=[jax.ShapeDtypeStruct(value.shape, value.dtype) for value in values],
        compiler_params=params(),
        name="copied",
    )(*values, *after)


def added_kernel(keep_ref, sent_ref, *refs, first):
    rows = refs[-1].shape[0]
    cut = slice(first, first + rows)
    refs[-1][...] = (keep_ref[cut] + sent_ref[cut].astype(F32)).astype(BF16)


def added(keep, sent, first, rows, after):
    whole = pl.BlockSpec(memory_space=pltpu.VMEM)
    return pl.pallas_call(
        functools.partial(added_kernel, first=first),
        in_specs=[whole] * 2 + [pl.BlockSpec(memory_space=pl.ANY)] * len(after),
        out_shape=jax.ShapeDtypeStruct((rows, keep.shape[1]), BF16),
        compiler_params=params(),
        name="added",
    )(keep, sent, *after)


def total_kernel(keep_ref, sent_ref, extra_ref, *refs, count, first):
    pieces = refs[count:]
    most = pieces[0].shape[0]
    cut = slice(first * most, (first + len(pieces)) * most)
    total = keep_ref[cut] + sent_ref[cut].astype(F32)
    for ref in refs[:count]:
        total += ref[...].astype(F32)
    total = total.astype(BF16)
    extra = extra_ref[cut]
    width = total.shape[1]
    for j, ref in enumerate(pieces):
        ref[:, :width] = total[j * most : (j + 1) * most]
        ref[:, width:] = extra[j * most : (j + 1) * most]


def totals(keep, sent, extra, arrived, first, count, most):
    return pl.pallas_call(
        functools.partial(total_kernel, count=len(arrived), first=first),
        out_shape=[jax.ShapeDtypeStruct((most, keep.shape[1] + EXTRA), BF16)] * count,
        compiler_params=params(),
        name="totals",
    )(keep, sent, extra, *arrived)


def combine_kernel(ids_ref, own_ids_ref, weights_ref, place_ref, *refs, experts, count):
    came = jnp.concatenate([ref[...] for ref in refs[:count]], axis=0)
    grad_ref, route_ref = refs[count:]
    tokens, width = grad_ref.shape
    weight = jnp.sum(jnp.where(ids_ref[...] < experts, weights_ref[...], 0.0), axis=0, keepdims=True)
    column = jnp.broadcast_to(weight, (tokens, tokens)).T[:, :1]
    pick = place_ref[...].astype(F32).T.astype(BF16)
    taken = jnp.dot(pick, came, preferred_element_type=F32)
    grad_ref[...] = (column * taken[:, :width]).astype(BF16)
    extra = taken[:, width:].T
    total = extra[0:1] + extra[1:2]
    route_ref[...] = jnp.where(own_ids_ref[...] < experts, total, 0.0)


def combine(ids_t, own_ids_t, weights_t, place, came, experts, width):
    tokens = ids_t.shape[1]
    return pl.pallas_call(
        functools.partial(combine_kernel, experts=experts, count=len(came)),
        out_shape=(
            jax.ShapeDtypeStruct((tokens, width), BF16),
            jax.ShapeDtypeStruct(own_ids_t.shape, F32),
        ),
        compiler_params=params(),
        name="combine",
    )(ids_t, own_ids_t, weights_t, place, *came)


def local(tokens, out_grad, expert_ids, route_weights, gate_proj, up_proj, down_proj):
    seq_count = lax.axis_size("seq")
    exp_count = lax.axis_size("exp")
    tok_dev, part = tokens.shape
    top_count = expert_ids.shape[1]
    expert_count = exp_count * gate_proj.shape[0]
    most = max(2, 2 * ((tok_dev + expert_count - 1) // expert_count))
    wg, wu, wd = gate_proj[0], up_proj[0], down_proj[0]
    chips = seq_count // 2
    unit = exp_count // 8

    def of_units(*units):
        return [u * unit + j for u in units for j in range(unit)]

    seq_at = lax.axis_index("seq")
    core = seq_at % 2
    chip = seq_at // 2

    def other_core(value):
        return lax.ppermute(value, "seq", [(s, s ^ 1) for s in range(seq_count)])

    def chip_shift(value, k):
        return lax.ppermute(value, "seq", [(s, (s + 2 * k) % seq_count) for s in range(seq_count)])

    def exp_swap(value, s):
        return lax.ppermute(value, "exp", [(e, e ^ s) for e in range(exp_count)]) if s else value

    def joined(values, axis=0):
        return values[0] if len(values) == 1 else jnp.concatenate(values, axis=axis)

    def blocks_from(k):
        from_chip = (chip - k) % chips
        return from_chip * 2 + core, from_chip * 2 + 1 - core

    def over_width(shares, weight, axis):
        total = None
        for k, pair in enumerate(shares):
            for rows, at in zip(pair, blocks_from(k)):
                block = lax.dynamic_slice_in_dim(weight, at * part, part, axis)
                term = lax.dot_general(
                    rows, block, (((1,), (axis,)), ((), ())), preferred_element_type=F32
                )
                total = term if total is None else total + term
        return total

    ids_t = expert_ids.T
    weights_t = route_weights.T
    columns = top_count // seq_count
    own_ids_t = lax.dynamic_slice_in_dim(ids_t, seq_at * columns, columns, 0)

    def from_chips(rows):
        return [chip_shift(rows, k) for k in range(1, chips)]

    came = [None] * exp_count

    def send(pieces, group):
        for s, piece in zip(group, pieces):
            came[s] = exp_swap(piece, s)

    def send_more(group, after):
        send(copied([pieces[s] for s in group], after), group)

    def arrived_of(group):
        return joined([came[s] for s in group])

    near = of_units(0, 1, 2, 4)
    place, pieces = pack(ids_t, tokens, out_grad, expert_count, most)
    send([pieces[s] for s in near], near)
    pairs = [of_units(0, 1), of_units(2, 4), of_units(3, 5), of_units(6)]
    rows = [from_chips(arrived_of(group)) for group in pairs[:2]]
    send_more(pairs[2], [came[pairs[0][-1]], came[pairs[1][0]]])
    send_more(pairs[3], [came[pairs[1][-1]]] + rows[0][:1])
    send_more(of_units(7), [came[pairs[2][-1]]] + rows[1][:1])
    rows.append(from_chips(copied([arrived_of(pairs[2])], rows[0][:1])[0]))
    rows.append(from_chips(copied([arrived_of(pairs[3])], rows[1][:1])[0]))
    end = arrived_of(of_units(7))
    end_x, end_dy = copied([end[:, :part], end[:, part:]], rows[2][:1] + rows[3][:1])
    end_x, end_dy = from_chips(end_x), from_chips(end_dy)

    def with_other(early, last):
        return joined([early, last]), joined([other_core(early), other_core(last)])

    own = [joined([v[:, :part] for v in came]), joined([v[:, part:] for v in came])]
    shares_x, shares_dy = [(own[0], other_core(own[0]))], [(own[1], other_core(own[1]))]
    for k in range(chips - 1):
        found = {}
        for values, group in zip([values[k] for values in rows], pairs):
            for j, s in enumerate(group):
                found[s] = values[j * most : (j + 1) * most]
        early = [found[s] for s in sorted(found)]
        shares_x.append(with_other(joined([value[:, :part] for value in early]), end_x[k]))
        shares_dy.append(with_other(joined([value[:, part:] for value in early]), end_dy[k]))

    pre_gate = over_width(shares_x, wg, 0)
    pre_up = over_width(shares_x, wu, 0)
    back_grad = over_width(shares_dy, wd, 1)

    sig = jax.nn.sigmoid(pre_gate)
    active = pre_gate * sig
    grad_gate = (back_grad * pre_up * sig * (1.0 + pre_gate * (1.0 - sig))).astype(BF16)
    grad_up = (back_grad * active).astype(BF16)
    route = jnp.sum(active * pre_up * back_grad, axis=-1)

    whole_grad = lax.dot_general(
        grad_gate, wg, CONTRACT, preferred_element_type=F32
    ) + lax.dot_general(grad_up, wu, CONTRACT, preferred_element_type=F32)

    def chip_part(k):
        there = (chip + k) % chips * 2

        def block(at):
            return lax.dynamic_slice_in_dim(whole_grad, at * part, part, 1)

        return block(there + core), other_core(block(there + 1 - core).astype(BF16))

    others = [chip_part(k) for k in range(1, chips)]
    keep, sent = chip_part(0)
    half = exp_count // 2
    order = [(exp_count - unit, unit), (half, half - unit), (0, half)]
    first, count = order[0]
    summed = [added(*values, first * most, count * most, []) for values in others]

    if summed:
        route = copied([route.reshape(1, -1)], summed)[0].reshape(-1)
    route = route + other_core(route)
    route = route + sum(chip_shift(route, k) for k in range(1, chips))
    high = route.astype(BF16)
    low = (route - high.astype(F32)).astype(BF16)
    lane = lax.broadcasted_iota(jnp.int32, (route.shape[0], EXTRA), 1)
    extra = jnp.where(lane == 0, high[:, None], jnp.where(lane == 1, low[:, None], 0))

    back = [None] * exp_count
    after = []
    for first, count in order:
        if after:
            if not first:
                after = after + [back[-1]]
            summed = [added(*values, first * most, count * most, after) for values in others]
        arrived = [chip_shift(values, k) for k, values in enumerate(summed, 1)]
        pieces = totals(keep, sent, extra, arrived, first, count, most)
        for j, piece in enumerate(pieces):
            back[first + j] = exp_swap(piece, first + j)
        after = list(pieces[:1])

    own_grad, own_route_t = combine(
        ids_t, own_ids_t, weights_t, place, back, expert_count, part
    )
    return own_grad, own_route_t.T


def solution(mesh):
    in_specs = (
        P("exp", "seq"),
        P("exp", "seq"),
        P("exp", None),
        P("exp", None),
        P("exp", None, "seq"),
        P("exp", None, "seq"),
        P("exp", "seq", None),
    )
    out_specs = (P("exp", "seq"), P("exp", "seq"))
    return jax.shard_map(local, mesh=mesh, in_specs=in_specs, out_specs=out_specs, check_vma=False)
```

```python
import functools

import jax
import jax.numpy as jnp
from jax import lax
from jax.experimental import pallas as pl
from jax.experimental.pallas import tpu as pltpu
from jax.sharding import PartitionSpec as P

CONTRACT = (((1,), (1,)), ((), ()))
BF16 = jnp.bfloat16
F32 = jnp.float32
VMEM_BYTES = 8 * 1024 * 1024
EXTRA = 128


def params():
    return pltpu.CompilerParams(vmem_limit_bytes=VMEM_BYTES)


def write_pieces(place, values, refs):
    most = refs[0].shape[0]
    at = 0
    for value in values:
        rows = jnp.dot(place, value, preferred_element_type=F32)
        width = rows.shape[1]
        for s, ref in enumerate(refs):
            ref[:, at : at + width] = rows[s * most : (s + 1) * most].astype(BF16)
        at += width


def pack_kernel(ids_ref, x_ref, dy_ref, place_ref, *pieces, experts, most):
    ids = ids_ref[...]
    tokens = ids.shape[1]
    named = jnp.min(ids, axis=0, keepdims=True)
    hot = (named == lax.broadcasted_iota(jnp.int32, (experts, tokens), 0)).astype(F32)
    rows = lax.broadcasted_iota(jnp.int32, (tokens, tokens), 0)
    cols = lax.broadcasted_iota(jnp.int32, (tokens, tokens), 1)
    before = (rows < cols).astype(F32).astype(BF16)
    earlier = jnp.dot(hot.astype(BF16), before, preferred_element_type=F32)
    rank = jnp.sum(earlier * hot, axis=0, keepdims=True).astype(jnp.int32)
    target = jnp.where(named < experts, (named ^ lax.axis_index("exp")) * most + rank, -1)
    slots = lax.broadcasted_iota(jnp.int32, (experts * most, tokens), 0)
    place = (target == slots).astype(F32).astype(BF16)
    place_ref[...] = place
    write_pieces(place, (x_ref[...], dy_ref[...]), pieces)


def pack(ids_t, x, dy, experts, most):
    tokens, width = x.shape
    place, *pieces = pl.pallas_call(
        functools.partial(pack_kernel, experts=experts, most=most),
        out_shape=[jax.ShapeDtypeStruct((experts * most, tokens), BF16)]
        + [jax.ShapeDtypeStruct((most, 2 * width), BF16)] * experts,
        compiler_params=params(),
        name="pack",
    )(ids_t, x, dy)
    return place, pieces


def copy_kernel(*refs, count, gates):
    for taken, given in zip(refs[:count], refs[count + gates :]):
        given[...] = taken[...]


def copied(values, after):
    whole = pl.BlockSpec(memory_space=pltpu.VMEM)
    return pl.pallas_call(
        functools.partial(copy_kernel, count=len(values), gates=len(after)),
        in_specs=[whole] * len(values) + [pl.BlockSpec(memory_space=pl.ANY)] * len(after),
        out_shape=[jax.ShapeDtypeStruct(value.shape, value.dtype) for value in values],
        compiler_params=params(),
        name="copied",
    )(*values, *after)


def blocks_kernel(*refs, weights):
    taken, given, done = refs[:weights], refs[weights:-1], refs[-1]
    count = len(given) // weights
    part = given[0].shape[0]
    chips = count // 2
    seq_at = lax.axis_index("seq")
    core = lax.rem(seq_at, 2)
    chip = lax.div(seq_at, 2)

    def copy(which, j):
        at = lax.rem(chip + chips - j // 2, chips) * 2 + (core if j % 2 == 0 else 1 - core)
        rows = pl.ds(pl.multiple_of(at * part, part), part)
        return pltpu.make_async_copy(
            taken[which].at[rows], given[which * count + j], done.at[which, j]
        )

    copies = [copy(which, j) for j in range(count) for which in range(weights)]
    for one in copies:
        one.start()
    for one in copies:
        one.wait()


def blocks(weights, count):
    rows, width = weights[0].shape
    block = jax.ShapeDtypeStruct((rows // count, width), BF16)
    given = pl.pallas_call(
        functools.partial(blocks_kernel, weights=len(weights)),
        in_specs=[pl.BlockSpec(memory_space=pl.ANY)] * len(weights),
        out_specs=[pl.BlockSpec(memory_space=pl.ANY)] * (count * len(weights)),
        out_shape=[block] * (count * len(weights)),
        scratch_shapes=[pltpu.SemaphoreType.DMA((len(weights), count))],
        compiler_params=params(),
        name="blocks",
    )(*weights)
    return [given[j * count : (j + 1) * count] for j in range(len(weights))]


def added_kernel(keep_ref, sent_ref, *refs, first):
    rows = refs[-1].shape[0]
    cut = slice(first, first + rows)
    refs[-1][...] = (keep_ref[cut] + sent_ref[cut].astype(F32)).astype(BF16)


def added(keep, sent, first, rows, after):
    whole = pl.BlockSpec(memory_space=pltpu.VMEM)
    return pl.pallas_call(
        functools.partial(added_kernel, first=first),
        in_specs=[whole] * 2 + [pl.BlockSpec(memory_space=pl.ANY)] * len(after),
        out_shape=jax.ShapeDtypeStruct((rows, keep.shape[1]), BF16),
        compiler_params=params(),
        name="added",
    )(keep, sent, *after)


def total_kernel(keep_ref, sent_ref, extra_ref, *refs, count, first):
    pieces = refs[count:]
    most = pieces[0].shape[0]
    cut = slice(first * most, (first + len(pieces)) * most)
    total = keep_ref[cut] + sent_ref[cut].astype(F32)
    for ref in refs[:count]:
        total += ref[...].astype(F32)
    total = total.astype(BF16)
    extra = extra_ref[cut]
    width = total.shape[1]
    for j, ref in enumerate(pieces):
        ref[:, :width] = total[j * most : (j + 1) * most]
        ref[:, width:] = extra[j * most : (j + 1) * most]


def totals(keep, sent, extra, arrived, first, count, most):
    return pl.pallas_call(
        functools.partial(total_kernel, count=len(arrived), first=first),
        out_shape=[jax.ShapeDtypeStruct((most, keep.shape[1] + EXTRA), BF16)] * count,
        compiler_params=params(),
        name="totals",
    )(keep, sent, extra, *arrived)


def combine_kernel(ids_ref, own_ids_ref, weights_ref, place_ref, *refs, experts, count):
    came = jnp.concatenate([ref[...] for ref in refs[:count]], axis=0)
    grad_ref, route_ref = refs[count:]
    tokens, width = grad_ref.shape
    weight = jnp.sum(jnp.where(ids_ref[...] < experts, weights_ref[...], 0.0), axis=0, keepdims=True)
    column = jnp.broadcast_to(weight, (tokens, tokens)).T[:, :1]
    pick = place_ref[...].astype(F32).T.astype(BF16)
    taken = jnp.dot(pick, came, preferred_element_type=F32)
    grad_ref[...] = (column * taken[:, :width]).astype(BF16)
    extra = taken[:, width:].T
    total = extra[0:1] + extra[1:2]
    route_ref[...] = jnp.where(own_ids_ref[...] < experts, total, 0.0)


def combine(ids_t, own_ids_t, weights_t, place, came, experts, width):
    tokens = ids_t.shape[1]
    return pl.pallas_call(
        functools.partial(combine_kernel, experts=experts, count=len(came)),
        out_shape=(
            jax.ShapeDtypeStruct((tokens, width), BF16),
            jax.ShapeDtypeStruct(own_ids_t.shape, F32),
        ),
        compiler_params=params(),
        name="combine",
    )(ids_t, own_ids_t, weights_t, place, *came)


def local(tokens, out_grad, expert_ids, route_weights, gate_proj, up_proj, down_proj):
    seq_count = lax.axis_size("seq")
    exp_count = lax.axis_size("exp")
    tok_dev, part = tokens.shape
    top_count = expert_ids.shape[1]
    expert_count = exp_count * gate_proj.shape[0]
    most = max(2, 2 * ((tok_dev + expert_count - 1) // expert_count))
    wg, wu, wd = gate_proj[0], up_proj[0], down_proj[0]
    chips = seq_count // 2
    unit = exp_count // 8

    def of_units(*units):
        return [u * unit + j for u in units for j in range(unit)]

    seq_at = lax.axis_index("seq")
    core = seq_at % 2
    chip = seq_at // 2

    def other_core(value):
        return lax.ppermute(value, "seq", [(s, s ^ 1) for s in range(seq_count)])

    def chip_shift(value, k):
        return lax.ppermute(value, "seq", [(s, (s + 2 * k) % seq_count) for s in range(seq_count)])

    def exp_swap(value, s):
        return lax.ppermute(value, "exp", [(e, e ^ s) for e in range(exp_count)]) if s else value

    def joined(values, axis=0):
        return values[0] if len(values) == 1 else jnp.concatenate(values, axis=axis)

    ids_t = expert_ids.T
    weights_t = route_weights.T
    columns = top_count // seq_count
    own_ids_t = lax.dynamic_slice_in_dim(ids_t, seq_at * columns, columns, 0)

    def from_chips(rows):
        return [chip_shift(rows, k) for k in range(1, chips)]

    came = [None] * exp_count

    def send(pieces, group):
        for s, piece in zip(group, pieces):
            came[s] = exp_swap(piece, s)

    def send_more(group, after):
        send(copied([pieces[s] for s in group], after), group)

    def arrived_of(group):
        return joined([came[s] for s in group])

    near = of_units(0, 1, 2, 4)
    place, pieces = pack(ids_t, tokens, out_grad, expert_count, most)
    send([pieces[s] for s in near], near)
    pairs = [of_units(0), of_units(1, 2, 4), of_units(3, 5), of_units(6)]
    rows = [from_chips(arrived_of(pairs[0]))]
    send_more(pairs[2], [came[unit]] + rows[0][:1])
    rows.append(from_chips(arrived_of(pairs[1])))
    send_more(pairs[3], [came[pairs[1][-1]]] + rows[0][:1])
    gate_blocks, up_blocks = blocks([wg, wu], seq_count)
    after = [came[pairs[2][-1]]] + rows[1][:1] + [gate_blocks[0]]
    send_more(of_units(7), after)
    rows.append(from_chips(arrived_of(pairs[2])))
    rows.append(from_chips(copied([arrived_of(pairs[3])], rows[1][:1])[0]))

    def three(x, dy, j):
        k, other = j // 2, j % 2
        at = (chip - k) % chips * 2 + (1 - core if other else core)
        down = lax.dynamic_slice_in_dim(wd, at * part, part, 1)
        return [
            jnp.dot(x, gate_blocks[j], preferred_element_type=F32),
            jnp.dot(x, up_blocks[j], preferred_element_type=F32),
            lax.dot_general(dy, down, CONTRACT, preferred_element_type=F32),
        ]

    def plus(terms, more):
        return [term + other for term, other in zip(terms, more)]

    own_x, own_dy = joined([v[:, :part] for v in came]), joined([v[:, part:] for v in came])
    end = arrived_of(of_units(7))
    terms = three(own_x, own_dy, 0)
    (end_x,) = copied([end[:, :part]], rows[2][:1] + rows[3][:1] + terms)
    end_x = from_chips(end_x)
    terms = plus(terms, three(other_core(own_x), other_core(own_dy), 1))
    (end_dy,) = copied([end[:, part:]], rows[2][:1] + rows[3][:1] + terms)
    end_dy = from_chips(end_dy)
    for k in range(1, chips):
        found = {}
        for values, group in zip([values[k - 1] for values in rows], pairs):
            for j, s in enumerate(group):
                found[s] = values[j * most : (j + 1) * most]
        early = [found[s] for s in sorted(found)]
        early_x = joined([value[:, :part] for value in early])
        early_dy = joined([value[:, part:] for value in early])
        last_x, last_dy = end_x[k - 1], end_dy[k - 1]
        terms = plus(terms, three(joined([early_x, last_x]), joined([early_dy, last_dy]), 2 * k))
        other_x = joined([other_core(early_x), other_core(last_x)])
        other_dy = joined([other_core(early_dy), other_core(last_dy)])
        terms = plus(terms, three(other_x, other_dy, 2 * k + 1))
    pre_gate, pre_up, back_grad = terms

    sig = jax.nn.sigmoid(pre_gate)
    active = pre_gate * sig
    grad_gate = (back_grad * pre_up * sig * (1.0 + pre_gate * (1.0 - sig))).astype(BF16)
    grad_up = (back_grad * active).astype(BF16)
    route = jnp.sum(active * pre_up * back_grad, axis=-1)

    def block_grad(j):
        return lax.dot_general(
            grad_gate, gate_blocks[j], CONTRACT, preferred_element_type=F32
        ) + lax.dot_general(grad_up, up_blocks[j], CONTRACT, preferred_element_type=F32)

    def chip_part(k):
        j = 2 * ((chips - k) % chips)
        sent = other_core(block_grad(j + 1).astype(BF16))
        return block_grad(j), sent

    others = [chip_part(k) for k in range(1, chips)]
    keep, sent = chip_part(0)
    half = exp_count // 2
    order = [(exp_count - unit, unit), (half, half - unit), (0, half)]
    first, count = order[0]
    summed = [added(*values, first * most, count * most, []) for values in others]

    route = route + other_core(route)
    route = route + sum(chip_shift(route, k) for k in range(1, chips))
    high = route.astype(BF16)
    low = (route - high.astype(F32)).astype(BF16)
    lane = lax.broadcasted_iota(jnp.int32, (route.shape[0], EXTRA), 1)
    extra = jnp.where(lane == 0, high[:, None], jnp.where(lane == 1, low[:, None], 0))

    back = [None] * exp_count
    after = []
    for first, count in order:
        if after:
            if not first:
                after = after + [back[-1]]
            summed = [added(*values, first * most, count * most, after) for values in others]
        arrived = [chip_shift(values, k) for k, values in enumerate(summed, 1)]
        pieces = totals(keep, sent, extra, arrived, first, count, most)
        for j, piece in enumerate(pieces):
            back[first + j] = exp_swap(piece, first + j)
        after = list(pieces[:1])

    own_grad, own_route_t = combine(
        ids_t, own_ids_t, weights_t, place, back, expert_count, part
    )
    return own_grad, own_route_t.T


def solution(mesh):
    in_specs = (
        P("exp", "seq"),
        P("exp", "seq"),
        P("exp", None),
        P("exp", None),
        P("exp", None, "seq"),
        P("exp", None, "seq"),
        P("exp", "seq", None),
    )
    out_specs = (P("exp", "seq"), P("exp", "seq"))
    return jax.shard_map(local, mesh=mesh, in_specs=in_specs, out_specs=out_specs, check_vma=False)
```

```python
import functools

import jax
import jax.numpy as jnp
from jax import lax
from jax.experimental import pallas as pl
from jax.experimental.pallas import tpu as pltpu
from jax.sharding import PartitionSpec as P

CONTRACT = (((1,), (1,)), ((), ()))
BF16 = jnp.bfloat16
F32 = jnp.float32
VMEM_BYTES = 8 * 1024 * 1024
BLOCKS_VMEM_BYTES = 56 * 1024 * 1024
EXTRA = 128


def params():
    return pltpu.CompilerParams(vmem_limit_bytes=VMEM_BYTES)


def write_pieces(place, values, refs):
    most = refs[0].shape[0]
    at = 0
    for value in values:
        rows = jnp.dot(place, value, preferred_element_type=F32)
        width = rows.shape[1]
        for s, ref in enumerate(refs):
            ref[:, at : at + width] = rows[s * most : (s + 1) * most].astype(BF16)
        at += width


def pack_kernel(ids_ref, x_ref, dy_ref, place_ref, *pieces, experts, most):
    ids = ids_ref[...]
    tokens = ids.shape[1]
    named = jnp.min(ids, axis=0, keepdims=True)
    hot = (named == lax.broadcasted_iota(jnp.int32, (experts, tokens), 0)).astype(F32)
    rows = lax.broadcasted_iota(jnp.int32, (tokens, tokens), 0)
    cols = lax.broadcasted_iota(jnp.int32, (tokens, tokens), 1)
    before = (rows < cols).astype(F32).astype(BF16)
    earlier = jnp.dot(hot.astype(BF16), before, preferred_element_type=F32)
    rank = jnp.sum(earlier * hot, axis=0, keepdims=True).astype(jnp.int32)
    target = jnp.where(named < experts, (named ^ lax.axis_index("exp")) * most + rank, -1)
    slots = lax.broadcasted_iota(jnp.int32, (experts * most, tokens), 0)
    place = (target == slots).astype(F32).astype(BF16)
    place_ref[...] = place
    write_pieces(place, (x_ref[...], dy_ref[...]), pieces)


def pack(ids_t, x, dy, experts, most):
    tokens, width = x.shape
    place, *pieces = pl.pallas_call(
        functools.partial(pack_kernel, experts=experts, most=most),
        out_shape=[jax.ShapeDtypeStruct((experts * most, tokens), BF16)]
        + [jax.ShapeDtypeStruct((most, 2 * width), BF16)] * experts,
        compiler_params=params(),
        name="pack",
    )(ids_t, x, dy)
    return place, pieces


def copy_kernel(*refs, count, gates):
    for taken, given in zip(refs[:count], refs[count + gates :]):
        given[...] = taken[...]


def copied(values, after):
    whole = pl.BlockSpec(memory_space=pltpu.VMEM)
    return pl.pallas_call(
        functools.partial(copy_kernel, count=len(values), gates=len(after)),
        in_specs=[whole] * len(values) + [pl.BlockSpec(memory_space=pl.ANY)] * len(after),
        out_shape=[jax.ShapeDtypeStruct(value.shape, value.dtype) for value in values],
        compiler_params=params(),
        name="copied",
    )(*values, *after)


def blocks_kernel(*refs, weights, gates, count, axis):
    taken, given = refs[:weights], refs[weights + gates : -2]
    made_ref, done = refs[-2:]
    part = given[0].shape[axis]
    chips = count // 2
    seq_at = lax.axis_index("seq")
    core = lax.rem(seq_at, 2)
    chip = lax.div(seq_at, 2)

    def copy(which, j):
        at = lax.rem(chip + chips - j // 2, chips) * 2 + (core if j % 2 == 0 else 1 - core)
        cut = pl.ds(pl.multiple_of(at * part, part), part)
        source = taken[which].at[cut] if axis == 0 else taken[which].at[:, cut]
        return pltpu.make_async_copy(source, given[which * count + j], done.at[which, j])

    copies = [copy(which, j) for j in range(count) for which in range(weights)]
    for one in copies:
        one.start()
    for one in copies:
        one.wait()
    made_ref[...] = jnp.zeros_like(made_ref)


def blocks(weights, axis, count, after):
    shape = list(weights[0].shape)
    shape[axis] //= count
    given = pl.pallas_call(
        functools.partial(
            blocks_kernel, weights=len(weights), gates=len(after), count=count, axis=axis
        ),
        in_specs=[pl.BlockSpec(memory_space=pl.ANY)] * (len(weights) + len(after)),
        out_specs=[pl.BlockSpec(memory_space=pl.ANY)] * (count * len(weights))
        + [pl.BlockSpec(memory_space=pltpu.VMEM)],
        out_shape=[pltpu.HBM(tuple(shape), BF16)] * (count * len(weights))
        + [jax.ShapeDtypeStruct((8, 128), F32)],
        scratch_shapes=[pltpu.SemaphoreType.DMA((len(weights), count))],
        compiler_params=pltpu.CompilerParams(vmem_limit_bytes=BLOCKS_VMEM_BYTES),
        name="blocks",
    )(*weights, *after)
    return [given[j * count : (j + 1) * count] for j in range(len(weights))] + [given[-1]]


def added_kernel(keep_ref, sent_ref, *refs, first):
    rows = refs[-1].shape[0]
    cut = slice(first, first + rows)
    refs[-1][...] = (keep_ref[cut] + sent_ref[cut].astype(F32)).astype(BF16)


def added(keep, sent, first, rows, after):
    whole = pl.BlockSpec(memory_space=pltpu.VMEM)
    return pl.pallas_call(
        functools.partial(added_kernel, first=first),
        in_specs=[whole] * 2 + [pl.BlockSpec(memory_space=pl.ANY)] * len(after),
        out_shape=jax.ShapeDtypeStruct((rows, keep.shape[1]), BF16),
        compiler_params=params(),
        name="added",
    )(keep, sent, *after)


def total_kernel(keep_ref, sent_ref, extra_ref, *refs, count, first):
    pieces = refs[count:]
    most = pieces[0].shape[0]
    cut = slice(first * most, (first + len(pieces)) * most)
    total = keep_ref[cut] + sent_ref[cut].astype(F32)
    for ref in refs[:count]:
        total += ref[...].astype(F32)
    total = total.astype(BF16)
    extra = extra_ref[cut]
    width = total.shape[1]
    for j, ref in enumerate(pieces):
        ref[:, :width] = total[j * most : (j + 1) * most]
        ref[:, width:] = extra[j * most : (j + 1) * most]


def totals(keep, sent, extra, arrived, first, count, most):
    return pl.pallas_call(
        functools.partial(total_kernel, count=len(arrived), first=first),
        out_shape=[jax.ShapeDtypeStruct((most, keep.shape[1] + EXTRA), BF16)] * count,
        compiler_params=params(),
        name="totals",
    )(keep, sent, extra, *arrived)


def combine_kernel(ids_ref, own_ids_ref, weights_ref, place_ref, *refs, experts, count):
    came = jnp.concatenate([ref[...] for ref in refs[:count]], axis=0)
    grad_ref, route_ref = refs[count:]
    tokens, width = grad_ref.shape
    weight = jnp.sum(jnp.where(ids_ref[...] < experts, weights_ref[...], 0.0), axis=0, keepdims=True)
    column = jnp.broadcast_to(weight, (tokens, tokens)).T[:, :1]
    pick = place_ref[...].astype(F32).T.astype(BF16)
    taken = jnp.dot(pick, came, preferred_element_type=F32)
    grad_ref[...] = (column * taken[:, :width]).astype(BF16)
    extra = taken[:, width:].T
    total = extra[0:1] + extra[1:2]
    route_ref[...] = jnp.where(own_ids_ref[...] < experts, total, 0.0)


def combine(ids_t, own_ids_t, weights_t, place, came, experts, width):
    tokens = ids_t.shape[1]
    return pl.pallas_call(
        functools.partial(combine_kernel, experts=experts, count=len(came)),
        out_shape=(
            jax.ShapeDtypeStruct((tokens, width), BF16),
            jax.ShapeDtypeStruct(own_ids_t.shape, F32),
        ),
        compiler_params=params(),
        name="combine",
    )(ids_t, own_ids_t, weights_t, place, *came)


def local(tokens, out_grad, expert_ids, route_weights, gate_proj, up_proj, down_proj):
    seq_count = lax.axis_size("seq")
    exp_count = lax.axis_size("exp")
    tok_dev, part = tokens.shape
    top_count = expert_ids.shape[1]
    expert_count = exp_count * gate_proj.shape[0]
    most = max(2, 2 * ((tok_dev + expert_count - 1) // expert_count))
    wg, wu, wd = gate_proj[0], up_proj[0], down_proj[0]
    chips = seq_count // 2
    unit = exp_count // 8

    def of_units(*units):
        return [u * unit + j for u in units for j in range(unit)]

    seq_at = lax.axis_index("seq")
    core = seq_at % 2
    chip = seq_at // 2

    def other_core(value):
        return lax.ppermute(value, "seq", [(s, s ^ 1) for s in range(seq_count)])

    def chip_shift(value, k):
        return lax.ppermute(value, "seq", [(s, (s + 2 * k) % seq_count) for s in range(seq_count)])

    def exp_swap(value, s):
        return lax.ppermute(value, "exp", [(e, e ^ s) for e in range(exp_count)]) if s else value

    def joined(values, axis=0):
        return values[0] if len(values) == 1 else jnp.concatenate(values, axis=axis)

    ids_t = expert_ids.T
    weights_t = route_weights.T
    columns = top_count // seq_count
    own_ids_t = lax.dynamic_slice_in_dim(ids_t, seq_at * columns, columns, 0)

    def from_chips(rows):
        return [chip_shift(rows, k) for k in range(1, chips)]

    came = [None] * exp_count

    def send(pieces, group):
        for s, piece in zip(group, pieces):
            came[s] = exp_swap(piece, s)

    def send_more(group, after):
        send(copied([pieces[s] for s in group], after), group)

    def arrived_of(group):
        return joined([came[s] for s in group])

    near = of_units(0, 1, 2, 4)
    place, pieces = pack(ids_t, tokens, out_grad, expert_count, most)
    send([pieces[s] for s in near], near)
    pairs = [of_units(0), of_units(1, 2, 4), of_units(3, 5), of_units(6)]
    rows = [from_chips(arrived_of(pairs[0]))]
    send_more(pairs[2], [came[unit]] + rows[0][:1])
    rows.append(from_chips(arrived_of(pairs[1])))
    send_more(pairs[3], [came[pairs[1][-1]]] + rows[0][:1])
    gate_blocks, up_blocks, made = blocks([wg, wu], 0, seq_count, [came[pairs[1][-1]]])
    down_blocks, made = blocks([wd], 1, seq_count, [came[pairs[2][-1]], made])
    after = [came[pairs[2][-1]]] + rows[1][:1] + [made]
    send_more(of_units(7), after)
    rows.append(from_chips(arrived_of(pairs[2])))
    rows.append(from_chips(copied([arrived_of(pairs[3])], rows[1][:1])[0]))

    def three(x, dy, j):
        return [
            jnp.dot(x, gate_blocks[j], preferred_element_type=F32),
            jnp.dot(x, up_blocks[j], preferred_element_type=F32),
            lax.dot_general(dy, down_blocks[j], CONTRACT, preferred_element_type=F32),
        ]

    def plus(terms, more):
        return [term + other for term, other in zip(terms, more)]

    own_x, own_dy = joined([v[:, :part] for v in came]), joined([v[:, part:] for v in came])
    end = arrived_of(of_units(7))
    terms = three(own_x, own_dy, 0)
    end_x, end_dy = copied(
        [end[:, :part], end[:, part:]], rows[2][:1] + rows[3][:1] + terms
    )
    end_x, end_dy = from_chips(end_x), from_chips(end_dy)
    terms = plus(terms, three(other_core(own_x), other_core(own_dy), 1))
    for k in range(1, chips):
        found = {}
        for values, group in zip([values[k - 1] for values in rows], pairs):
            for j, s in enumerate(group):
                found[s] = values[j * most : (j + 1) * most]
        early = [found[s] for s in sorted(found)]
        early_x = joined([value[:, :part] for value in early])
        early_dy = joined([value[:, part:] for value in early])
        last_x, last_dy = end_x[k - 1], end_dy[k - 1]
        terms = plus(terms, three(joined([early_x, last_x]), joined([early_dy, last_dy]), 2 * k))
        other_x = joined([other_core(early_x), other_core(last_x)])
        other_dy = joined([other_core(early_dy), other_core(last_dy)])
        terms = plus(terms, three(other_x, other_dy, 2 * k + 1))
    pre_gate, pre_up, back_grad = terms

    sig = jax.nn.sigmoid(pre_gate)
    active = pre_gate * sig
    grad_gate = (back_grad * pre_up * sig * (1.0 + pre_gate * (1.0 - sig))).astype(BF16)
    grad_up = (back_grad * active).astype(BF16)
    route = jnp.sum(active * pre_up * back_grad, axis=-1)

    def block_grad(j):
        return lax.dot_general(
            grad_gate, gate_blocks[j], CONTRACT, preferred_element_type=F32
        ) + lax.dot_general(grad_up, up_blocks[j], CONTRACT, preferred_element_type=F32)

    def chip_part(k):
        j = 2 * ((chips - k) % chips)
        sent = other_core(block_grad(j + 1).astype(BF16))
        return block_grad(j), sent

    others = [chip_part(k) for k in range(1, chips)]
    keep, sent = chip_part(0)
    half = exp_count // 2
    order = [(exp_count - unit, unit), (half, half - unit), (0, half)]
    first, count = order[0]
    summed = [added(*values, first * most, count * most, []) for values in others]

    route = route + other_core(route)
    if summed:
        route = copied([route.reshape(1, -1)], summed)[0].reshape(-1)
    route = route + sum(chip_shift(route, k) for k in range(1, chips))
    high = route.astype(BF16)
    low = (route - high.astype(F32)).astype(BF16)
    lane = lax.broadcasted_iota(jnp.int32, (route.shape[0], EXTRA), 1)
    extra = jnp.where(lane == 0, high[:, None], jnp.where(lane == 1, low[:, None], 0))

    back = [None] * exp_count
    after = []
    for first, count in order:
        if after:
            if not first:
                after = after + [back[-1]]
            summed = [added(*values, first * most, count * most, after) for values in others]
        arrived = [chip_shift(values, k) for k, values in enumerate(summed, 1)]
        pieces = totals(keep, sent, extra, arrived, first, count, most)
        for j, piece in enumerate(pieces):
            back[first + j] = exp_swap(piece, first + j)
        after = list(pieces[:1])

    own_grad, own_route_t = combine(
        ids_t, own_ids_t, weights_t, place, back, expert_count, part
    )
    return own_grad, own_route_t.T


def solution(mesh):
    in_specs = (
        P("exp", "seq"),
        P("exp", "seq"),
        P("exp", None),
        P("exp", None),
        P("exp", None, "seq"),
        P("exp", None, "seq"),
        P("exp", "seq", None),
    )
    out_specs = (P("exp", "seq"), P("exp", "seq"))
    return jax.shard_map(local, mesh=mesh, in_specs=in_specs, out_specs=out_specs, check_vma=False)
```

```python
import functools

import jax
import jax.numpy as jnp
from jax import lax
from jax.experimental import pallas as pl
from jax.experimental.pallas import tpu as pltpu
from jax.sharding import PartitionSpec as P

CONTRACT = (((1,), (1,)), ((), ()))
BF16 = jnp.bfloat16
F32 = jnp.float32
VMEM_BYTES = 8 * 1024 * 1024
EXTRA = 128


def params():
    return pltpu.CompilerParams(vmem_limit_bytes=VMEM_BYTES)


def write_pieces(place, values, refs):
    most = refs[0].shape[0]
    at = 0
    for value in values:
        rows = jnp.dot(place, value, preferred_element_type=F32)
        width = rows.shape[1]
        for s, ref in enumerate(refs):
            ref[:, at : at + width] = rows[s * most : (s + 1) * most].astype(BF16)
        at += width


def pack_kernel(ids_ref, x_ref, dy_ref, place_ref, *pieces, experts, most):
    ids = ids_ref[...]
    tokens = ids.shape[1]
    named = jnp.min(ids, axis=0, keepdims=True)
    hot = (named == lax.broadcasted_iota(jnp.int32, (experts, tokens), 0)).astype(F32)
    rows = lax.broadcasted_iota(jnp.int32, (tokens, tokens), 0)
    cols = lax.broadcasted_iota(jnp.int32, (tokens, tokens), 1)
    before = (rows < cols).astype(F32).astype(BF16)
    earlier = jnp.dot(hot.astype(BF16), before, preferred_element_type=F32)
    rank = jnp.sum(earlier * hot, axis=0, keepdims=True).astype(jnp.int32)
    target = jnp.where(named < experts, (named ^ lax.axis_index("exp")) * most + rank, -1)
    slots = lax.broadcasted_iota(jnp.int32, (experts * most, tokens), 0)
    place = (target == slots).astype(F32).astype(BF16)
    place_ref[...] = place
    write_pieces(place, (x_ref[...], dy_ref[...]), pieces)


def pack(ids_t, x, dy, experts, most):
    tokens, width = x.shape
    place, *pieces = pl.pallas_call(
        functools.partial(pack_kernel, experts=experts, most=most),
        out_shape=[jax.ShapeDtypeStruct((experts * most, tokens), BF16)]
        + [jax.ShapeDtypeStruct((most, 2 * width), BF16)] * experts,
        compiler_params=params(),
        name="pack",
    )(ids_t, x, dy)
    return place, pieces


def copy_kernel(*refs, count, gates):
    for taken, given in zip(refs[:count], refs[count + gates :]):
        given[...] = taken[...]


def copied(values, after):
    whole = pl.BlockSpec(memory_space=pltpu.VMEM)
    return pl.pallas_call(
        functools.partial(copy_kernel, count=len(values), gates=len(after)),
        in_specs=[whole] * len(values) + [pl.BlockSpec(memory_space=pl.ANY)] * len(after),
        out_shape=[jax.ShapeDtypeStruct(value.shape, value.dtype) for value in values],
        compiler_params=params(),
        name="copied",
    )(*values, *after)


def added_kernel(keep_ref, sent_ref, *refs, first):
    rows = refs[-1].shape[0]
    cut = slice(first, first + rows)
    refs[-1][...] = (keep_ref[cut].astype(F32) + sent_ref[cut].astype(F32)).astype(BF16)


def added(keep, sent, first, rows, after):
    whole = pl.BlockSpec(memory_space=pltpu.VMEM)
    return pl.pallas_call(
        functools.partial(added_kernel, first=first),
        in_specs=[whole] * 2 + [pl.BlockSpec(memory_space=pl.ANY)] * len(after),
        out_shape=jax.ShapeDtypeStruct((rows, keep.shape[1]), BF16),
        compiler_params=params(),
        name="added",
    )(keep, sent, *after)


def total_kernel(keep_ref, sent_ref, extra_ref, *refs, count, first):
    pieces = refs[count:]
    most = pieces[0].shape[0]
    cut = slice(first * most, (first + len(pieces)) * most)
    total = keep_ref[cut].astype(F32) + sent_ref[cut].astype(F32)
    for ref in refs[:count]:
        total += ref[...].astype(F32)
    total = total.astype(BF16)
    extra = extra_ref[cut]
    width = total.shape[1]
    for j, ref in enumerate(pieces):
        ref[:, :width] = total[j * most : (j + 1) * most]
        ref[:, width:] = extra[j * most : (j + 1) * most]


def totals(keep, sent, extra, arrived, first, count, most):
    return pl.pallas_call(
        functools.partial(total_kernel, count=len(arrived), first=first),
        out_shape=[jax.ShapeDtypeStruct((most, keep.shape[1] + EXTRA), BF16)] * count,
        compiler_params=params(),
        name="totals",
    )(keep, sent, extra, *arrived)


def combine_kernel(ids_ref, own_ids_ref, weights_ref, place_ref, *refs, experts, count):
    came = jnp.concatenate([ref[...] for ref in refs[:count]], axis=0)
    grad_ref, route_ref = refs[count:]
    tokens, width = grad_ref.shape
    weight = jnp.sum(jnp.where(ids_ref[...] < experts, weights_ref[...], 0.0), axis=0, keepdims=True)
    column = jnp.broadcast_to(weight, (tokens, tokens)).T[:, :1]
    pick = place_ref[...].astype(F32).T.astype(BF16)
    taken = jnp.dot(pick, came, preferred_element_type=F32)
    grad_ref[...] = (column * taken[:, :width]).astype(BF16)
    extra = taken[:, width:].T
    total = extra[0:1] + extra[1:2]
    route_ref[...] = jnp.where(own_ids_ref[...] < experts, total, 0.0)


def combine(ids_t, own_ids_t, weights_t, place, came, experts, width):
    tokens = ids_t.shape[1]
    return pl.pallas_call(
        functools.partial(combine_kernel, experts=experts, count=len(came)),
        out_shape=(
            jax.ShapeDtypeStruct((tokens, width), BF16),
            jax.ShapeDtypeStruct(own_ids_t.shape, F32),
        ),
        compiler_params=params(),
        name="combine",
    )(ids_t, own_ids_t, weights_t, place, *came)


def local(tokens, out_grad, expert_ids, route_weights, gate_proj, up_proj, down_proj):
    seq_count = lax.axis_size("seq")
    exp_count = lax.axis_size("exp")
    tok_dev, part = tokens.shape
    top_count = expert_ids.shape[1]
    expert_count = exp_count * gate_proj.shape[0]
    most = max(2, 2 * ((tok_dev + expert_count - 1) // expert_count))
    wg, wu, wd = gate_proj[0], up_proj[0], down_proj[0]
    chips = seq_count // 2
    unit = exp_count // 8

    def of_units(*units):
        return [u * unit + j for u in units for j in range(unit)]

    seq_at = lax.axis_index("seq")
    core = seq_at % 2
    chip = seq_at // 2

    def other_core(value):
        return lax.ppermute(value, "seq", [(s, s ^ 1) for s in range(seq_count)])

    def chip_shift(value, k):
        return lax.ppermute(value, "seq", [(s, (s + 2 * k) % seq_count) for s in range(seq_count)])

    def exp_swap(value, s):
        return lax.ppermute(value, "exp", [(e, e ^ s) for e in range(exp_count)]) if s else value

    def joined(values, axis=0):
        return values[0] if len(values) == 1 else jnp.concatenate(values, axis=axis)

    ids_t = expert_ids.T
    weights_t = route_weights.T
    columns = top_count // seq_count
    own_ids_t = lax.dynamic_slice_in_dim(ids_t, seq_at * columns, columns, 0)

    def from_chips(rows):
        return [chip_shift(rows, k) for k in range(1, chips)]

    came = [None] * exp_count

    def send(pieces, group):
        for s, piece in zip(group, pieces):
            came[s] = exp_swap(piece, s)

    def send_more(group, after):
        send(copied([pieces[s] for s in group], after), group)

    def arrived_of(group):
        return joined([came[s] for s in group])

    near = of_units(0, 1, 2, 4)
    place, pieces = pack(ids_t, tokens, out_grad, expert_count, most)
    send([pieces[s] for s in near], near)
    pairs = [of_units(0), of_units(1, 2, 4), of_units(3, 5), of_units(6)]
    rows = [from_chips(arrived_of(pairs[0]))]
    send_more(pairs[2], [came[unit]] + rows[0][:1])
    rows.append(from_chips(arrived_of(pairs[1])))
    send_more(pairs[3], [came[pairs[1][-1]]] + rows[0][:1])
    after = [came[pairs[2][-1]]] + rows[1][:1]
    send_more(of_units(7), after)
    rows.append(from_chips(arrived_of(pairs[2])))
    rows.append(from_chips(copied([arrived_of(pairs[3])], rows[1][:1])[0]))

    def three(x, dy, j):
        k, other = j // 2, j % 2
        at = (chip - k) % chips * 2 + (1 - core if other else core)

        def block(weight, axis):
            return lax.dynamic_slice_in_dim(weight, at * part, part, axis)

        return [
            jnp.dot(x, block(wg, 0), preferred_element_type=F32),
            jnp.dot(x, block(wu, 0), preferred_element_type=F32),
            lax.dot_general(dy, block(wd, 1), CONTRACT, preferred_element_type=F32),
        ]

    def plus(terms, more):
        return [term + other for term, other in zip(terms, more)]

    own_x, own_dy = joined([v[:, :part] for v in came]), joined([v[:, part:] for v in came])
    end = arrived_of(of_units(7))
    terms = three(own_x, own_dy, 0)
    end_x, end_dy = copied(
        [end[:, :part], end[:, part:]], rows[2][:1] + rows[3][:1] + terms
    )
    end_x, end_dy = from_chips(end_x), from_chips(end_dy)
    terms = plus(terms, three(other_core(own_x), other_core(own_dy), 1))
    for k in range(1, chips):
        found = {}
        for values, group in zip([values[k - 1] for values in rows], pairs):
            for j, s in enumerate(group):
                found[s] = values[j * most : (j + 1) * most]
        early = [found[s] for s in sorted(found)]
        early_x = joined([value[:, :part] for value in early])
        early_dy = joined([value[:, part:] for value in early])
        last_x, last_dy = end_x[k - 1], end_dy[k - 1]
        terms = plus(terms, three(joined([early_x, last_x]), joined([early_dy, last_dy]), 2 * k))
        other_x = joined([other_core(early_x), other_core(last_x)])
        other_dy = joined([other_core(early_dy), other_core(last_dy)])
        terms = plus(terms, three(other_x, other_dy, 2 * k + 1))
    pre_gate, pre_up, back_grad = terms

    sig = jax.nn.sigmoid(pre_gate)
    active = pre_gate * sig
    grad_gate = (back_grad * pre_up * sig * (1.0 + pre_gate * (1.0 - sig))).astype(BF16)
    grad_up = (back_grad * active).astype(BF16)
    route = jnp.sum(active * pre_up * back_grad, axis=-1)

    whole_grad = (
        lax.dot_general(grad_gate, wg, CONTRACT, preferred_element_type=F32)
        + lax.dot_general(grad_up, wu, CONTRACT, preferred_element_type=F32)
    ).astype(BF16)

    def chip_part(k):
        there = (chip + k) % chips * 2

        def block(at):
            return lax.dynamic_slice_in_dim(whole_grad, at * part, part, 1)

        return block(there + core), other_core(block(there + 1 - core))

    others = [chip_part(k) for k in range(1, chips)]
    keep, sent = chip_part(0)
    half = exp_count // 2
    order = [(exp_count - unit, unit), (half, half - unit), (0, half)]
    first, count = order[0]
    summed = [added(*values, first * most, count * most, []) for values in others]

    route = route + other_core(route)
    if summed:
        route = copied([route.reshape(1, -1)], summed)[0].reshape(-1)
    route = route + sum(chip_shift(route, k) for k in range(1, chips))
    high = route.astype(BF16)
    low = (route - high.astype(F32)).astype(BF16)
    lane = lax.broadcasted_iota(jnp.int32, (route.shape[0], EXTRA), 1)
    extra = jnp.where(lane == 0, high[:, None], jnp.where(lane == 1, low[:, None], 0))

    back = [None] * exp_count
    after = []
    for first, count in order:
        if after:
            if not first:
                after = after + [back[-1]]
            summed = [added(*values, first * most, count * most, after) for values in others]
        arrived = [chip_shift(values, k) for k, values in enumerate(summed, 1)]
        pieces = totals(keep, sent, extra, arrived, first, count, most)
        for j, piece in enumerate(pieces):
            back[first + j] = exp_swap(piece, first + j)
        after = list(pieces[:1])

    own_grad, own_route_t = combine(
        ids_t, own_ids_t, weights_t, place, back, expert_count, part
    )
    return own_grad, own_route_t.T


def solution(mesh):
    in_specs = (
        P("exp", "seq"),
        P("exp", "seq"),
        P("exp", None),
        P("exp", None),
        P("exp", None, "seq"),
        P("exp", None, "seq"),
        P("exp", "seq", None),
    )
    out_specs = (P("exp", "seq"), P("exp", "seq"))
    return jax.shard_map(local, mesh=mesh, in_specs=in_specs, out_specs=out_specs, check_vma=False)
```

```python
import functools

import jax
import jax.numpy as jnp
from jax import lax
from jax.experimental import pallas as pl
from jax.experimental.pallas import tpu as pltpu
from jax.sharding import PartitionSpec as P

CONTRACT = (((1,), (1,)), ((), ()))
BF16 = jnp.bfloat16
F32 = jnp.float32
VMEM_BYTES = 8 * 1024 * 1024
EXTRA = 128


def params():
    return pltpu.CompilerParams(vmem_limit_bytes=VMEM_BYTES)


def write_pieces(place, values, refs):
    most = refs[0].shape[0]
    at = 0
    for value in values:
        rows = jnp.dot(place, value, preferred_element_type=F32)
        width = rows.shape[1]
        for s, ref in enumerate(refs):
            ref[:, at : at + width] = rows[s * most : (s + 1) * most].astype(BF16)
        at += width


def pack_kernel(ids_ref, x_ref, dy_ref, place_ref, *pieces, experts, most):
    ids = ids_ref[...]
    tokens = ids.shape[1]
    named = jnp.min(ids, axis=0, keepdims=True)
    hot = (named == lax.broadcasted_iota(jnp.int32, (experts, tokens), 0)).astype(F32)
    rows = lax.broadcasted_iota(jnp.int32, (tokens, tokens), 0)
    cols = lax.broadcasted_iota(jnp.int32, (tokens, tokens), 1)
    before = (rows < cols).astype(F32).astype(BF16)
    earlier = jnp.dot(hot.astype(BF16), before, preferred_element_type=F32)
    rank = jnp.sum(earlier * hot, axis=0, keepdims=True).astype(jnp.int32)
    target = jnp.where(named < experts, (named ^ lax.axis_index("exp")) * most + rank, -1)
    slots = lax.broadcasted_iota(jnp.int32, (experts * most, tokens), 0)
    place = (target == slots).astype(F32).astype(BF16)
    place_ref[...] = place
    write_pieces(place, (x_ref[...], dy_ref[...]), pieces)


def pack(ids_t, x, dy, experts, most):
    tokens, width = x.shape
    place, *pieces = pl.pallas_call(
        functools.partial(pack_kernel, experts=experts, most=most),
        out_shape=[jax.ShapeDtypeStruct((experts * most, tokens), BF16)]
        + [jax.ShapeDtypeStruct((most, 2 * width), BF16)] * experts,
        compiler_params=params(),
        name="pack",
    )(ids_t, x, dy)
    return place, pieces


def copy_kernel(*refs, count, gates):
    for taken, given in zip(refs[:count], refs[count + gates :]):
        given[...] = taken[...]


def copied(values, after):
    whole = pl.BlockSpec(memory_space=pltpu.VMEM)
    return pl.pallas_call(
        functools.partial(copy_kernel, count=len(values), gates=len(after)),
        in_specs=[whole] * len(values) + [pl.BlockSpec(memory_space=pl.ANY)] * len(after),
        out_shape=[jax.ShapeDtypeStruct(value.shape, value.dtype) for value in values],
        compiler_params=params(),
        name="copied",
    )(*values, *after)


def added_kernel(keep_ref, sent_ref, *refs, first):
    rows = refs[-1].shape[0]
    cut = slice(first, first + rows)
    refs[-1][...] = (keep_ref[cut].astype(F32) + sent_ref[cut].astype(F32)).astype(BF16)


def added(keep, sent, first, rows, after):
    whole = pl.BlockSpec(memory_space=pltpu.VMEM)
    return pl.pallas_call(
        functools.partial(added_kernel, first=first),
        in_specs=[whole] * 2 + [pl.BlockSpec(memory_space=pl.ANY)] * len(after),
        out_shape=jax.ShapeDtypeStruct((rows, keep.shape[1]), BF16),
        compiler_params=params(),
        name="added",
    )(keep, sent, *after)


def total_kernel(keep_ref, sent_ref, extra_ref, *refs, count, first):
    pieces = refs[count:]
    most = pieces[0].shape[0]
    cut = slice(first * most, (first + len(pieces)) * most)
    total = keep_ref[cut].astype(F32) + sent_ref[cut].astype(F32)
    for ref in refs[:count]:
        total += ref[...].astype(F32)
    total = total.astype(BF16)
    extra = extra_ref[cut]
    width = total.shape[1]
    for j, ref in enumerate(pieces):
        ref[:, :width] = total[j * most : (j + 1) * most]
        ref[:, width:] = extra[j * most : (j + 1) * most]


def totals(keep, sent, extra, arrived, first, count, most):
    return pl.pallas_call(
        functools.partial(total_kernel, count=len(arrived), first=first),
        out_shape=[jax.ShapeDtypeStruct((most, keep.shape[1] + EXTRA), BF16)] * count,
        compiler_params=params(),
        name="totals",
    )(keep, sent, extra, *arrived)


def combine_kernel(ids_ref, own_ids_ref, weights_ref, place_ref, *refs, experts, count):
    came = jnp.concatenate([ref[...] for ref in refs[:count]], axis=0)
    grad_ref, route_ref = refs[count:]
    tokens, width = grad_ref.shape
    weight = jnp.sum(jnp.where(ids_ref[...] < experts, weights_ref[...], 0.0), axis=0, keepdims=True)
    column = jnp.broadcast_to(weight, (tokens, tokens)).T[:, :1]
    pick = place_ref[...].astype(F32).T.astype(BF16)
    taken = jnp.dot(pick, came, preferred_element_type=F32)
    grad_ref[...] = (column * taken[:, :width]).astype(BF16)
    extra = taken[:, width:].T
    total = extra[0:1] + extra[1:2]
    route_ref[...] = jnp.where(own_ids_ref[...] < experts, total, 0.0)


def combine(ids_t, own_ids_t, weights_t, place, came, experts, width):
    tokens = ids_t.shape[1]
    return pl.pallas_call(
        functools.partial(combine_kernel, experts=experts, count=len(came)),
        out_shape=(
            jax.ShapeDtypeStruct((tokens, width), BF16),
            jax.ShapeDtypeStruct(own_ids_t.shape, F32),
        ),
        compiler_params=params(),
        name="combine",
    )(ids_t, own_ids_t, weights_t, place, *came)


def local(tokens, out_grad, expert_ids, route_weights, gate_proj, up_proj, down_proj):
    seq_count = lax.axis_size("seq")
    exp_count = lax.axis_size("exp")
    tok_dev, part = tokens.shape
    top_count = expert_ids.shape[1]
    expert_count = exp_count * gate_proj.shape[0]
    most = max(2, 2 * ((tok_dev + expert_count - 1) // expert_count))
    wg, wu, wd = gate_proj[0], up_proj[0], down_proj[0]
    chips = seq_count // 2
    unit = exp_count // 8

    def of_units(*units):
        return [u * unit + j for u in units for j in range(unit)]

    seq_at = lax.axis_index("seq")
    core = seq_at % 2
    chip = seq_at // 2

    def other_core(value):
        return lax.ppermute(value, "seq", [(s, s ^ 1) for s in range(seq_count)])

    def chip_shift(value, k):
        return lax.ppermute(value, "seq", [(s, (s + 2 * k) % seq_count) for s in range(seq_count)])

    def exp_swap(value, s):
        return lax.ppermute(value, "exp", [(e, e ^ s) for e in range(exp_count)]) if s else value

    def joined(values, axis=0):
        return values[0] if len(values) == 1 else jnp.concatenate(values, axis=axis)

    ids_t = expert_ids.T
    weights_t = route_weights.T
    columns = top_count // seq_count
    own_ids_t = lax.dynamic_slice_in_dim(ids_t, seq_at * columns, columns, 0)

    def from_chips(rows):
        return [chip_shift(rows, k) for k in range(1, chips)]

    came = [None] * exp_count

    def send(pieces, group):
        for s, piece in zip(group, pieces):
            came[s] = exp_swap(piece, s)

    def send_more(group, after):
        send(copied([pieces[s] for s in group], after), group)

    def arrived_of(group):
        return joined([came[s] for s in group])

    near = of_units(0, 1, 2, 4)
    place, pieces = pack(ids_t, tokens, out_grad, expert_count, most)
    send([pieces[s] for s in near], near)
    pairs = [of_units(0), of_units(1, 2, 4), of_units(3, 5), of_units(6)]
    rows = [from_chips(arrived_of(pairs[0]))]
    send_more(pairs[2], [came[unit]] + rows[0][:1])
    rows.append(from_chips(arrived_of(pairs[1])))
    send_more(pairs[3], [came[pairs[2][0]]])
    after = [came[pairs[2][-1]]] + rows[1][:1]
    send_more(of_units(7), after)
    rows.append(from_chips(arrived_of(pairs[2])))
    rows.append(from_chips(copied([arrived_of(pairs[3])], rows[1][:1])[0]))

    def three(x, dy, j):
        k, other = j // 2, j % 2
        at = (chip - k) % chips * 2 + (1 - core if other else core)

        def block(weight, axis):
            return lax.dynamic_slice_in_dim(weight, at * part, part, axis)

        return [
            jnp.dot(x, block(wg, 0), preferred_element_type=F32),
            jnp.dot(x, block(wu, 0), preferred_element_type=F32),
            lax.dot_general(dy, block(wd, 1), CONTRACT, preferred_element_type=F32),
        ]

    def plus(terms, more):
        return [term + other for term, other in zip(terms, more)]

    own_x, own_dy = joined([v[:, :part] for v in came]), joined([v[:, part:] for v in came])
    end = arrived_of(of_units(7))
    terms = three(own_x, own_dy, 0)
    end_x, end_dy = copied([end[:, :part], end[:, part:]], rows[2][:1] + rows[3][:1])
    end_x, end_dy = from_chips(end_x), from_chips(end_dy)
    terms = plus(terms, three(other_core(own_x), other_core(own_dy), 1))
    for k in range(1, chips):
        found = {}
        for values, group in zip([values[k - 1] for values in rows], pairs):
            for j, s in enumerate(group):
                found[s] = values[j * most : (j + 1) * most]
        early = [found[s] for s in sorted(found)]
        early_x = joined([value[:, :part] for value in early])
        early_dy = joined([value[:, part:] for value in early])
        last_x, last_dy = end_x[k - 1], end_dy[k - 1]
        terms = plus(terms, three(joined([early_x, last_x]), joined([early_dy, last_dy]), 2 * k))
        other_x = joined([other_core(early_x), other_core(last_x)])
        other_dy = joined([other_core(early_dy), other_core(last_dy)])
        terms = plus(terms, three(other_x, other_dy, 2 * k + 1))
    pre_gate, pre_up, back_grad = terms

    sig = jax.nn.sigmoid(pre_gate)
    active = pre_gate * sig
    grad_gate = (back_grad * pre_up * sig * (1.0 + pre_gate * (1.0 - sig))).astype(BF16)
    grad_up = (back_grad * active).astype(BF16)
    route = jnp.sum(active * pre_up * back_grad, axis=-1)

    def block_grad(at):
        cut = slice(at * part, (at + 1) * part)
        return (
            lax.dot_general(grad_gate, wg[cut], CONTRACT, preferred_element_type=F32)
            + lax.dot_general(grad_up, wu[cut], CONTRACT, preferred_element_type=F32)
        ).astype(BF16)

    whole_grad = joined([block_grad(at) for at in range(seq_count)], axis=1)

    def chip_part(k):
        there = (chip + k) % chips * 2

        def block(at):
            return lax.dynamic_slice_in_dim(whole_grad, at * part, part, 1)

        return block(there + core), other_core(block(there + 1 - core))

    others = [chip_part(k) for k in range(1, chips)]
    keep, sent = chip_part(0)
    half = exp_count // 2
    order = [(exp_count - unit, unit), (half, half - unit), (0, half)]
    first, count = order[0]
    summed = [added(*values, first * most, count * most, []) for values in others]

    route = route + other_core(route)
    if summed:
        route = copied([route.reshape(1, -1)], summed)[0].reshape(-1)
    route = route + sum(chip_shift(route, k) for k in range(1, chips))
    high = route.astype(BF16)
    low = (route - high.astype(F32)).astype(BF16)
    lane = lax.broadcasted_iota(jnp.int32, (route.shape[0], EXTRA), 1)
    extra = jnp.where(lane == 0, high[:, None], jnp.where(lane == 1, low[:, None], 0))

    back = [None] * exp_count
    after = []
    for first, count in order:
        if after:
            if not first:
                after = after + [back[-1]]
            summed = [added(*values, first * most, count * most, after) for values in others]
        arrived = [chip_shift(values, k) for k, values in enumerate(summed, 1)]
        pieces = totals(keep, sent, extra, arrived, first, count, most)
        for j, piece in enumerate(pieces):
            back[first + j] = exp_swap(piece, first + j)
        after = list(pieces[:1])

    own_grad, own_route_t = combine(
        ids_t, own_ids_t, weights_t, place, back, expert_count, part
    )
    return own_grad, own_route_t.T


def solution(mesh):
    in_specs = (
        P("exp", "seq"),
        P("exp", "seq"),
        P("exp", None),
        P("exp", None),
        P("exp", None, "seq"),
        P("exp", None, "seq"),
        P("exp", "seq", None),
    )
    out_specs = (P("exp", "seq"), P("exp", "seq"))
    return jax.shard_map(local, mesh=mesh, in_specs=in_specs, out_specs=out_specs, check_vma=False)
```

```python
import functools

import jax
import jax.numpy as jnp
from jax import lax
from jax.experimental import pallas as pl
from jax.experimental.pallas import tpu as pltpu
from jax.sharding import PartitionSpec as P

CONTRACT = (((1,), (1,)), ((), ()))
BF16 = jnp.bfloat16
F32 = jnp.float32
VMEM_BYTES = 8 * 1024 * 1024
EXTRA = 128


def params():
    return pltpu.CompilerParams(vmem_limit_bytes=VMEM_BYTES)


def write_pieces(place, values, refs):
    most = refs[0].shape[0]
    at = 0
    for value in values:
        rows = jnp.dot(place, value, preferred_element_type=F32)
        width = rows.shape[1]
        for s, ref in enumerate(refs):
            ref[:, at : at + width] = rows[s * most : (s + 1) * most].astype(BF16)
        at += width


def pack_kernel(ids_ref, x_ref, dy_ref, place_ref, *pieces, experts, most):
    ids = ids_ref[...]
    tokens = ids.shape[1]
    named = jnp.min(ids, axis=0, keepdims=True)
    hot = (named == lax.broadcasted_iota(jnp.int32, (experts, tokens), 0)).astype(F32)
    rows = lax.broadcasted_iota(jnp.int32, (tokens, tokens), 0)
    cols = lax.broadcasted_iota(jnp.int32, (tokens, tokens), 1)
    before = (rows < cols).astype(F32).astype(BF16)
    earlier = jnp.dot(hot.astype(BF16), before, preferred_element_type=F32)
    rank = jnp.sum(earlier * hot, axis=0, keepdims=True).astype(jnp.int32)
    target = jnp.where(named < experts, (named ^ lax.axis_index("exp")) * most + rank, -1)
    slots = lax.broadcasted_iota(jnp.int32, (experts * most, tokens), 0)
    place = (target == slots).astype(F32).astype(BF16)
    place_ref[...] = place
    write_pieces(place, (x_ref[...], dy_ref[...]), pieces)


def pack(ids_t, x, dy, experts, most):
    tokens, width = x.shape
    place, *pieces = pl.pallas_call(
        functools.partial(pack_kernel, experts=experts, most=most),
        out_shape=[jax.ShapeDtypeStruct((experts * most, tokens), BF16)]
        + [jax.ShapeDtypeStruct((most, 2 * width), BF16)] * experts,
        compiler_params=params(),
        name="pack",
    )(ids_t, x, dy)
    return place, pieces


def copy_kernel(*refs, count, gates):
    for taken, given in zip(refs[:count], refs[count + gates :]):
        given[...] = taken[...]


def copied(values, after):
    whole = pl.BlockSpec(memory_space=pltpu.VMEM)
    return pl.pallas_call(
        functools.partial(copy_kernel, count=len(values), gates=len(after)),
        in_specs=[whole] * len(values) + [pl.BlockSpec(memory_space=pl.ANY)] * len(after),
        out_shape=[jax.ShapeDtypeStruct(value.shape, value.dtype) for value in values],
        compiler_params=params(),
        name="copied",
    )(*values, *after)


def split_kernel(*refs, count, shift):
    taken, sums_ref, keep_ref, sent_ref = refs[:count], *refs[count:]
    seq_at = lax.axis_index("seq")
    core = lax.rem(seq_at, 2)
    there = lax.rem(lax.div(seq_at, 2) + shift, count // 2) * 2
    width = keep_ref.shape[1]
    sent_ref[:, width:] = sums_ref[...]
    for j in range(count):

        @pl.when(there + core == j)
        def _(j=j):
            keep_ref[...] = taken[j][...]

        @pl.when(there + 1 - core == j)
        def _(j=j):
            sent_ref[:, :width] = taken[j][...]


def split(taken, sums, shift):
    rows, width = taken[0].shape
    return pl.pallas_call(
        functools.partial(split_kernel, count=len(taken), shift=shift),
        out_shape=[
            jax.ShapeDtypeStruct((rows, width), BF16),
            jax.ShapeDtypeStruct((rows, width + EXTRA), BF16),
        ],
        compiler_params=params(),
        name="split",
    )(*taken, sums)


def two_halves(value):
    high = value.astype(BF16).astype(F32)
    lane = lax.broadcasted_iota(jnp.int32, (value.shape[0], EXTRA), 1)
    return jnp.where(lane == 0, high, jnp.where(lane == 1, value - high, 0.0)).astype(BF16)


def add_up(keep, sums, sent, arrived):
    width = keep.shape[1]
    total = keep.astype(F32)
    route = jnp.sum(sums.astype(F32), axis=1, keepdims=True)
    for message in (sent, *arrived):
        total += message[:, :width].astype(F32)
        route += jnp.sum(message[:, width:].astype(F32), axis=1, keepdims=True)
    return total.astype(BF16), two_halves(route)


def added_kernel(keep_ref, sums_ref, sent_ref, *refs, first):
    rows, width = refs[-1].shape[0], keep_ref.shape[1]
    cut = slice(first, first + rows)
    total, route = add_up(keep_ref[cut], sums_ref[cut], sent_ref[cut], ())
    refs[-1][:, :width] = total
    refs[-1][:, width:] = route


def added(keep, sums, sent, first, rows, after):
    whole = pl.BlockSpec(memory_space=pltpu.VMEM)
    return pl.pallas_call(
        functools.partial(added_kernel, first=first),
        in_specs=[whole] * 3 + [pl.BlockSpec(memory_space=pl.ANY)] * len(after),
        out_shape=jax.ShapeDtypeStruct((rows, sent.shape[1]), BF16),
        compiler_params=params(),
        name="added",
    )(keep, sums, sent, *after)


def total_kernel(keep_ref, sums_ref, sent_ref, *refs, count, first):
    pieces = refs[count:]
    most, width = pieces[0].shape[0], keep_ref.shape[1]
    cut = slice(first * most, (first + len(pieces)) * most)
    arrived = [ref[...] for ref in refs[:count]]
    total, route = add_up(keep_ref[cut], sums_ref[cut], sent_ref[cut], arrived)
    for j, ref in enumerate(pieces):
        ref[:, :width] = total[j * most : (j + 1) * most]
        ref[:, width:] = route[j * most : (j + 1) * most]


def totals(keep, sums, sent, arrived, first, count, most):
    return pl.pallas_call(
        functools.partial(total_kernel, count=len(arrived), first=first),
        out_shape=[jax.ShapeDtypeStruct((most, sent.shape[1]), BF16)] * count,
        compiler_params=params(),
        name="totals",
    )(keep, sums, sent, *arrived)


def combine_kernel(ids_ref, own_ids_ref, weights_ref, place_ref, *refs, experts, count):
    came = jnp.concatenate([ref[...] for ref in refs[:count]], axis=0)
    grad_ref, route_ref = refs[count:]
    tokens, width = grad_ref.shape
    weight = jnp.sum(jnp.where(ids_ref[...] < experts, weights_ref[...], 0.0), axis=0, keepdims=True)
    column = jnp.broadcast_to(weight, (tokens, tokens)).T[:, :1]
    pick = place_ref[...].astype(F32).T.astype(BF16)
    taken = jnp.dot(pick, came, preferred_element_type=F32)
    grad_ref[...] = (column * taken[:, :width]).astype(BF16)
    extra = taken[:, width:].T
    total = extra[0:1] + extra[1:2]
    route_ref[...] = jnp.where(own_ids_ref[...] < experts, total, 0.0)


def combine(ids_t, own_ids_t, weights_t, place, came, experts, width):
    tokens = ids_t.shape[1]
    return pl.pallas_call(
        functools.partial(combine_kernel, experts=experts, count=len(came)),
        out_shape=(
            jax.ShapeDtypeStruct((tokens, width), BF16),
            jax.ShapeDtypeStruct(own_ids_t.shape, F32),
        ),
        compiler_params=params(),
        name="combine",
    )(ids_t, own_ids_t, weights_t, place, *came)


def local(tokens, out_grad, expert_ids, route_weights, gate_proj, up_proj, down_proj):
    seq_count = lax.axis_size("seq")
    exp_count = lax.axis_size("exp")
    tok_dev, part = tokens.shape
    top_count = expert_ids.shape[1]
    expert_count = exp_count * gate_proj.shape[0]
    most = max(2, 2 * ((tok_dev + expert_count - 1) // expert_count))
    wg, wu, wd = gate_proj[0], up_proj[0], down_proj[0]
    chips = seq_count // 2
    unit = exp_count // 8

    def of_units(*units):
        return [u * unit + j for u in units for j in range(unit)]

    seq_at = lax.axis_index("seq")
    core = seq_at % 2
    chip = seq_at // 2

    def other_core(value):
        return lax.ppermute(value, "seq", [(s, s ^ 1) for s in range(seq_count)])

    def chip_shift(value, k):
        return lax.ppermute(value, "seq", [(s, (s + 2 * k) % seq_count) for s in range(seq_count)])

    def exp_swap(value, s):
        return lax.ppermute(value, "exp", [(e, e ^ s) for e in range(exp_count)]) if s else value

    def joined(values, axis=0):
        return values[0] if len(values) == 1 else jnp.concatenate(values, axis=axis)

    ids_t = expert_ids.T
    weights_t = route_weights.T
    columns = top_count // seq_count
    own_ids_t = lax.dynamic_slice_in_dim(ids_t, seq_at * columns, columns, 0)

    def from_chips(rows):
        return [chip_shift(rows, k) for k in range(1, chips)]

    came = [None] * exp_count

    def send(pieces, group):
        for s, piece in zip(group, pieces):
            came[s] = exp_swap(piece, s)

    def send_more(group, after):
        send(copied([pieces[s] for s in group], after), group)

    def arrived_of(group):
        return joined([came[s] for s in group])

    near = of_units(0, 1, 2, 4, 5)
    place, pieces = pack(ids_t, tokens, out_grad, expert_count, most)
    send([pieces[s] for s in near], near)
    pairs = [of_units(0), of_units(1, 2), of_units(3, 4, 5), of_units(6)]
    rows = [from_chips(arrived_of(pairs[0]))]
    send_more(of_units(3), rows[0][:1])
    rows.append(from_chips(arrived_of(pairs[1])))
    send_more(of_units(6), [came[of_units(4)[-1]]])
    send_more(of_units(7), [came[of_units(5)[-1]]] + rows[1][:1])
    rows.append(from_chips(arrived_of(pairs[2])))
    rows.append(from_chips(copied([arrived_of(pairs[3])], rows[1][:1])[0]))

    def three(x, dy, j):
        k, other = j // 2, j % 2
        at = (chip - k) % chips * 2 + (1 - core if other else core)

        def block(weight, axis):
            return lax.dynamic_slice_in_dim(weight, at * part, part, axis)

        return [
            jnp.dot(x, block(wg, 0), preferred_element_type=F32),
            jnp.dot(x, block(wu, 0), preferred_element_type=F32),
            lax.dot_general(dy, block(wd, 1), CONTRACT, preferred_element_type=F32),
        ]

    def plus(terms, more):
        return [term + other for term, other in zip(terms, more)]

    own_x, own_dy = joined([v[:, :part] for v in came]), joined([v[:, part:] for v in came])
    end = arrived_of(of_units(7))
    terms = three(own_x, own_dy, 0)
    end_x, end_dy = copied([end[:, :part], end[:, part:]], rows[2][:1] + rows[3][:1])
    end_x, end_dy = from_chips(end_x), from_chips(end_dy)
    terms = plus(terms, three(other_core(own_x), other_core(own_dy), 1))
    for k in range(1, chips):
        found = {}
        for values, group in zip([values[k - 1] for values in rows], pairs):
            for j, s in enumerate(group):
                found[s] = values[j * most : (j + 1) * most]
        early = [found[s] for s in sorted(found)]
        early_x = joined([value[:, :part] for value in early])
        early_dy = joined([value[:, part:] for value in early])
        last_x, last_dy = end_x[k - 1], end_dy[k - 1]
        terms = plus(terms, three(joined([early_x, last_x]), joined([early_dy, last_dy]), 2 * k))
        other_x = joined([other_core(early_x), other_core(last_x)])
        other_dy = joined([other_core(early_dy), other_core(last_dy)])
        terms = plus(terms, three(other_x, other_dy, 2 * k + 1))
    pre_gate, pre_up, back_grad = terms

    sig = jax.nn.sigmoid(pre_gate)
    active = pre_gate * sig
    grad_gate = (back_grad * pre_up * sig * (1.0 + pre_gate * (1.0 - sig))).astype(BF16)
    grad_up = (back_grad * active).astype(BF16)
    route = jnp.sum(active * pre_up * back_grad, axis=-1)

    def block_grad(at):
        cut = slice(at * part, (at + 1) * part)
        return (
            lax.dot_general(grad_gate, wg[cut], CONTRACT, preferred_element_type=F32)
            + lax.dot_general(grad_up, wu[cut], CONTRACT, preferred_element_type=F32)
        ).astype(BF16)

    block_grads = [block_grad(at) for at in range(seq_count)]
    sums = two_halves(route[:, None])
    others = []
    for k in range(1, chips):
        keep, sent = split(block_grads, sums, k)
        others.append((keep, sums, other_core(sent)))
    half = exp_count // 2
    order = [(exp_count - unit, unit), (half, half - unit), (0, half)]
    first, count = order[0]
    summed = [added(*values, first * most, count * most, []) for values in others]
    keep, sent = split(block_grads, sums, 0)
    sent = other_core(copied([sent], summed)[0])

    back = [None] * exp_count
    after = []
    for first, count in order:
        if after:
            if not first:
                after = after + [back[-1]]
            summed = [added(*values, first * most, count * most, after) for values in others]
        arrived = [chip_shift(values, k) for k, values in enumerate(summed, 1)]
        pieces = totals(keep, sums, sent, arrived, first, count, most)
        for j, piece in enumerate(pieces):
            back[first + j] = exp_swap(piece, first + j)
        after = list(pieces[:1])

    own_grad, own_route_t = combine(
        ids_t, own_ids_t, weights_t, place, back, expert_count, part
    )
    return own_grad, own_route_t.T


def solution(mesh):
    in_specs = (
        P("exp", "seq"),
        P("exp", "seq"),
        P("exp", None),
        P("exp", None),
        P("exp", None, "seq"),
        P("exp", None, "seq"),
        P("exp", "seq", None),
    )
    out_specs = (P("exp", "seq"), P("exp", "seq"))
    return jax.shard_map(local, mesh=mesh, in_specs=in_specs, out_specs=out_specs, check_vma=False)
```

```python
import functools

import jax
import jax.numpy as jnp
from jax import lax
from jax.experimental import pallas as pl
from jax.experimental.pallas import tpu as pltpu
from jax.sharding import PartitionSpec as P

CONTRACT = (((1,), (1,)), ((), ()))
BF16 = jnp.bfloat16
F32 = jnp.float32
VMEM_BYTES = 8 * 1024 * 1024
EXTRA = 128


def params():
    return pltpu.CompilerParams(vmem_limit_bytes=VMEM_BYTES)


def write_pieces(place, values, refs):
    most = refs[0].shape[0]
    at = 0
    for value in values:
        rows = jnp.dot(place, value, preferred_element_type=F32)
        width = rows.shape[1]
        for s, ref in enumerate(refs):
            ref[:, at : at + width] = rows[s * most : (s + 1) * most].astype(BF16)
        at += width


def pack_kernel(ids_ref, x_ref, dy_ref, place_ref, *pieces, experts, most):
    ids = ids_ref[...]
    tokens = ids.shape[1]
    named = jnp.min(ids, axis=0, keepdims=True)
    hot = (named == lax.broadcasted_iota(jnp.int32, (experts, tokens), 0)).astype(F32)
    rows = lax.broadcasted_iota(jnp.int32, (tokens, tokens), 0)
    cols = lax.broadcasted_iota(jnp.int32, (tokens, tokens), 1)
    before = (rows < cols).astype(F32).astype(BF16)
    earlier = jnp.dot(hot.astype(BF16), before, preferred_element_type=F32)
    rank = jnp.sum(earlier * hot, axis=0, keepdims=True).astype(jnp.int32)
    target = jnp.where(named < experts, (named ^ lax.axis_index("exp")) * most + rank, -1)
    slots = lax.broadcasted_iota(jnp.int32, (experts * most, tokens), 0)
    place = (target == slots).astype(F32).astype(BF16)
    place_ref[...] = place
    write_pieces(place, (x_ref[...], dy_ref[...]), pieces)


def pack(ids_t, x, dy, experts, most):
    tokens, width = x.shape
    place, *pieces = pl.pallas_call(
        functools.partial(pack_kernel, experts=experts, most=most),
        out_shape=[jax.ShapeDtypeStruct((experts * most, tokens), BF16)]
        + [jax.ShapeDtypeStruct((most, 2 * width), BF16)] * experts,
        compiler_params=params(),
        name="pack",
    )(ids_t, x, dy)
    return place, pieces


def copy_kernel(*refs, count, gates):
    for taken, given in zip(refs[:count], refs[count + gates :]):
        given[...] = taken[...]


def copied(values, after):
    whole = pl.BlockSpec(memory_space=pltpu.VMEM)
    return pl.pallas_call(
        functools.partial(copy_kernel, count=len(values), gates=len(after)),
        in_specs=[whole] * len(values) + [pl.BlockSpec(memory_space=pl.ANY)] * len(after),
        out_shape=[jax.ShapeDtypeStruct(value.shape, value.dtype) for value in values],
        compiler_params=params(),
        name="copied",
    )(*values, *after)


def split_kernel(*refs, count, shift):
    taken, sums_ref, keep_ref, sent_ref = refs[:count], *refs[count:]
    seq_at = lax.axis_index("seq")
    core = lax.rem(seq_at, 2)
    there = lax.rem(lax.div(seq_at, 2) + shift, count // 2) * 2
    width = keep_ref.shape[1]
    sent_ref[:, width:] = sums_ref[...]
    for j in range(count):

        @pl.when(there + core == j)
        def _(j=j):
            keep_ref[...] = taken[j][...]

        @pl.when(there + 1 - core == j)
        def _(j=j):
            sent_ref[:, :width] = taken[j][...]


def split(taken, sums, shift):
    rows, width = taken[0].shape
    return pl.pallas_call(
        functools.partial(split_kernel, count=len(taken), shift=shift),
        out_shape=[
            jax.ShapeDtypeStruct((rows, width), BF16),
            jax.ShapeDtypeStruct((rows, width + EXTRA), BF16),
        ],
        compiler_params=params(),
        name="split",
    )(*taken, sums)


def two_halves(value):
    high = value.astype(BF16).astype(F32)
    lane = lax.broadcasted_iota(jnp.int32, (value.shape[0], EXTRA), 1)
    return jnp.where(lane == 0, high, jnp.where(lane == 1, value - high, 0.0)).astype(BF16)


def add_up(keep, sums, sent, arrived):
    width = keep.shape[1]
    total = keep.astype(F32)
    route = jnp.sum(sums.astype(F32), axis=1, keepdims=True)
    for message in (sent, *arrived):
        total += message[:, :width].astype(F32)
        route += jnp.sum(message[:, width:].astype(F32), axis=1, keepdims=True)
    return total.astype(BF16), two_halves(route)


def added_kernel(keep_ref, sums_ref, sent_ref, *refs, first):
    rows, width = refs[-1].shape[0], keep_ref.shape[1]
    cut = slice(first, first + rows)
    total, route = add_up(keep_ref[cut], sums_ref[cut], sent_ref[cut], ())
    refs[-1][:, :width] = total
    refs[-1][:, width:] = route


def added(keep, sums, sent, first, rows, after):
    whole = pl.BlockSpec(memory_space=pltpu.VMEM)
    return pl.pallas_call(
        functools.partial(added_kernel, first=first),
        in_specs=[whole] * 3 + [pl.BlockSpec(memory_space=pl.ANY)] * len(after),
        out_shape=jax.ShapeDtypeStruct((rows, sent.shape[1]), BF16),
        compiler_params=params(),
        name="added",
    )(keep, sums, sent, *after)


def total_kernel(keep_ref, sums_ref, sent_ref, *refs, count, first):
    pieces = refs[count:]
    most, width = pieces[0].shape[0], keep_ref.shape[1]
    cut = slice(first * most, (first + len(pieces)) * most)
    arrived = [ref[...] for ref in refs[:count]]
    total, route = add_up(keep_ref[cut], sums_ref[cut], sent_ref[cut], arrived)
    for j, ref in enumerate(pieces):
        ref[:, :width] = total[j * most : (j + 1) * most]
        ref[:, width:] = route[j * most : (j + 1) * most]


def totals(keep, sums, sent, arrived, first, count, most):
    return pl.pallas_call(
        functools.partial(total_kernel, count=len(arrived), first=first),
        out_shape=[jax.ShapeDtypeStruct((most, sent.shape[1]), BF16)] * count,
        compiler_params=params(),
        name="totals",
    )(keep, sums, sent, *arrived)


def combine_kernel(ids_ref, own_ids_ref, weights_ref, place_ref, *refs, experts, count):
    came = jnp.concatenate([ref[...] for ref in refs[:count]], axis=0)
    grad_ref, route_ref = refs[count:]
    tokens, width = grad_ref.shape
    weight = jnp.sum(jnp.where(ids_ref[...] < experts, weights_ref[...], 0.0), axis=0, keepdims=True)
    column = jnp.broadcast_to(weight, (tokens, tokens)).T[:, :1]
    pick = place_ref[...].astype(F32).T.astype(BF16)
    taken = jnp.dot(pick, came, preferred_element_type=F32)
    grad_ref[...] = (column * taken[:, :width]).astype(BF16)
    extra = taken[:, width:].T
    total = extra[0:1] + extra[1:2]
    route_ref[...] = jnp.where(own_ids_ref[...] < experts, total, 0.0)


def combine(ids_t, own_ids_t, weights_t, place, came, experts, width):
    tokens = ids_t.shape[1]
    return pl.pallas_call(
        functools.partial(combine_kernel, experts=experts, count=len(came)),
        out_shape=(
            jax.ShapeDtypeStruct((tokens, width), BF16),
            jax.ShapeDtypeStruct(own_ids_t.shape, F32),
        ),
        compiler_params=params(),
        name="combine",
    )(ids_t, own_ids_t, weights_t, place, *came)


def local(tokens, out_grad, expert_ids, route_weights, gate_proj, up_proj, down_proj):
    seq_count = lax.axis_size("seq")
    exp_count = lax.axis_size("exp")
    tok_dev, part = tokens.shape
    top_count = expert_ids.shape[1]
    expert_count = exp_count * gate_proj.shape[0]
    most = max(2, 2 * ((tok_dev + expert_count - 1) // expert_count))
    wg, wu, wd = gate_proj[0], up_proj[0], down_proj[0]
    chips = seq_count // 2
    unit = exp_count // 8

    def of_units(*units):
        return [u * unit + j for u in units for j in range(unit)]

    seq_at = lax.axis_index("seq")
    core = seq_at % 2
    chip = seq_at // 2

    def other_core(value):
        return lax.ppermute(value, "seq", [(s, s ^ 1) for s in range(seq_count)])

    def chip_shift(value, k):
        return lax.ppermute(value, "seq", [(s, (s + 2 * k) % seq_count) for s in range(seq_count)])

    def exp_swap(value, s):
        return lax.ppermute(value, "exp", [(e, e ^ s) for e in range(exp_count)]) if s else value

    def joined(values, axis=0):
        return values[0] if len(values) == 1 else jnp.concatenate(values, axis=axis)

    ids_t = expert_ids.T
    weights_t = route_weights.T
    columns = top_count // seq_count
    own_ids_t = lax.dynamic_slice_in_dim(ids_t, seq_at * columns, columns, 0)

    def from_chips(rows):
        return [chip_shift(rows, k) for k in range(1, chips)]

    came = [None] * exp_count

    def send(pieces, group):
        for s, piece in zip(group, pieces):
            came[s] = exp_swap(piece, s)

    def send_more(group, after):
        send(copied([pieces[s] for s in group], after), group)

    def arrived_of(group):
        return joined([came[s] for s in group])

    near = of_units(0, 1, 2, 4, 5)
    place, pieces = pack(ids_t, tokens, out_grad, expert_count, most)
    send([pieces[s] for s in near], near)
    pairs = [of_units(0), of_units(1, 2), of_units(3, 4, 5), of_units(6)]
    rows = [from_chips(arrived_of(pairs[0]))]
    send_more(of_units(3), rows[0][:1])
    rows.append(from_chips(arrived_of(pairs[1])))
    send_more(of_units(6), [came[of_units(j)[-1]] for j in (3, 4)] + rows[1][:1])
    send_more(of_units(7), [came[of_units(5)[-1]]] + rows[1][:1])
    rows.append(from_chips(arrived_of(pairs[2])))
    rows.append(from_chips(copied([arrived_of(pairs[3])], rows[1][:1])[0]))

    def three(x, dy, j):
        k, other = j // 2, j % 2
        at = (chip - k) % chips * 2 + (1 - core if other else core)

        def block(weight, axis):
            return lax.dynamic_slice_in_dim(weight, at * part, part, axis)

        return [
            jnp.dot(x, block(wg, 0), preferred_element_type=F32),
            jnp.dot(x, block(wu, 0), preferred_element_type=F32),
            lax.dot_general(dy, block(wd, 1), CONTRACT, preferred_element_type=F32),
        ]

    def plus(terms, more):
        return [term + other for term, other in zip(terms, more)]

    own_x, own_dy = joined([v[:, :part] for v in came]), joined([v[:, part:] for v in came])
    end = arrived_of(of_units(7))
    terms = three(own_x, own_dy, 0)
    end_x, end_dy = copied([end[:, :part], end[:, part:]], rows[2][:1] + rows[3][:1])
    end_x, end_dy = from_chips(end_x), from_chips(end_dy)
    terms = plus(terms, three(other_core(own_x), other_core(own_dy), 1))
    for k in range(1, chips):
        found = {}
        for values, group in zip([values[k - 1] for values in rows], pairs):
            for j, s in enumerate(group):
                found[s] = values[j * most : (j + 1) * most]
        early = [found[s] for s in sorted(found)]
        early_x = joined([value[:, :part] for value in early])
        early_dy = joined([value[:, part:] for value in early])
        last_x, last_dy = end_x[k - 1], end_dy[k - 1]
        terms = plus(terms, three(joined([early_x, last_x]), joined([early_dy, last_dy]), 2 * k))
        other_x = joined([other_core(early_x), other_core(last_x)])
        other_dy = joined([other_core(early_dy), other_core(last_dy)])
        terms = plus(terms, three(other_x, other_dy, 2 * k + 1))
    pre_gate, pre_up, back_grad = terms

    sig = jax.nn.sigmoid(pre_gate)
    active = pre_gate * sig
    grad_gate = (back_grad * pre_up * sig * (1.0 + pre_gate * (1.0 - sig))).astype(BF16)
    grad_up = (back_grad * active).astype(BF16)
    route = jnp.sum(active * pre_up * back_grad, axis=-1)

    def block_grad(at):
        cut = slice(at * part, (at + 1) * part)
        return (
            lax.dot_general(grad_gate, wg[cut], CONTRACT, preferred_element_type=F32)
            + lax.dot_general(grad_up, wu[cut], CONTRACT, preferred_element_type=F32)
        ).astype(BF16)

    block_grads = [block_grad(at) for at in range(seq_count)]
    sums = two_halves(route[:, None])
    others = []
    for k in range(1, chips):
        keep, sent = split(block_grads, sums, k)
        others.append((keep, sums, other_core(sent)))
    order = [(7 * unit, unit), (3 * unit, 4 * unit), (0, 3 * unit)]
    first, count = order[0]
    summed = [added(*values, first * most, count * most, []) for values in others]
    keep, sent = split(block_grads, sums, 0)
    sent = other_core(copied([sent], summed)[0])

    back = [None] * exp_count
    after = []
    for first, count in order:
        if after:
            if not first:
                after = after + [back[-1]]
            summed = [added(*values, first * most, count * most, after) for values in others]
        arrived = [chip_shift(values, k) for k, values in enumerate(summed, 1)]
        pieces = totals(keep, sums, sent, arrived, first, count, most)
        for j, piece in enumerate(pieces):
            back[first + j] = exp_swap(piece, first + j)
        after = list(pieces[:1])

    own_grad, own_route_t = combine(
        ids_t, own_ids_t, weights_t, place, back, expert_count, part
    )
    return own_grad, own_route_t.T


def solution(mesh):
    in_specs = (
        P("exp", "seq"),
        P("exp", "seq"),
        P("exp", None),
        P("exp", None),
        P("exp", None, "seq"),
        P("exp", None, "seq"),
        P("exp", "seq", None),
    )
    out_specs = (P("exp", "seq"), P("exp", "seq"))
    return jax.shard_map(local, mesh=mesh, in_specs=in_specs, out_specs=out_specs, check_vma=False)
```

```python
import functools

import jax
import jax.numpy as jnp
from jax import lax
from jax.experimental import pallas as pl
from jax.experimental.pallas import tpu as pltpu
from jax.sharding import PartitionSpec as P

CONTRACT = (((1,), (1,)), ((), ()))
BF16 = jnp.bfloat16
F32 = jnp.float32
VMEM_BYTES = 8 * 1024 * 1024
EXTRA = 128


def params():
    return pltpu.CompilerParams(vmem_limit_bytes=VMEM_BYTES)


def write_pieces(place, values, refs):
    most = refs[0].shape[0]
    at = 0
    for value in values:
        rows = jnp.dot(place, value, preferred_element_type=F32)
        width = rows.shape[1]
        for s, ref in enumerate(refs):
            ref[:, at : at + width] = rows[s * most : (s + 1) * most].astype(BF16)
        at += width


def pack_kernel(ids_ref, x_ref, dy_ref, place_ref, *pieces, experts, most):
    ids = ids_ref[...]
    tokens = ids.shape[1]
    named = jnp.min(ids, axis=0, keepdims=True)
    hot = (named == lax.broadcasted_iota(jnp.int32, (experts, tokens), 0)).astype(F32)
    rows = lax.broadcasted_iota(jnp.int32, (tokens, tokens), 0)
    cols = lax.broadcasted_iota(jnp.int32, (tokens, tokens), 1)
    before = (rows < cols).astype(F32).astype(BF16)
    earlier = jnp.dot(hot.astype(BF16), before, preferred_element_type=F32)
    rank = jnp.sum(earlier * hot, axis=0, keepdims=True).astype(jnp.int32)
    target = jnp.where(named < experts, (named ^ lax.axis_index("exp")) * most + rank, -1)
    slots = lax.broadcasted_iota(jnp.int32, (experts * most, tokens), 0)
    place = (target == slots).astype(F32).astype(BF16)
    place_ref[...] = place
    write_pieces(place, (x_ref[...], dy_ref[...]), pieces)


def pack(ids_t, x, dy, experts, most):
    tokens, width = x.shape
    place, *pieces = pl.pallas_call(
        functools.partial(pack_kernel, experts=experts, most=most),
        out_shape=[jax.ShapeDtypeStruct((experts * most, tokens), BF16)]
        + [jax.ShapeDtypeStruct((most, 2 * width), BF16)] * experts,
        compiler_params=params(),
        name="pack",
    )(ids_t, x, dy)
    return place, pieces


def copy_kernel(*refs, count, gates):
    for taken, given in zip(refs[:count], refs[count + gates :]):
        given[...] = taken[...]


def copied(values, after):
    whole = pl.BlockSpec(memory_space=pltpu.VMEM)
    return pl.pallas_call(
        functools.partial(copy_kernel, count=len(values), gates=len(after)),
        in_specs=[whole] * len(values) + [pl.BlockSpec(memory_space=pl.ANY)] * len(after),
        out_shape=[jax.ShapeDtypeStruct(value.shape, value.dtype) for value in values],
        compiler_params=params(),
        name="copied",
    )(*values, *after)


def split_kernel(*refs, count, shift):
    taken, sums_ref, keep_ref, sent_ref = refs[:count], *refs[count:]
    seq_at = lax.axis_index("seq")
    core = lax.rem(seq_at, 2)
    there = lax.rem(lax.div(seq_at, 2) + shift, count // 2) * 2
    width = keep_ref.shape[1]
    sent_ref[:, width:] = sums_ref[...]
    for j in range(count):

        @pl.when(there + core == j)
        def _(j=j):
            keep_ref[...] = taken[j][...]

        @pl.when(there + 1 - core == j)
        def _(j=j):
            sent_ref[:, :width] = taken[j][...]


def split(taken, sums, shift):
    rows, width = taken[0].shape
    return pl.pallas_call(
        functools.partial(split_kernel, count=len(taken), shift=shift),
        out_shape=[
            jax.ShapeDtypeStruct((rows, width), BF16),
            jax.ShapeDtypeStruct((rows, width + EXTRA), BF16),
        ],
        compiler_params=params(),
        name="split",
    )(*taken, sums)


def two_halves(value):
    high = value.astype(BF16).astype(F32)
    lane = lax.broadcasted_iota(jnp.int32, (value.shape[0], EXTRA), 1)
    return jnp.where(lane == 0, high, jnp.where(lane == 1, value - high, 0.0)).astype(BF16)


def add_up(keep, sums, sent, arrived):
    width = keep.shape[1]
    total = keep.astype(F32)
    route = jnp.sum(sums.astype(F32), axis=1, keepdims=True)
    for message in (sent, *arrived):
        total += message[:, :width].astype(F32)
        route += jnp.sum(message[:, width:].astype(F32), axis=1, keepdims=True)
    return total.astype(BF16), two_halves(route)


def added_kernel(keep_ref, sums_ref, sent_ref, *refs, first):
    rows, width = refs[-1].shape[0], keep_ref.shape[1]
    cut = slice(first, first + rows)
    total, route = add_up(keep_ref[cut], sums_ref[cut], sent_ref[cut], ())
    refs[-1][:, :width] = total
    refs[-1][:, width:] = route


def added(keep, sums, sent, first, rows, after):
    whole = pl.BlockSpec(memory_space=pltpu.VMEM)
    return pl.pallas_call(
        functools.partial(added_kernel, first=first),
        in_specs=[whole] * 3 + [pl.BlockSpec(memory_space=pl.ANY)] * len(after),
        out_shape=jax.ShapeDtypeStruct((rows, sent.shape[1]), BF16),
        compiler_params=params(),
        name="added",
    )(keep, sums, sent, *after)


def total_kernel(keep_ref, sums_ref, sent_ref, *refs, count, first):
    pieces = refs[count:]
    most, width = pieces[0].shape[0], keep_ref.shape[1]
    cut = slice(first * most, (first + len(pieces)) * most)
    arrived = [ref[...] for ref in refs[:count]]
    total, route = add_up(keep_ref[cut], sums_ref[cut], sent_ref[cut], arrived)
    for j, ref in enumerate(pieces):
        ref[:, :width] = total[j * most : (j + 1) * most]
        ref[:, width:] = route[j * most : (j + 1) * most]


def totals(keep, sums, sent, arrived, first, count, most):
    return pl.pallas_call(
        functools.partial(total_kernel, count=len(arrived), first=first),
        out_shape=[jax.ShapeDtypeStruct((most, sent.shape[1]), BF16)] * count,
        compiler_params=params(),
        name="totals",
    )(keep, sums, sent, *arrived)


def combine_kernel(ids_ref, own_ids_ref, weights_ref, place_ref, *refs, experts, count):
    came = jnp.concatenate([ref[...] for ref in refs[:count]], axis=0)
    grad_ref, route_ref = refs[count:]
    tokens, width = grad_ref.shape
    weight = jnp.sum(jnp.where(ids_ref[...] < experts, weights_ref[...], 0.0), axis=0, keepdims=True)
    column = jnp.broadcast_to(weight, (tokens, tokens)).T[:, :1]
    pick = place_ref[...].astype(F32).T.astype(BF16)
    taken = jnp.dot(pick, came, preferred_element_type=F32)
    grad_ref[...] = (column * taken[:, :width]).astype(BF16)
    extra = taken[:, width:].T
    total = extra[0:1] + extra[1:2]
    route_ref[...] = jnp.where(own_ids_ref[...] < experts, total, 0.0)


def combine(ids_t, own_ids_t, weights_t, place, came, experts, width):
    tokens = ids_t.shape[1]
    return pl.pallas_call(
        functools.partial(combine_kernel, experts=experts, count=len(came)),
        out_shape=(
            jax.ShapeDtypeStruct((tokens, width), BF16),
            jax.ShapeDtypeStruct(own_ids_t.shape, F32),
        ),
        compiler_params=params(),
        name="combine",
    )(ids_t, own_ids_t, weights_t, place, *came)


def local(tokens, out_grad, expert_ids, route_weights, gate_proj, up_proj, down_proj):
    seq_count = lax.axis_size("seq")
    exp_count = lax.axis_size("exp")
    tok_dev, part = tokens.shape
    top_count = expert_ids.shape[1]
    expert_count = exp_count * gate_proj.shape[0]
    most = max(2, 2 * ((tok_dev + expert_count - 1) // expert_count))
    wg, wu, wd = gate_proj[0], up_proj[0], down_proj[0]
    chips = seq_count // 2
    unit = exp_count // 8

    def of_units(*units):
        return [u * unit + j for u in units for j in range(unit)]

    seq_at = lax.axis_index("seq")
    core = seq_at % 2
    chip = seq_at // 2

    def other_core(value):
        return lax.ppermute(value, "seq", [(s, s ^ 1) for s in range(seq_count)])

    def chip_shift(value, k):
        return lax.ppermute(value, "seq", [(s, (s + 2 * k) % seq_count) for s in range(seq_count)])

    def exp_swap(value, s):
        return lax.ppermute(value, "exp", [(e, e ^ s) for e in range(exp_count)]) if s else value

    def joined(values, axis=0):
        return values[0] if len(values) == 1 else jnp.concatenate(values, axis=axis)

    ids_t = expert_ids.T
    weights_t = route_weights.T
    columns = top_count // seq_count
    own_ids_t = lax.dynamic_slice_in_dim(ids_t, seq_at * columns, columns, 0)

    def from_chips(rows):
        return [chip_shift(rows, k) for k in range(1, chips)]

    came = [None] * exp_count

    def send(pieces, group):
        for s, piece in zip(group, pieces):
            came[s] = exp_swap(piece, s)

    def send_more(group, after):
        send(copied([pieces[s] for s in group], after), group)

    def arrived_of(group):
        return joined([came[s] for s in group])

    near = of_units(0, 1, 2, 4, 5)
    place, pieces = pack(ids_t, tokens, out_grad, expert_count, most)
    send([pieces[s] for s in near], near)
    pairs = [of_units(0), of_units(1, 2), of_units(3, 4, 5), of_units(6)]
    rows = [from_chips(arrived_of(pairs[0]))]
    send_more(of_units(3), rows[0][:1])
    rows.append(from_chips(arrived_of(pairs[1])))
    send_more(of_units(6), [came[of_units(j)[-1]] for j in (3, 4)] + rows[1][:1])
    send_more(of_units(7), [came[of_units(5)[-1]]] + rows[1][:1])
    rows.append(from_chips(arrived_of(pairs[2])))
    rows.append(from_chips(copied([arrived_of(pairs[3])], rows[1][:1])[0]))

    def three(x, dy, j):
        k, other = j // 2, j % 2
        at = (chip - k) % chips * 2 + (1 - core if other else core)

        def block(weight, axis):
            return lax.dynamic_slice_in_dim(weight, at * part, part, axis)

        return [
            jnp.dot(x, block(wg, 0), preferred_element_type=F32),
            jnp.dot(x, block(wu, 0), preferred_element_type=F32),
            lax.dot_general(dy, block(wd, 1), CONTRACT, preferred_element_type=F32),
        ]

    def plus(terms, more):
        return [term + other for term, other in zip(terms, more)]

    own_x, own_dy = joined([v[:, :part] for v in came]), joined([v[:, part:] for v in came])
    end = arrived_of(of_units(7))
    terms = three(own_x, own_dy, 0)
    terms = plus(terms, three(other_core(own_x), other_core(own_dy), 1))
    end_x = from_chips(copied([end[:, :part]], rows[2][:1])[0])
    end_dy = from_chips(copied([end[:, part:]], rows[2][:1] + terms)[0])
    for k in range(1, chips):
        found = {}
        for values, group in zip([values[k - 1] for values in rows], pairs):
            for j, s in enumerate(group):
                found[s] = values[j * most : (j + 1) * most]
        early = [found[s] for s in sorted(found)]
        early_x = joined([value[:, :part] for value in early])
        early_dy = joined([value[:, part:] for value in early])
        last_x, last_dy = end_x[k - 1], end_dy[k - 1]
        terms = plus(terms, three(joined([early_x, last_x]), joined([early_dy, last_dy]), 2 * k))
        other_x = joined([other_core(early_x), other_core(last_x)])
        other_dy = joined([other_core(early_dy), other_core(last_dy)])
        terms = plus(terms, three(other_x, other_dy, 2 * k + 1))
    pre_gate, pre_up, back_grad = terms

    sig = jax.nn.sigmoid(pre_gate)
    active = pre_gate * sig
    grad_gate = (back_grad * pre_up * sig * (1.0 + pre_gate * (1.0 - sig))).astype(BF16)
    grad_up = (back_grad * active).astype(BF16)
    route = jnp.sum(active * pre_up * back_grad, axis=-1)

    def block_grad(at):
        cut = slice(at * part, (at + 1) * part)
        return (
            lax.dot_general(grad_gate, wg[cut], CONTRACT, preferred_element_type=F32)
            + lax.dot_general(grad_up, wu[cut], CONTRACT, preferred_element_type=F32)
        ).astype(BF16)

    block_grads = [block_grad(at) for at in range(seq_count)]
    sums = two_halves(route[:, None])
    others = []
    for k in range(1, chips):
        keep, sent = split(block_grads, sums, k)
        others.append((keep, sums, other_core(sent)))
    order = [(7 * unit, unit), (3 * unit, 4 * unit), (0, 3 * unit)]
    first, count = order[0]
    summed = [added(*values, first * most, count * most, []) for values in others]
    keep, sent = split(block_grads, sums, 0)
    sent = other_core(copied([sent], summed)[0])

    back = [None] * exp_count
    after = []
    for first, count in order:
        if after:
            if not first:
                after = after + [back[-1]]
            summed = [added(*values, first * most, count * most, after) for values in others]
        arrived = [chip_shift(values, k) for k, values in enumerate(summed, 1)]
        pieces = totals(keep, sums, sent, arrived, first, count, most)
        for j, piece in enumerate(pieces):
            back[first + j] = exp_swap(piece, first + j)
        after = list(pieces[:1])

    own_grad, own_route_t = combine(
        ids_t, own_ids_t, weights_t, place, back, expert_count, part
    )
    return own_grad, own_route_t.T


def solution(mesh):
    in_specs = (
        P("exp", "seq"),
        P("exp", "seq"),
        P("exp", None),
        P("exp", None),
        P("exp", None, "seq"),
        P("exp", None, "seq"),
        P("exp", "seq", None),
    )
    out_specs = (P("exp", "seq"), P("exp", "seq"))
    return jax.shard_map(local, mesh=mesh, in_specs=in_specs, out_specs=out_specs, check_vma=False)
```

```python
import functools

import jax
import jax.numpy as jnp
from jax import lax
from jax.experimental import pallas as pl
from jax.experimental.pallas import tpu as pltpu
from jax.sharding import PartitionSpec as P

CONTRACT = (((1,), (1,)), ((), ()))
BF16 = jnp.bfloat16
F32 = jnp.float32
VMEM_BYTES = 8 * 1024 * 1024
EXTRA = 128


def params():
    return pltpu.CompilerParams(vmem_limit_bytes=VMEM_BYTES)


def write_pieces(place, values, refs):
    most = refs[0].shape[0]
    at = 0
    for value in values:
        rows = jnp.dot(place, value, preferred_element_type=F32)
        width = rows.shape[1]
        for s, ref in enumerate(refs):
            ref[:, at : at + width] = rows[s * most : (s + 1) * most].astype(BF16)
        at += width


def pack_kernel(ids_ref, x_ref, dy_ref, place_ref, *pieces, experts, most):
    ids = ids_ref[...]
    tokens = ids.shape[1]
    named = jnp.min(ids, axis=0, keepdims=True)
    hot = (named == lax.broadcasted_iota(jnp.int32, (experts, tokens), 0)).astype(F32)
    rows = lax.broadcasted_iota(jnp.int32, (tokens, tokens), 0)
    cols = lax.broadcasted_iota(jnp.int32, (tokens, tokens), 1)
    before = (rows < cols).astype(F32).astype(BF16)
    earlier = jnp.dot(hot.astype(BF16), before, preferred_element_type=F32)
    rank = jnp.sum(earlier * hot, axis=0, keepdims=True).astype(jnp.int32)
    target = jnp.where(named < experts, (named ^ lax.axis_index("exp")) * most + rank, -1)
    slots = lax.broadcasted_iota(jnp.int32, (experts * most, tokens), 0)
    place = (target == slots).astype(F32).astype(BF16)
    place_ref[...] = place
    write_pieces(place, (x_ref[...], dy_ref[...]), pieces)


def pack(ids_t, x, dy, experts, most):
    tokens, width = x.shape
    place, *pieces = pl.pallas_call(
        functools.partial(pack_kernel, experts=experts, most=most),
        out_shape=[jax.ShapeDtypeStruct((experts * most, tokens), BF16)]
        + [jax.ShapeDtypeStruct((most, 2 * width), BF16)] * experts,
        compiler_params=params(),
        name="pack",
    )(ids_t, x, dy)
    return place, pieces


def copy_kernel(*refs, count, gates):
    for taken, given in zip(refs[:count], refs[count + gates :]):
        given[...] = taken[...]


def copied(values, after):
    whole = pl.BlockSpec(memory_space=pltpu.VMEM)
    return pl.pallas_call(
        functools.partial(copy_kernel, count=len(values), gates=len(after)),
        in_specs=[whole] * len(values) + [pl.BlockSpec(memory_space=pl.ANY)] * len(after),
        out_shape=[jax.ShapeDtypeStruct(value.shape, value.dtype) for value in values],
        compiler_params=params(),
        name="copied",
    )(*values, *after)


def split_kernel(*refs, count, shift):
    taken, sums_ref, keep_ref, sent_ref = refs[:count], *refs[count:]
    seq_at = lax.axis_index("seq")
    core = lax.rem(seq_at, 2)
    there = lax.rem(lax.div(seq_at, 2) + shift, count // 2) * 2
    width = keep_ref.shape[1]
    sent_ref[:, width:] = sums_ref[...]
    for j in range(count):

        @pl.when(there + core == j)
        def _(j=j):
            keep_ref[...] = taken[j][...]

        @pl.when(there + 1 - core == j)
        def _(j=j):
            sent_ref[:, :width] = taken[j][...]


def split(taken, sums, shift):
    rows, width = taken[0].shape
    return pl.pallas_call(
        functools.partial(split_kernel, count=len(taken), shift=shift),
        out_shape=[
            jax.ShapeDtypeStruct((rows, width), BF16),
            jax.ShapeDtypeStruct((rows, width + EXTRA), BF16),
        ],
        compiler_params=params(),
        name="split",
    )(*taken, sums)


def two_halves(value):
    high = value.astype(BF16).astype(F32)
    lane = lax.broadcasted_iota(jnp.int32, (value.shape[0], EXTRA), 1)
    return jnp.where(lane == 0, high, jnp.where(lane == 1, value - high, 0.0)).astype(BF16)


def add_up(keep, sums, sent, arrived):
    width = keep.shape[1]
    total = keep.astype(F32)
    route = jnp.sum(sums.astype(F32), axis=1, keepdims=True)
    for message in (sent, *arrived):
        total += message[:, :width].astype(F32)
        route += jnp.sum(message[:, width:].astype(F32), axis=1, keepdims=True)
    return total.astype(BF16), two_halves(route)


def added_kernel(keep_ref, sums_ref, sent_ref, *refs, first):
    rows, width = refs[-1].shape[0], keep_ref.shape[1]
    cut = slice(first, first + rows)
    total, route = add_up(keep_ref[cut], sums_ref[cut], sent_ref[cut], ())
    refs[-1][:, :width] = total
    refs[-1][:, width:] = route


def added(keep, sums, sent, first, rows, after):
    whole = pl.BlockSpec(memory_space=pltpu.VMEM)
    return pl.pallas_call(
        functools.partial(added_kernel, first=first),
        in_specs=[whole] * 3 + [pl.BlockSpec(memory_space=pl.ANY)] * len(after),
        out_shape=jax.ShapeDtypeStruct((rows, sent.shape[1]), BF16),
        compiler_params=params(),
        name="added",
    )(keep, sums, sent, *after)


def total_kernel(keep_ref, sums_ref, sent_ref, *refs, count, first):
    pieces = refs[count:]
    most, width = pieces[0].shape[0], keep_ref.shape[1]
    cut = slice(first * most, (first + len(pieces)) * most)
    arrived = [ref[...] for ref in refs[:count]]
    total, route = add_up(keep_ref[cut], sums_ref[cut], sent_ref[cut], arrived)
    for j, ref in enumerate(pieces):
        ref[:, :width] = total[j * most : (j + 1) * most]
        ref[:, width:] = route[j * most : (j + 1) * most]


def totals(keep, sums, sent, arrived, first, count, most):
    return pl.pallas_call(
        functools.partial(total_kernel, count=len(arrived), first=first),
        out_shape=[jax.ShapeDtypeStruct((most, sent.shape[1]), BF16)] * count,
        compiler_params=params(),
        name="totals",
    )(keep, sums, sent, *arrived)


def combine_kernel(ids_ref, own_ids_ref, weights_ref, place_ref, *refs, experts, count):
    came = jnp.concatenate([ref[...] for ref in refs[:count]], axis=0)
    grad_ref, route_ref = refs[count:]
    tokens, width = grad_ref.shape
    weight = jnp.sum(jnp.where(ids_ref[...] < experts, weights_ref[...], 0.0), axis=0, keepdims=True)
    column = jnp.broadcast_to(weight, (tokens, tokens)).T[:, :1]
    pick = place_ref[...].astype(F32).T.astype(BF16)
    taken = jnp.dot(pick, came, preferred_element_type=F32)
    grad_ref[...] = (column * taken[:, :width]).astype(BF16)
    extra = taken[:, width:].T
    total = extra[0:1] + extra[1:2]
    route_ref[...] = jnp.where(own_ids_ref[...] < experts, total, 0.0)


def combine(ids_t, own_ids_t, weights_t, place, came, experts, width):
    tokens = ids_t.shape[1]
    return pl.pallas_call(
        functools.partial(combine_kernel, experts=experts, count=len(came)),
        out_shape=(
            jax.ShapeDtypeStruct((tokens, width), BF16),
            jax.ShapeDtypeStruct(own_ids_t.shape, F32),
        ),
        compiler_params=params(),
        name="combine",
    )(ids_t, own_ids_t, weights_t, place, *came)


def local(tokens, out_grad, expert_ids, route_weights, gate_proj, up_proj, down_proj):
    seq_count = lax.axis_size("seq")
    exp_count = lax.axis_size("exp")
    tok_dev, part = tokens.shape
    top_count = expert_ids.shape[1]
    expert_count = exp_count * gate_proj.shape[0]
    most = max(2, 2 * ((tok_dev + expert_count - 1) // expert_count))
    wg, wu, wd = gate_proj[0], up_proj[0], down_proj[0]
    chips = seq_count // 2
    unit = exp_count // 8

    def of_units(*units):
        return [u * unit + j for u in units for j in range(unit)]

    seq_at = lax.axis_index("seq")
    core = seq_at % 2
    chip = seq_at // 2

    def other_core(value):
        return lax.ppermute(value, "seq", [(s, s ^ 1) for s in range(seq_count)])

    def chip_shift(value, k):
        return lax.ppermute(value, "seq", [(s, (s + 2 * k) % seq_count) for s in range(seq_count)])

    def exp_swap(value, s):
        return lax.ppermute(value, "exp", [(e, e ^ s) for e in range(exp_count)]) if s else value

    def joined(values, axis=0):
        return values[0] if len(values) == 1 else jnp.concatenate(values, axis=axis)

    ids_t = expert_ids.T
    weights_t = route_weights.T
    columns = top_count // seq_count
    own_ids_t = lax.dynamic_slice_in_dim(ids_t, seq_at * columns, columns, 0)

    def from_chips(rows):
        return [chip_shift(rows, k) for k in range(1, chips)]

    came = [None] * exp_count

    def send(pieces, group):
        for s, piece in zip(group, pieces):
            came[s] = exp_swap(piece, s)

    def send_more(group, after):
        send(copied([pieces[s] for s in group], after), group)

    def arrived_of(group):
        return joined([came[s] for s in group])

    near = of_units(0, 1, 2, 4, 5)
    place, pieces = pack(ids_t, tokens, out_grad, expert_count, most)
    send([pieces[s] for s in near], near)
    pairs = [of_units(0), of_units(1, 2), of_units(3, 4, 5), of_units(6)]
    rows = [from_chips(arrived_of(pairs[0]))]
    send_more(of_units(3), rows[0][:1])
    rows.append(from_chips(arrived_of(pairs[1])))
    send_more(of_units(6), [came[of_units(j)[-1]] for j in (3, 4)] + rows[1][:1])
    send_more(of_units(7), [came[of_units(5)[-1]]] + rows[1][:1])
    rows.append(from_chips(arrived_of(pairs[2])))
    rows.append(from_chips(copied([arrived_of(pairs[3])], rows[1][:1])[0]))

    def three(x, dy, j):
        k, other = j // 2, j % 2
        at = (chip - k) % chips * 2 + (1 - core if other else core)

        def block(weight, axis):
            return lax.dynamic_slice_in_dim(weight, at * part, part, axis)

        return [
            jnp.dot(x, block(wg, 0), preferred_element_type=F32),
            jnp.dot(x, block(wu, 0), preferred_element_type=F32),
            lax.dot_general(dy, block(wd, 1), CONTRACT, preferred_element_type=F32),
        ]

    def plus(terms, more):
        return [term + other for term, other in zip(terms, more)]

    own_x, own_dy = joined([v[:, :part] for v in came]), joined([v[:, part:] for v in came])
    end = arrived_of(of_units(7))
    terms = three(own_x, own_dy, 0)
    terms = plus(terms, three(other_core(own_x), other_core(own_dy), 1))
    end_x, end_dy = copied([end[:, :part], end[:, part:]], rows[2][:1])
    end_x, end_dy = from_chips(end_x), from_chips(end_dy)
    for k in range(1, chips):
        found = {}
        for values, group in zip([values[k - 1] for values in rows], pairs):
            for j, s in enumerate(group):
                found[s] = values[j * most : (j + 1) * most]
        early = [found[s] for s in sorted(found)]
        early_x = joined([value[:, :part] for value in early])
        early_dy = joined([value[:, part:] for value in early])
        last_x, last_dy = end_x[k - 1], end_dy[k - 1]
        terms = plus(terms, three(joined([early_x, last_x]), joined([early_dy, last_dy]), 2 * k))
        other_x = joined([other_core(early_x), other_core(last_x)])
        other_dy = joined([other_core(early_dy), other_core(last_dy)])
        terms = plus(terms, three(other_x, other_dy, 2 * k + 1))
    pre_gate, pre_up, back_grad = terms

    sig = jax.nn.sigmoid(pre_gate)
    active = pre_gate * sig
    grad_gate = (back_grad * pre_up * sig * (1.0 + pre_gate * (1.0 - sig))).astype(BF16)
    grad_up = (back_grad * active).astype(BF16)
    route = jnp.sum(active * pre_up * back_grad, axis=-1)

    def block_grad(at):
        cut = slice(at * part, (at + 1) * part)
        return (
            lax.dot_general(grad_gate, wg[cut], CONTRACT, preferred_element_type=F32)
            + lax.dot_general(grad_up, wu[cut], CONTRACT, preferred_element_type=F32)
        ).astype(BF16)

    block_grads = [block_grad(at) for at in range(seq_count)]
    sums = two_halves(route[:, None])
    others = []
    for k in range(1, chips):
        keep, sent = split(block_grads, sums, k)
        others.append((keep, sums, other_core(sent)))
    order = [(7 * unit, unit), (4 * unit, 3 * unit), (0, 4 * unit)]
    first, count = order[0]
    summed = [added(*values, first * most, count * most, []) for values in others]
    keep, sent = split(block_grads, sums, 0)
    sent = other_core(copied([sent], summed)[0])

    back = [None] * exp_count
    after = []
    for first, count in order:
        if not first:
            after = [pieces[0], back[-1]]
        summed = [added(*values, first * most, count * most, after) for values in others]
        arrived = [chip_shift(values, k) for k, values in enumerate(summed, 1)]
        pieces = totals(keep, sums, sent, arrived, first, count, most)
        for j, piece in enumerate(pieces):
            back[first + j] = exp_swap(piece, first + j)

    own_grad, own_route_t = combine(
        ids_t, own_ids_t, weights_t, place, back, expert_count, part
    )
    return own_grad, own_route_t.T


def solution(mesh):
    in_specs = (
        P("exp", "seq"),
        P("exp", "seq"),
        P("exp", None),
        P("exp", None),
        P("exp", None, "seq"),
        P("exp", None, "seq"),
        P("exp", "seq", None),
    )
    out_specs = (P("exp", "seq"), P("exp", "seq"))
    return jax.shard_map(local, mesh=mesh, in_specs=in_specs, out_specs=out_specs, check_vma=False)
```

```python
import functools

import jax
import jax.numpy as jnp
from jax import lax
from jax.experimental import pallas as pl
from jax.experimental.pallas import tpu as pltpu
from jax.sharding import PartitionSpec as P

CONTRACT = (((1,), (1,)), ((), ()))
BF16 = jnp.bfloat16
F32 = jnp.float32
VMEM_BYTES = 8 * 1024 * 1024
EXTRA = 128


def params():
    return pltpu.CompilerParams(vmem_limit_bytes=VMEM_BYTES)


def write_pieces(place, values, refs):
    most = refs[0].shape[0]
    at = 0
    for value in values:
        rows = jnp.dot(place, value, preferred_element_type=F32)
        width = rows.shape[1]
        for s, ref in enumerate(refs):
            ref[:, at : at + width] = rows[s * most : (s + 1) * most].astype(BF16)
        at += width


def pack_kernel(ids_ref, x_ref, dy_ref, place_ref, *pieces, experts, most):
    ids = ids_ref[...]
    tokens = ids.shape[1]
    named = jnp.min(ids, axis=0, keepdims=True)
    hot = (named == lax.broadcasted_iota(jnp.int32, (experts, tokens), 0)).astype(F32)
    rows = lax.broadcasted_iota(jnp.int32, (tokens, tokens), 0)
    cols = lax.broadcasted_iota(jnp.int32, (tokens, tokens), 1)
    before = (rows < cols).astype(F32).astype(BF16)
    earlier = jnp.dot(hot.astype(BF16), before, preferred_element_type=F32)
    rank = jnp.sum(earlier * hot, axis=0, keepdims=True).astype(jnp.int32)
    target = jnp.where(named < experts, (named ^ lax.axis_index("exp")) * most + rank, -1)
    slots = lax.broadcasted_iota(jnp.int32, (experts * most, tokens), 0)
    place = (target == slots).astype(F32).astype(BF16)
    place_ref[...] = place
    write_pieces(place, (x_ref[...], dy_ref[...]), pieces)


def pack(ids_t, x, dy, experts, most):
    tokens, width = x.shape
    place, *pieces = pl.pallas_call(
        functools.partial(pack_kernel, experts=experts, most=most),
        out_shape=[jax.ShapeDtypeStruct((experts * most, tokens), BF16)]
        + [jax.ShapeDtypeStruct((most, 2 * width), BF16)] * experts,
        compiler_params=params(),
        name="pack",
    )(ids_t, x, dy)
    return place, pieces


def copy_kernel(*refs, count, gates):
    for taken, given in zip(refs[:count], refs[count + gates :]):
        given[...] = taken[...]


def copied(values, after):
    whole = pl.BlockSpec(memory_space=pltpu.VMEM)
    return pl.pallas_call(
        functools.partial(copy_kernel, count=len(values), gates=len(after)),
        in_specs=[whole] * len(values) + [pl.BlockSpec(memory_space=pl.ANY)] * len(after),
        out_shape=[jax.ShapeDtypeStruct(value.shape, value.dtype) for value in values],
        compiler_params=params(),
        name="copied",
    )(*values, *after)


def split_kernel(*refs, count, shift):
    taken, sums_ref, keep_ref, sent_ref = refs[:count], *refs[count:]
    seq_at = lax.axis_index("seq")
    core = lax.rem(seq_at, 2)
    there = lax.rem(lax.div(seq_at, 2) + shift, count // 2) * 2
    width = keep_ref.shape[1]
    sent_ref[:, width:] = sums_ref[...]
    for j in range(count):

        @pl.when(there + core == j)
        def _(j=j):
            keep_ref[...] = taken[j][...]

        @pl.when(there + 1 - core == j)
        def _(j=j):
            sent_ref[:, :width] = taken[j][...]


def split(taken, sums, shift):
    rows, width = taken[0].shape
    return pl.pallas_call(
        functools.partial(split_kernel, count=len(taken), shift=shift),
        out_shape=[
            jax.ShapeDtypeStruct((rows, width), BF16),
            jax.ShapeDtypeStruct((rows, width + EXTRA), BF16),
        ],
        compiler_params=params(),
        name="split",
    )(*taken, sums)


def two_halves(value):
    high = value.astype(BF16).astype(F32)
    lane = lax.broadcasted_iota(jnp.int32, (value.shape[0], EXTRA), 1)
    return jnp.where(lane == 0, high, jnp.where(lane == 1, value - high, 0.0)).astype(BF16)


def add_up(keep, sums, sent, arrived):
    width = keep.shape[1]
    total = keep.astype(F32)
    route = jnp.sum(sums.astype(F32), axis=1, keepdims=True)
    for message in (sent, *arrived):
        total += message[:, :width].astype(F32)
        route += jnp.sum(message[:, width:].astype(F32), axis=1, keepdims=True)
    return total.astype(BF16), two_halves(route)


def added_kernel(keep_ref, sums_ref, sent_ref, *refs, first):
    rows, width = refs[-1].shape[0], keep_ref.shape[1]
    cut = slice(first, first + rows)
    total, route = add_up(keep_ref[cut], sums_ref[cut], sent_ref[cut], ())
    refs[-1][:, :width] = total
    refs[-1][:, width:] = route


def added(keep, sums, sent, first, rows, after):
    whole = pl.BlockSpec(memory_space=pltpu.VMEM)
    return pl.pallas_call(
        functools.partial(added_kernel, first=first),
        in_specs=[whole] * 3 + [pl.BlockSpec(memory_space=pl.ANY)] * len(after),
        out_shape=jax.ShapeDtypeStruct((rows, sent.shape[1]), BF16),
        compiler_params=params(),
        name="added",
    )(keep, sums, sent, *after)


def total_kernel(keep_ref, sums_ref, sent_ref, *refs, count, first):
    pieces = refs[count:]
    most, width = pieces[0].shape[0], keep_ref.shape[1]
    cut = slice(first * most, (first + len(pieces)) * most)
    arrived = [ref[...] for ref in refs[:count]]
    total, route = add_up(keep_ref[cut], sums_ref[cut], sent_ref[cut], arrived)
    for j, ref in enumerate(pieces):
        ref[:, :width] = total[j * most : (j + 1) * most]
        ref[:, width:] = route[j * most : (j + 1) * most]


def totals(keep, sums, sent, arrived, first, count, most):
    return pl.pallas_call(
        functools.partial(total_kernel, count=len(arrived), first=first),
        out_shape=[jax.ShapeDtypeStruct((most, sent.shape[1]), BF16)] * count,
        compiler_params=params(),
        name="totals",
    )(keep, sums, sent, *arrived)


def combine_kernel(ids_ref, own_ids_ref, weights_ref, place_ref, *refs, experts, count):
    came = jnp.concatenate([ref[...] for ref in refs[:count]], axis=0)
    grad_ref, route_ref = refs[count:]
    tokens, width = grad_ref.shape
    weight = jnp.sum(jnp.where(ids_ref[...] < experts, weights_ref[...], 0.0), axis=0, keepdims=True)
    column = jnp.broadcast_to(weight, (tokens, tokens)).T[:, :1]
    pick = place_ref[...].astype(F32).T.astype(BF16)
    taken = jnp.dot(pick, came, preferred_element_type=F32)
    grad_ref[...] = (column * taken[:, :width]).astype(BF16)
    extra = taken[:, width:].T
    total = extra[0:1] + extra[1:2]
    route_ref[...] = jnp.where(own_ids_ref[...] < experts, total, 0.0)


def combine(ids_t, own_ids_t, weights_t, place, came, experts, width):
    tokens = ids_t.shape[1]
    return pl.pallas_call(
        functools.partial(combine_kernel, experts=experts, count=len(came)),
        out_shape=(
            jax.ShapeDtypeStruct((tokens, width), BF16),
            jax.ShapeDtypeStruct(own_ids_t.shape, F32),
        ),
        compiler_params=params(),
        name="combine",
    )(ids_t, own_ids_t, weights_t, place, *came)


def local(tokens, out_grad, expert_ids, route_weights, gate_proj, up_proj, down_proj):
    seq_count = lax.axis_size("seq")
    exp_count = lax.axis_size("exp")
    tok_dev, part = tokens.shape
    top_count = expert_ids.shape[1]
    expert_count = exp_count * gate_proj.shape[0]
    most = max(2, 2 * ((tok_dev + expert_count - 1) // expert_count))
    wg, wu, wd = gate_proj[0], up_proj[0], down_proj[0]
    chips = seq_count // 2
    unit = exp_count // 8

    def of_units(*units):
        return [u * unit + j for u in units for j in range(unit)]

    seq_at = lax.axis_index("seq")
    core = seq_at % 2
    chip = seq_at // 2

    def other_core(value):
        return lax.ppermute(value, "seq", [(s, s ^ 1) for s in range(seq_count)])

    def chip_shift(value, k):
        return lax.ppermute(value, "seq", [(s, (s + 2 * k) % seq_count) for s in range(seq_count)])

    def exp_swap(value, s):
        return lax.ppermute(value, "exp", [(e, e ^ s) for e in range(exp_count)]) if s else value

    def joined(values, axis=0):
        return values[0] if len(values) == 1 else jnp.concatenate(values, axis=axis)

    ids_t = expert_ids.T
    weights_t = route_weights.T
    columns = top_count // seq_count
    own_ids_t = lax.dynamic_slice_in_dim(ids_t, seq_at * columns, columns, 0)

    def from_chips(rows):
        return [chip_shift(rows, k) for k in range(1, chips)]

    came = [None] * exp_count

    def send(pieces, group):
        for s, piece in zip(group, pieces):
            came[s] = exp_swap(piece, s)

    def send_more(group, after):
        send(copied([pieces[s] for s in group], after), group)

    def arrived_of(group):
        return joined([came[s] for s in group])

    near = of_units(0, 1, 2, 4, 5)
    place, pieces = pack(ids_t, tokens, out_grad, expert_count, most)
    send([pieces[s] for s in near], near)
    pairs = [of_units(0), of_units(1, 2), of_units(3, 4, 5), of_units(6)]
    rows = [from_chips(arrived_of(pairs[0]))]
    send_more(of_units(3), rows[0][:1])
    rows.append(from_chips(arrived_of(pairs[1])))
    send_more(of_units(6), [came[of_units(j)[-1]] for j in (3, 4)] + rows[1][:1])
    send_more(of_units(7), [came[of_units(5)[-1]]] + rows[1][:1])
    rows.append(from_chips(arrived_of(pairs[2])))
    rows.append(from_chips(copied([arrived_of(pairs[3])], rows[1][:1])[0]))

    def three(x, dy, j):
        k, other = j // 2, j % 2
        at = (chip - k) % chips * 2 + (1 - core if other else core)

        def block(weight, axis):
            return lax.dynamic_slice_in_dim(weight, at * part, part, axis)

        return [
            jnp.dot(x, block(wg, 0), preferred_element_type=F32),
            jnp.dot(x, block(wu, 0), preferred_element_type=F32),
            lax.dot_general(dy, block(wd, 1), CONTRACT, preferred_element_type=F32),
        ]

    def plus(terms, more):
        return [term + other for term, other in zip(terms, more)]

    own_x, own_dy = joined([v[:, :part] for v in came]), joined([v[:, part:] for v in came])
    end = arrived_of(of_units(7))
    terms = three(own_x, own_dy, 0)
    terms = plus(terms, three(other_core(own_x), other_core(own_dy), 1))
    end_x, end_dy = copied([end[:, :part], end[:, part:]], rows[2][:1])
    end_x, end_dy = from_chips(end_x), from_chips(end_dy)
    for k in range(1, chips):
        found = {}
        for values, group in zip([values[k - 1] for values in rows], pairs):
            for j, s in enumerate(group):
                found[s] = values[j * most : (j + 1) * most]
        early = [found[s] for s in sorted(found)]
        early_x = joined([value[:, :part] for value in early])
        early_dy = joined([value[:, part:] for value in early])
        last_x, last_dy = end_x[k - 1], end_dy[k - 1]
        terms = plus(terms, three(joined([early_x, last_x]), joined([early_dy, last_dy]), 2 * k))
        other_x = joined([other_core(early_x), other_core(last_x)])
        other_dy = joined([other_core(early_dy), other_core(last_dy)])
        terms = plus(terms, three(other_x, other_dy, 2 * k + 1))
    pre_gate, pre_up, back_grad = terms

    sig = jax.nn.sigmoid(pre_gate)
    active = pre_gate * sig
    grad_gate = (back_grad * pre_up * sig * (1.0 + pre_gate * (1.0 - sig))).astype(BF16)
    grad_up = (back_grad * active).astype(BF16)
    route = jnp.sum(active * pre_up * back_grad, axis=-1)

    def block_grad(at):
        cut = slice(at * part, (at + 1) * part)
        return (
            lax.dot_general(grad_gate, wg[cut], CONTRACT, preferred_element_type=F32)
            + lax.dot_general(grad_up, wu[cut], CONTRACT, preferred_element_type=F32)
        ).astype(BF16)

    block_grads = [block_grad(at) for at in range(seq_count)]
    sums = two_halves(route[:, None])
    others = []
    for k in range(1, chips):
        keep, sent = split(block_grads, sums, k)
        others.append((keep, sums, other_core(sent)))
    order = [(7 * unit, unit), (4 * unit, 3 * unit), (0, 4 * unit)]
    first, count = order[0]
    summed = [added(*values, first * most, count * most, []) for values in others]
    keep, sent = split(block_grads, sums, 0)
    sent = other_core(copied([sent], summed)[0])

    back = [None] * exp_count
    after = []
    for first, count in order:
        if not first:
            after.append(back[-1])
        summed = [added(*values, first * most, count * most, after) for values in others]
        arrived = [chip_shift(values, k) for k, values in enumerate(summed, 1)]
        pieces = totals(keep, sums, sent, arrived, first, count, most)
        for j, piece in enumerate(pieces):
            back[first + j] = exp_swap(piece, first + j)
        after = [pieces[0]]

    own_grad, own_route_t = combine(
        ids_t, own_ids_t, weights_t, place, back, expert_count, part
    )
    return own_grad, own_route_t.T


def solution(mesh):
    in_specs = (
        P("exp", "seq"),
        P("exp", "seq"),
        P("exp", None),
        P("exp", None),
        P("exp", None, "seq"),
        P("exp", None, "seq"),
        P("exp", "seq", None),
    )
    out_specs = (P("exp", "seq"), P("exp", "seq"))
    return jax.shard_map(local, mesh=mesh, in_specs=in_specs, out_specs=out_specs, check_vma=False)
```

```python
import functools

import jax
import jax.numpy as jnp
from jax import lax
from jax.experimental import pallas as pl
from jax.experimental.pallas import tpu as pltpu
from jax.sharding import PartitionSpec as P

CONTRACT = (((1,), (1,)), ((), ()))
BF16 = jnp.bfloat16
F32 = jnp.float32
VMEM_BYTES = 8 * 1024 * 1024
EXTRA = 128


def params():
    return pltpu.CompilerParams(vmem_limit_bytes=VMEM_BYTES)


def write_pieces(place, values, refs):
    most = refs[0].shape[0]
    at = 0
    for value in values:
        rows = jnp.dot(place, value, preferred_element_type=F32)
        width = rows.shape[1]
        for s, ref in enumerate(refs):
            ref[:, at : at + width] = rows[s * most : (s + 1) * most].astype(BF16)
        at += width


def pack_kernel(ids_ref, x_ref, dy_ref, place_ref, *pieces, experts, most):
    ids = ids_ref[...]
    tokens = ids.shape[1]
    named = jnp.min(ids, axis=0, keepdims=True)
    hot = (named == lax.broadcasted_iota(jnp.int32, (experts, tokens), 0)).astype(F32)
    rows = lax.broadcasted_iota(jnp.int32, (tokens, tokens), 0)
    cols = lax.broadcasted_iota(jnp.int32, (tokens, tokens), 1)
    before = (rows < cols).astype(F32).astype(BF16)
    earlier = jnp.dot(hot.astype(BF16), before, preferred_element_type=F32)
    rank = jnp.sum(earlier * hot, axis=0, keepdims=True).astype(jnp.int32)
    target = jnp.where(named < experts, (named ^ lax.axis_index("exp")) * most + rank, -1)
    slots = lax.broadcasted_iota(jnp.int32, (experts * most, tokens), 0)
    place = (target == slots).astype(F32).astype(BF16)
    place_ref[...] = place
    write_pieces(place, (x_ref[...], dy_ref[...]), pieces)


def pack(ids_t, x, dy, experts, most):
    tokens, width = x.shape
    place, *pieces = pl.pallas_call(
        functools.partial(pack_kernel, experts=experts, most=most),
        out_shape=[jax.ShapeDtypeStruct((experts * most, tokens), BF16)]
        + [jax.ShapeDtypeStruct((most, 2 * width), BF16)] * experts,
        compiler_params=params(),
        name="pack",
    )(ids_t, x, dy)
    return place, pieces


def copy_kernel(*refs, count, gates):
    for taken, given in zip(refs[:count], refs[count + gates :]):
        given[...] = taken[...]


def copied(values, after):
    whole = pl.BlockSpec(memory_space=pltpu.VMEM)
    return pl.pallas_call(
        functools.partial(copy_kernel, count=len(values), gates=len(after)),
        in_specs=[whole] * len(values) + [pl.BlockSpec(memory_space=pl.ANY)] * len(after),
        out_shape=[jax.ShapeDtypeStruct(value.shape, value.dtype) for value in values],
        compiler_params=params(),
        name="copied",
    )(*values, *after)


def split_kernel(*refs, count, shift):
    taken, sums_ref, keep_ref, sent_ref = refs[:count], *refs[count:]
    seq_at = lax.axis_index("seq")
    core = lax.rem(seq_at, 2)
    there = lax.rem(lax.div(seq_at, 2) + shift, count // 2) * 2
    width = keep_ref.shape[1]
    sent_ref[:, width:] = sums_ref[...]
    for j in range(count):

        @pl.when(there + core == j)
        def _(j=j):
            keep_ref[...] = taken[j][...]

        @pl.when(there + 1 - core == j)
        def _(j=j):
            sent_ref[:, :width] = taken[j][...]


def split(taken, sums, shift):
    rows, width = taken[0].shape
    return pl.pallas_call(
        functools.partial(split_kernel, count=len(taken), shift=shift),
        out_shape=[
            jax.ShapeDtypeStruct((rows, width), BF16),
            jax.ShapeDtypeStruct((rows, width + EXTRA), BF16),
        ],
        compiler_params=params(),
        name="split",
    )(*taken, sums)


def two_halves(value):
    high = value.astype(BF16).astype(F32)
    lane = lax.broadcasted_iota(jnp.int32, (value.shape[0], EXTRA), 1)
    return jnp.where(lane == 0, high, jnp.where(lane == 1, value - high, 0.0)).astype(BF16)


def add_up(keep, sums, sent, arrived):
    width = keep.shape[1]
    total = keep.astype(F32)
    route = jnp.sum(sums.astype(F32), axis=1, keepdims=True)
    for message in (sent, *arrived):
        total += message[:, :width].astype(F32)
        route += jnp.sum(message[:, width:].astype(F32), axis=1, keepdims=True)
    return total.astype(BF16), two_halves(route)


def added_kernel(keep_ref, sums_ref, sent_ref, *refs, first):
    rows, width = refs[-1].shape[0], keep_ref.shape[1]
    cut = slice(first, first + rows)
    total, route = add_up(keep_ref[cut], sums_ref[cut], sent_ref[cut], ())
    refs[-1][:, :width] = total
    refs[-1][:, width:] = route


def added(keep, sums, sent, first, rows, after):
    whole = pl.BlockSpec(memory_space=pltpu.VMEM)
    return pl.pallas_call(
        functools.partial(added_kernel, first=first),
        in_specs=[whole] * 3 + [pl.BlockSpec(memory_space=pl.ANY)] * len(after),
        out_shape=jax.ShapeDtypeStruct((rows, sent.shape[1]), BF16),
        compiler_params=params(),
        name="added",
    )(keep, sums, sent, *after)


def total_kernel(keep_ref, sums_ref, sent_ref, *refs, count, first):
    pieces = refs[count:]
    most, width = pieces[0].shape[0], keep_ref.shape[1]
    cut = slice(first * most, (first + len(pieces)) * most)
    arrived = [ref[...] for ref in refs[:count]]
    total, route = add_up(keep_ref[cut], sums_ref[cut], sent_ref[cut], arrived)
    for j, ref in enumerate(pieces):
        ref[:, :width] = total[j * most : (j + 1) * most]
        ref[:, width:] = route[j * most : (j + 1) * most]


def totals(keep, sums, sent, arrived, first, count, most):
    return pl.pallas_call(
        functools.partial(total_kernel, count=len(arrived), first=first),
        out_shape=[jax.ShapeDtypeStruct((most, sent.shape[1]), BF16)] * count,
        compiler_params=params(),
        name="totals",
    )(keep, sums, sent, *arrived)


def combine_kernel(ids_ref, own_ids_ref, weights_ref, place_ref, *refs, experts, count):
    came = jnp.concatenate([ref[...] for ref in refs[:count]], axis=0)
    grad_ref, route_ref = refs[count:]
    tokens, width = grad_ref.shape
    weight = jnp.sum(jnp.where(ids_ref[...] < experts, weights_ref[...], 0.0), axis=0, keepdims=True)
    column = jnp.broadcast_to(weight, (tokens, tokens)).T[:, :1]
    pick = place_ref[...].astype(F32).T.astype(BF16)
    taken = jnp.dot(pick, came, preferred_element_type=F32)
    grad_ref[...] = (column * taken[:, :width]).astype(BF16)
    extra = taken[:, width:].T
    total = extra[0:1] + extra[1:2]
    route_ref[...] = jnp.where(own_ids_ref[...] < experts, total, 0.0)


def combine(ids_t, own_ids_t, weights_t, place, came, experts, width):
    tokens = ids_t.shape[1]
    return pl.pallas_call(
        functools.partial(combine_kernel, experts=experts, count=len(came)),
        out_shape=(
            jax.ShapeDtypeStruct((tokens, width), BF16),
            jax.ShapeDtypeStruct(own_ids_t.shape, F32),
        ),
        compiler_params=params(),
        name="combine",
    )(ids_t, own_ids_t, weights_t, place, *came)


def local(tokens, out_grad, expert_ids, route_weights, gate_proj, up_proj, down_proj):
    seq_count = lax.axis_size("seq")
    exp_count = lax.axis_size("exp")
    tok_dev, part = tokens.shape
    top_count = expert_ids.shape[1]
    expert_count = exp_count * gate_proj.shape[0]
    most = max(2, 2 * ((tok_dev + expert_count - 1) // expert_count))
    wg, wu, wd = gate_proj[0], up_proj[0], down_proj[0]
    chips = seq_count // 2
    unit = exp_count // 8

    def of_units(*units):
        return [u * unit + j for u in units for j in range(unit)]

    seq_at = lax.axis_index("seq")
    core = seq_at % 2
    chip = seq_at // 2

    def other_core(value):
        return lax.ppermute(value, "seq", [(s, s ^ 1) for s in range(seq_count)])

    def chip_shift(value, k):
        return lax.ppermute(value, "seq", [(s, (s + 2 * k) % seq_count) for s in range(seq_count)])

    def exp_swap(value, s):
        return lax.ppermute(value, "exp", [(e, e ^ s) for e in range(exp_count)]) if s else value

    def joined(values, axis=0):
        return values[0] if len(values) == 1 else jnp.concatenate(values, axis=axis)

    ids_t = expert_ids.T
    weights_t = route_weights.T
    columns = top_count // seq_count
    own_ids_t = lax.dynamic_slice_in_dim(ids_t, seq_at * columns, columns, 0)

    def from_chips(rows):
        return [chip_shift(rows, k) for k in range(1, chips)]

    came = [None] * exp_count

    def send(pieces, group):
        for s, piece in zip(group, pieces):
            came[s] = exp_swap(piece, s)

    def send_more(group, after):
        send(copied([pieces[s] for s in group], after), group)

    def arrived_of(group):
        return joined([came[s] for s in group])

    near = of_units(0, 1, 2, 4, 5)
    place, pieces = pack(ids_t, tokens, out_grad, expert_count, most)
    send([pieces[s] for s in near], near)
    pairs = [of_units(0), of_units(1, 2), of_units(3, 4, 5), of_units(6)]
    rows = [from_chips(arrived_of(pairs[0]))]
    send_more(of_units(3), rows[0][:1])
    rows.append(from_chips(arrived_of(pairs[1])))
    send_more(of_units(6), [came[of_units(j)[-1]] for j in (3, 4)] + rows[1][:1])
    send_more(of_units(7), [came[of_units(5)[-1]]] + rows[1][:1])
    rows.append(from_chips(arrived_of(pairs[2])))
    rows.append(from_chips(copied([arrived_of(pairs[3])], rows[1][:1])[0]))

    def three(x, dy, j):
        k, other = j // 2, j % 2
        at = (chip - k) % chips * 2 + (1 - core if other else core)

        def block(weight, axis):
            return lax.dynamic_slice_in_dim(weight, at * part, part, axis)

        return [
            jnp.dot(x, block(wg, 0), preferred_element_type=F32),
            jnp.dot(x, block(wu, 0), preferred_element_type=F32),
            lax.dot_general(dy, block(wd, 1), CONTRACT, preferred_element_type=F32),
        ]

    def plus(terms, more):
        return [term + other for term, other in zip(terms, more)]

    own_x, own_dy = joined([v[:, :part] for v in came]), joined([v[:, part:] for v in came])
    end = arrived_of(of_units(7))
    terms = three(own_x, own_dy, 0)
    terms = plus(terms, three(other_core(own_x), other_core(own_dy), 1))
    end_x, end_dy = copied([end[:, :part], end[:, part:]], rows[2][:1])
    end_x, end_dy = from_chips(end_x), from_chips(end_dy)
    for k in range(1, chips):
        found = {}
        for values, group in zip([values[k - 1] for values in rows], pairs):
            for j, s in enumerate(group):
                found[s] = values[j * most : (j + 1) * most]
        early = [found[s] for s in sorted(found)]
        early_x = joined([value[:, :part] for value in early])
        early_dy = joined([value[:, part:] for value in early])
        last_x, last_dy = end_x[k - 1], end_dy[k - 1]
        terms = plus(terms, three(joined([early_x, last_x]), joined([early_dy, last_dy]), 2 * k))
        other_x = joined([other_core(early_x), other_core(last_x)])
        other_dy = joined([other_core(early_dy), other_core(last_dy)])
        terms = plus(terms, three(other_x, other_dy, 2 * k + 1))
    pre_gate, pre_up, back_grad = terms

    sig = jax.nn.sigmoid(pre_gate)
    active = pre_gate * sig
    grad_gate = (back_grad * pre_up * sig * (1.0 + pre_gate * (1.0 - sig))).astype(BF16)
    grad_up = (back_grad * active).astype(BF16)
    route = jnp.sum(active * pre_up * back_grad, axis=-1)

    def block_grad(at):
        cut = slice(at * part, (at + 1) * part)
        return (
            lax.dot_general(grad_gate, wg[cut], CONTRACT, preferred_element_type=F32)
            + lax.dot_general(grad_up, wu[cut], CONTRACT, preferred_element_type=F32)
        ).astype(BF16)

    block_grads = [block_grad(at) for at in range(seq_count)]
    sums = two_halves(route[:, None])
    others = []
    for k in range(1, chips):
        keep, sent = split(block_grads, sums, k)
        others.append((keep, sums, other_core(sent)))
    order = [(7 * unit, unit), (3 * unit, 4 * unit), (0, 3 * unit)]
    first, count = order[0]
    summed = [added(*values, first * most, count * most, []) for values in others]
    keep, sent = split(block_grads, sums, 0)
    sent = other_core(copied([sent], summed)[0])

    back = [None] * exp_count
    after = []
    for first, count in order:
        if not first:
            after.append(back[-1])
        summed = [added(*values, first * most, count * most, after) for values in others]
        arrived = [chip_shift(values, k) for k, values in enumerate(summed, 1)]
        pieces = totals(keep, sums, sent, arrived, first, count, most)
        for j, piece in enumerate(pieces):
            back[first + j] = exp_swap(piece, first + j)
        after = [pieces[0]]

    own_grad, own_route_t = combine(
        ids_t, own_ids_t, weights_t, place, back, expert_count, part
    )
    return own_grad, own_route_t.T


def solution(mesh):
    in_specs = (
        P("exp", "seq"),
        P("exp", "seq"),
        P("exp", None),
        P("exp", None),
        P("exp", None, "seq"),
        P("exp", None, "seq"),
        P("exp", "seq", None),
    )
    out_specs = (P("exp", "seq"), P("exp", "seq"))
    return jax.shard_map(local, mesh=mesh, in_specs=in_specs, out_specs=out_specs, check_vma=False)
```
